512 devices in a mesh: gx: 16 (over z), gy: 8 (over x, core), gz: 4 (over y).
Axes of the slice: x: 4, y: 4, z: 16, core: 2. Of those that a mesh axis runs over, the one named last changes fastest.
Arguments:
- residuals: float32 [8, 4, 64, 32, 512], P(None, None, 'gx', 'gy', 'gz'), may hold values from -8 to 8
- shear_rate: float32 [64, 32, 512], P('gx', 'gy', 'gz'), may hold values from 0.05 to 20
- coupling: float32 [4, 4, 64, 32, 512], P(None, None, 'gx', 'gy', 'gz'), may hold values from -0.5 to 4, as said below
Outputs:
- correction: float32 [8, 4, 64, 32, 512], P(None, None, 'gx', 'gy', 'gz')
- factor: float32 [40, 40], replicated
The draws below stay inside these ranges and needn't reach their ends.
Inputs may be any that keep to these rules, and one draw needn't show every extreme that they name: `coupling`: diagonal entries of each block lie between 2 and 4; off-diagonal entries have magnitude at most 0.5.
All inputs are finite; a program needn't handle non-finite values.
Results may differ from the reference program's by a relative error of at most 0.0003.
Values sent between devices are 32-bit elements; how exact they have to be, the bound alone decides.
No kernel may reach another device: no remote copies, remote signals or barrier semaphores. Data moves between devices by JAX's collectives and lax.ppermute only.
A program may use at most 64 MiB of HBM per device.

```python
import math
import jax
import jax.numpy as jnp
from jax import lax

RHS = 8
COMP = 4
POWERS = 4
NX = 64
NY = 32
NZ = 512


def draw_coupling(key, part):
    first_key, second_key = jax.random.split(jax.random.fold_in(key, 11))
    full_shape = (COMP, COMP, NX, NY, NZ)
    spread = jax.random.uniform(second_key, full_shape, jnp.float32, -0.4, 0.4)
    diagonal_values = jax.random.uniform(first_key, full_shape, jnp.float32, 2.0, 4.0)
    identity = jnp.eye(COMP, dtype=jnp.float32)[:, :, None, None, None]
    return identity * diagonal_values + (1.0 - identity) * spread


def steps_of(own_key, dims, cuts, least, top_value):
    level = 1.0
    for position, parts in cuts:
        steps = jax.random.uniform(jax.random.fold_in(jax.random.fold_in(own_key, 6), position), (parts,), jnp.float32, least / len(cuts), top_value / len(cuts))
        level = level * jnp.repeat(jnp.exp(steps), dims[position] // parts).reshape((-1,) + (1,) * (len(dims) - 1 - position))
    return level


def centred(stream_key, dims, deviation, limit, cuts=(), held_as=jnp.bfloat16):
    level = steps_of(stream_key, dims, cuts, -0.22, 0.18) if cuts else 1.0
    values = jax.random.normal(stream_key, dims, jnp.float32) * deviation * level
    return jnp.minimum(jnp.maximum(values, -limit), limit).astype(held_as)


def setup_inputs(seed: int = 0) -> dict:
    key_list = jax.random.split(jax.random.key(seed), 4)
    residuals = centred(key_list[0], (RHS, COMP, NX, NY, NZ), 1.0, 8.0, ((2, 16), (3, 8), (4, 4)), jnp.float32)
    shear_rate = jnp.clip(jnp.exp(math.log(20.0) - 5.9914645 * jax.random.uniform(key_list[1], (NX, NY, NZ), jnp.float32) ** steps_of(key_list[1], (NX, NY, NZ), ((0, 16), (1, 8), (2, 4)), -0.2, 0.2)), 0.05, 20.0)
    coupling = draw_coupling(jax.random.fold_in(key_list[3], 71), 0)
    return {"residuals": residuals, "shear_rate": shear_rate, "coupling": coupling}


VISCOSITY = 0.2
YIELD_STRESS = 1.0
REGULARIZE = 100.0
HIGHEST = lax.Precision.HIGHEST

def viscosity(shear_rate):
    return VISCOSITY + YIELD_STRESS * (1.0 - jnp.exp(-REGULARIZE * shear_rate)) / shear_rate

def coefficient_stack(shear_rate, coupling):
    cell_shape = shear_rate.shape
    entries = coupling.shape[0] * coupling.shape[1]
    return jnp.concatenate([coupling.reshape((entries,) + cell_shape), viscosity(shear_rate)[None], jnp.ones((1,) + cell_shape, jnp.float32)], axis=0)

def inner_part(values_in, shift_x, shift_y, shift_z):
    size_x, size_y, size_z = values_in.shape[-3:]
    return values_in[..., shift_x:shift_x + size_x - 2, shift_y:shift_y + size_y - 2, shift_z:shift_z + size_z - 2]

def advance(padded, coeffs):
    centre = inner_part(padded, 1, 1, 1)
    components = centre.shape[1]
    eta_all = coeffs[components * components]
    eta_mid = inner_part(eta_all, 1, 1, 1)
    inside_flag = inner_part(coeffs[components * components + 1], 1, 1, 1)
    beside = jnp.zeros_like(centre)
    kappa_sum = jnp.zeros_like(eta_mid)
    for offsets in ((0, 1, 1), (2, 1, 1), (1, 0, 1), (1, 2, 1), (1, 1, 0), (1, 1, 2)):
        face_kappa = 0.5 * (eta_mid + inner_part(eta_all, offsets[0], offsets[1], offsets[2]))
        kappa_sum = kappa_sum + face_kappa
        beside = beside + face_kappa[None, None] * inner_part(padded, offsets[0], offsets[1], offsets[2])
    coupled = inner_part(coeffs[:components * components], 1, 1, 1)
    results = []
    for row_index in range(components):
        summed = -beside[:, row_index]
        for column_index in range(components):
            if column_index != row_index:
                summed = summed + coupled[row_index * components + column_index][None] * centre[:, column_index]
        denom = coupled[row_index * components + row_index] + kappa_sum + 1.0 - inside_flag
        results.append(inside_flag[None] * summed / denom[None])
    return jnp.stack(results, axis=1)

def cholesky_upper(gram_matrix):
    order = gram_matrix.shape[0]
    positions = jnp.arange(order, dtype=jnp.int32)

    def row_step(row, upper):
        column = lax.dynamic_slice_in_dim(upper, row, 1, 1)[:, 0]
        gram_row = lax.dynamic_slice_in_dim(gram_matrix, row, 1, 0)[0]
        remain = gram_row - jnp.dot(column, upper, precision=HIGHEST)
        pivot = jnp.sum(jnp.where(positions == row, remain, 0.0))
        root = jnp.sqrt(pivot)
        new_row = jnp.where(positions >= row, remain / root, 0.0)
        return lax.dynamic_update_slice_in_dim(upper, new_row[None, :], row, 0)
    return lax.fori_loop(0, order, row_step, jnp.zeros((order, order), jnp.float32))

def back_solve(upper, target):
    order = upper.shape[0]
    positions = jnp.arange(order, dtype=jnp.int32)

    def solve_step(count, solution):
        row = order - 1 - count
        upper_row = lax.dynamic_slice_in_dim(upper, row, 1, 0)[0]
        pivot = jnp.sum(jnp.where(positions == row, upper_row, 0.0))
        target_row = lax.dynamic_slice_in_dim(target, row, 1, 0)[0]
        value = (target_row - jnp.dot(upper_row, solution, precision=HIGHEST)) / pivot
        return lax.dynamic_update_slice_in_dim(solution, value[None, :], row, 0)
    return lax.fori_loop(0, order, solve_step, jnp.zeros(target.shape, jnp.float32))

def gram_schmidt(matrix):
    row_count, column_count = matrix.shape

    def column_step(column, state_pair):
        ortho_basis, upper_factor = state_pair
        vector = lax.dynamic_slice_in_dim(matrix, column, 1, 1)[:, 0]
        first_coef = jnp.dot(ortho_basis.T, vector, precision=HIGHEST)
        vector = vector - jnp.dot(ortho_basis, first_coef, precision=HIGHEST)
        second_coef = jnp.dot(ortho_basis.T, vector, precision=HIGHEST)
        vector = vector - jnp.dot(ortho_basis, second_coef, precision=HIGHEST)
        length = jnp.sqrt(jnp.sum(vector * vector))
        unit_pick = (jnp.arange(column_count) == column).astype(jnp.float32)
        ortho_basis = lax.dynamic_update_slice_in_dim(ortho_basis, (vector / length)[:, None], column, 1)
        upper_factor = lax.dynamic_update_slice_in_dim(upper_factor, (first_coef + second_coef + length * unit_pick)[:, None], column, 1)
        return (ortho_basis, upper_factor)
    initial = (jnp.zeros((row_count, column_count), jnp.float32), jnp.zeros((column_count, column_count), jnp.float32))
    return lax.fori_loop(0, column_count, column_step, initial)

def small_solve(factor, rhs_count):
    target = factor[:, :rhs_count]
    hessenberg = factor[:, :-rhs_count] + factor[:, rhs_count:]
    ortho_basis, upper_factor = gram_schmidt(hessenberg)
    projected = jnp.dot(ortho_basis.T, target, precision=HIGHEST)
    return back_solve(upper_factor, projected)

def reference(residuals, shear_rate, coupling):
    coeffs = coefficient_stack(shear_rate, coupling)
    coeff_pad = jnp.pad(coeffs, ((0, 0), (1, 1), (1, 1), (1, 1)))
    krylov_basis = [residuals]
    for power_step in range(POWERS):
        padded = jnp.pad(krylov_basis[-1], ((0, 0), (0, 0), (1, 1), (1, 1), (1, 1)))
        krylov_basis.append(advance(padded, coeff_pad))
    flat_list = [member.reshape(RHS, -1) for member in krylov_basis]
    block_rows = []
    for left_index in range(POWERS + 1):
        block_rows.append([jnp.dot(flat_list[left_index], flat_list[right_index].T, precision=HIGHEST) for right_index in range(POWERS + 1)])
    gram_matrix = jnp.block(block_rows)
    factor = cholesky_upper(gram_matrix)
    update = small_solve(factor, RHS)
    correction = jnp.zeros_like(flat_list[0])
    for power_step in range(POWERS):
        correction = correction + jnp.dot(update[power_step * RHS:(power_step + 1) * RHS].T, flat_list[power_step], precision=HIGHEST)
    return (correction.reshape(residuals.shape), factor)
```

```python
import jax
import jax.numpy as jnp
from jax import lax
from jax.experimental import pallas as pl
from jax.experimental.pallas import tpu as pltpu
from jax.sharding import PartitionSpec as P

POWERS = 4
RHS = 8
COMP = 4
BX = 4
BY = 4
LANES = 128
COLS = BX * BY
GRID = BX + 2 * POWERS
HIGHEST = lax.Precision.HIGHEST
VMEM = pl.BlockSpec(memory_space=pltpu.VMEM)

FIELD_ROWS = COMP * COLS * RHS
COUPLE_AT = FIELD_ROWS
ETA_AT = COUPLE_AT + COMP * COMP * COLS
MAIN_ROWS = ETA_AT + COLS
GHOST_ROWS = COMP * RHS + 24
BLOCK_ROWS = MAIN_ROWS + GHOST_ROWS

NEAR = [(1, 1), (1, 2), (2, 1)]
FAR = [(1, 3), (2, 2), (3, 1)]
CORNER = [(side, a, b) for a, b in NEAR + FAR for side in (0, 1)]
NEAR_COUNT = 2 * len(NEAR)
C_COUPLE_AT = len(CORNER) * COMP * RHS
C_ETA_AT = C_COUPLE_AT + NEAR_COUNT * 16
C_GHOST_AT = C_ETA_AT + 16
CORNER_ROWS = C_GHOST_AT + 2 * GHOST_ROWS


def lane_index():
    return lax.broadcasted_iota(jnp.int32, (RHS, LANES), 1)


def pack_kernel(res_ref, shear_ref, couple_ref, main_ref, low_ref, high_ref):
    lane = lane_index()
    shear = shear_ref[...]
    eta = 0.2 + (1.0 - jnp.exp(-100.0 * shear)) / shear
    main_ref[ETA_AT:MAIN_ROWS, :] = eta
    main_ref[COUPLE_AT:ETA_AT, :] = couple_ref[...]

    def pack(group, load):
        low = jnp.zeros((RHS, LANES), jnp.float32)
        high = jnp.zeros((RHS, LANES), jnp.float32)
        for col in range(COLS):
            turned = pltpu.roll(load(col), (8 * col + 4) % LANES, 1)
            here = lane // 4
            high = jnp.where(here == 2 * col, turned, high)
            low = jnp.where(here == 2 * col + 1, turned, low)
        low_ref[group * 8 : group * 8 + 8, :] = low
        high_ref[group * 8 : group * 8 + 8, :] = high

    for comp in range(COMP):

        def load_field(col):
            place = comp * COLS + col
            value = res_ref[pl.ds(place, RHS, stride=COMP * COLS), :]
            main_ref[place * RHS : place * RHS + RHS, :] = value
            return value

        pack(comp, load_field)
    for half in range(2):
        pack(
            COMP + half,
            lambda col: couple_ref[pl.ds(half * 8 * COLS + col, 8, stride=COLS), :],
        )
    pack(
        COMP + 2,
        lambda col: jnp.broadcast_to(eta[col : col + 1, :], (RHS, LANES)),
    )


def pack(residuals, shear_rate, coupling):
    return pl.pallas_call(
        pack_kernel,
        out_shape=(
            jax.ShapeDtypeStruct((MAIN_ROWS, LANES), jnp.float32),
            jax.ShapeDtypeStruct((GHOST_ROWS, LANES), jnp.float32),
            jax.ShapeDtypeStruct((GHOST_ROWS, LANES), jnp.float32),
        ),
        in_specs=[VMEM] * 3,
        out_specs=(VMEM,) * 3,
        compiler_params=pltpu.CompilerParams(vmem_limit_bytes=4 * 2**20),
    )(
        residuals.reshape(RHS * COMP * COLS, LANES),
        shear_rate.reshape(COLS, LANES),
        coupling.reshape(COMP * COMP * COLS, LANES),
    )


def corner_kernel(left_ref, right_ref, down_ref, up_ref):
    for out_ref, top in ((down_ref, False), (up_ref, True)):
        for place, (side, a, b) in enumerate(CORNER):
            src = right_ref if side else left_ref
            x = a - 1 if side else BX - a
            y = BY - b if top else b - 1
            col = x * BY + y
            for comp in range(COMP):
                start = (comp * COLS + col) * RHS
                row = (place * COMP + comp) * RHS
                out_ref[row : row + RHS, :] = src[start : start + RHS, :]
            if place < NEAR_COUNT:
                for half in range(2):
                    row = C_COUPLE_AT + place * 16 + half * 8
                    out_ref[row : row + 8, :] = src[
                        pl.ds(COUPLE_AT + half * 8 * COLS + col, 8, stride=COLS), :
                    ]
            out_ref[C_ETA_AT + place : C_ETA_AT + place + 1, :] = src[
                ETA_AT + col : ETA_AT + col + 1, :
            ]
        out_ref[C_ETA_AT + len(CORNER) : C_GHOST_AT, :] = jnp.zeros(
            (16 - len(CORNER), LANES), jnp.float32
        )
        out_ref[C_GHOST_AT : C_GHOST_AT + GHOST_ROWS, :] = left_ref[MAIN_ROWS:BLOCK_ROWS, :]
        out_ref[C_GHOST_AT + GHOST_ROWS : CORNER_ROWS, :] = right_ref[MAIN_ROWS:BLOCK_ROWS, :]


def corners(left, right):
    return pl.pallas_call(
        corner_kernel,
        out_shape=(jax.ShapeDtypeStruct((CORNER_ROWS, LANES), jnp.float32),) * 2,
        in_specs=[VMEM] * 2,
        out_specs=(VMEM,) * 2,
        compiler_params=pltpu.CompilerParams(vmem_limit_bytes=4 * 2**20),
    )(left, right)


def distance(place):
    return max(POWERS - place, 0, place - (POWERS + BX - 1))


def powers_kernel(
    own_ref, left_ref, right_ref, front_ref, back_ref, low_ref, high_ref,
    basis_ref, gram_ref,
    main, ghost, coef, coef_ghost, face, face_ghost, square,
):
    lane = lane_index()
    first, last = lane == 0, lane == LANES - 1

    def slot(x, y):
        return x * GRID + y

    def place_column(src, x, y, field_at, couple_at, couple_stride, eta_at, ghost_at, col):
        reach = distance(x) + distance(y)
        at = slot(x, y)
        for comp in range(COMP):
            main[0, at * COMP + comp] = src[field_at[comp] : field_at[comp] + RHS, :]
        coef[at, 16:24, :] = jnp.broadcast_to(src[eta_at : eta_at + 1, :], (8, LANES))
        if reach >= POWERS:
            return
        for half in range(2):
            start = couple_at + half * 8 * couple_stride
            coef[at, half * 8 : half * 8 + 8, :] = (
                src[pl.ds(start, 8, stride=couple_stride), :]
                if couple_stride > 1
                else src[start : start + 8, :]
            )
        shift = (-8 * col - 4) % LANES
        for comp in range(COMP):
            row = ghost_at + comp * RHS
            ghost[0, at * COMP + comp] = pltpu.roll(src[row : row + RHS, :], shift, 1)
        for part in range(3):
            row = ghost_at + COMP * RHS + part * 8
            coef_ghost[at, part * 8 : part * 8 + 8, :] = pltpu.roll(
                src[row : row + 8, :], shift, 1
            )

    for src, off_x, off_y in (
        (own_ref, 0, 0), (left_ref, -1, 0), (right_ref, 1, 0), (front_ref, 0, -1), (back_ref, 0, 1)
    ):
        for x in range(BX):
            for y in range(BY):
                col = x * BY + y
                place_column(
                    src, POWERS + off_x * BX + x, POWERS + off_y * BY + y,
                    [(comp * COLS + col) * RHS for comp in range(COMP)],
                    COUPLE_AT + col, COLS, ETA_AT + col, MAIN_ROWS, col,
                )
    for src, top in ((low_ref, True), (high_ref, False)):
        for place, (side, a, b) in enumerate(CORNER):
            x = POWERS + BX - 1 + a if side else POWERS - a
            y = POWERS - b if top else POWERS + BY - 1 + b
            col = (a - 1 if side else BX - a) * BY + (BY - b if top else b - 1)
            at = slot(x, y)
            for comp in range(COMP):
                row = (place * COMP + comp) * RHS
                main[0, at * COMP + comp] = src[row : row + RHS, :]
            coef[at, 16:24, :] = jnp.broadcast_to(
                src[C_ETA_AT + place : C_ETA_AT + place + 1, :], (8, LANES)
            )
            if place < NEAR_COUNT:
                for half in range(2):
                    row = C_COUPLE_AT + place * 16 + half * 8
                    coef[at, half * 8 : half * 8 + 8, :] = src[row : row + 8, :]
                shift = (-8 * col - 4) % LANES
                base = C_GHOST_AT + side * GHOST_ROWS
                for comp in range(COMP):
                    row = base + comp * RHS
                    ghost[0, at * COMP + comp] = pltpu.roll(src[row : row + RHS, :], shift, 1)
                for part in range(3):
                    row = base + COMP * RHS + part * 8
                    coef_ghost[at, part * 8 : part * 8 + 8, :] = pltpu.roll(
                        src[row : row + 8, :], shift, 1
                    )

    def over_columns(reach, body):
        for off in range(reach + 1):
            ys = range(POWERS - (reach - off), POWERS + BY + reach - off)
            if off == 0:
                xs, count = (lambda i: POWERS + i), BX
            else:
                xs, count = (lambda i, off=off: POWERS - off + i * (BX - 1 + 2 * off)), 2

            def step(i, carry, ys=ys, xs=xs, off=off):
                x = xs(i)
                for y in ys:
                    body(x, y, off + distance(y))
                return carry

            lax.fori_loop(0, count, step, 0)

    def shifted(value, other):
        up, down = pltpu.roll(value, LANES - 1, 1), pltpu.roll(value, 1, 1)
        other_up, other_down = pltpu.roll(other, LANES - 1, 1), pltpu.roll(other, 1, 1)
        return (
            jnp.where(last, other_up, up), jnp.where(first, other_down, down),
            jnp.where(last, up, other_up), jnp.where(first, down, other_down),
        )

    def faces(table, out, x, y, at, eta, up, down):
        around = [
            table[slot(x - 1, y), 16:24, :], table[slot(x + 1, y), 16:24, :],
            table[slot(x, y - 1), 16:24, :], table[slot(x, y + 1), 16:24, :],
            down, up,
        ]
        total = jnp.zeros_like(eta)
        for index, beside in enumerate(around):
            kappa = 0.5 * (eta + beside)
            total = total + kappa
            out[at * 10 + index] = -kappa
        for comp in range(COMP):
            diagonal = jnp.broadcast_to(
                table[at, 5 * comp : 5 * comp + 1, :], (RHS, LANES)
            )
            out[at * 10 + 6 + comp] = jnp.where(eta > 0.0, 1.0 / (diagonal + total), 0.0)

    def prepare(x, y, reach):
        at = slot(x, y)
        eta, eta_ghost = coef[at, 16:24, :], coef_ghost[at, 16:24, :]
        up, down, ghost_up, ghost_down = shifted(eta, eta_ghost)
        faces(coef, face, x, y, at, eta, up, down)
        if reach < POWERS - 1:
            faces(coef_ghost, face_ghost, x, y, at, eta_ghost, ghost_up, ghost_down)

    over_columns(POWERS - 1, prepare)

    def apply(field, table, faces_of, at, x, y, source, centre, up, down):
        kappa = [faces_of[at * 10 + index] for index in range(6)]
        entry = {}
        for row in range(COMP):
            for col in range(COMP):
                if row != col:
                    e = row * COMP + col
                    entry[row, col] = jnp.broadcast_to(table[at, e : e + 1, :], (RHS, LANES))
        results = []
        for comp in range(COMP):
            beside = [
                field[source, slot(x - 1, y) * COMP + comp],
                field[source, slot(x + 1, y) * COMP + comp],
                field[source, slot(x, y - 1) * COMP + comp],
                field[source, slot(x, y + 1) * COMP + comp],
                down[comp],
                up[comp],
            ]
            terms = [k * v for k, v in zip(kappa, beside)]
            terms += [entry[comp, d] * centre[d] for d in range(COMP) if d != comp]
            while len(terms) > 1:
                terms = [
                    terms[i] + terms[i + 1] if i + 1 < len(terms) else terms[i]
                    for i in range(0, len(terms), 2)
                ]
            results.append(terms[0] * faces_of[at * 10 + 6 + comp])
        return results

    for power in range(1, POWERS + 1):
        limit = POWERS - power
        source, target = (power - 1) % 2, power % 2

        def advance(x, y, reach, limit=limit, source=source, target=target, power=power):
            at = slot(x, y)
            centre = [main[source, at * COMP + comp] for comp in range(COMP)]
            outer = [ghost[source, at * COMP + comp] for comp in range(COMP)]
            moved = [shifted(c, o) for c, o in zip(centre, outer)]
            results = apply(
                main, coef, face, at, x, y, source, centre,
                [m[0] for m in moved], [m[1] for m in moved],
            )
            for comp in range(COMP):
                main[target, at * COMP + comp] = results[comp]
            if reach == 0:
                results_at = (x - POWERS) * BY + (y - POWERS)
            if reach < limit:
                outside = apply(
                    ghost, coef_ghost, face_ghost, at, x, y, source, outer,
                    [m[2] for m in moved], [m[3] for m in moved],
                )
                for comp in range(COMP):
                    ghost[target, at * COMP + comp] = outside[comp]

        over_columns(limit, advance)
        for comp in range(COMP):
            for x in range(BX):
                for y in range(BY):
                    tile = comp * COLS + x * BY + y
                    at = slot(POWERS + x, POWERS + y)
                    if power == 1:
                        basis_ref[tile, 0:RHS, :] = main[0, at * COMP + comp]
                    basis_ref[tile, power * RHS : power * RHS + RHS, :] = main[
                        target, at * COMP + comp
                    ]

    order = (POWERS + 1) * RHS
    total = jnp.zeros((order, order), jnp.float32)
    for tile in range(0, COMP * COLS, 2):
        both = jnp.concatenate([basis_ref[tile], basis_ref[tile + 1]], axis=1)
        total = total + lax.dot_general(
            both, both, (((1,), (1,)), ((), ())),
            precision=HIGHEST, preferred_element_type=jnp.float32,
        )
    square[...] = jnp.zeros_like(square)
    square[:, 0:order] = total
    packed = jnp.zeros((RHS, LANES), jnp.float32)
    start = 0
    for block in range(POWERS + 1):
        width = order - block * RHS
        value = pltpu.roll(
            square[block * RHS : block * RHS + RHS, :], (start - block * RHS) % LANES, 1
        )
        packed = jnp.where((lane >= start) & (lane < start + width), value, packed)
        start += width
    gram_ref[...] = packed


def powers(own, left, right, front, back, low, high):
    count = GRID * GRID
    return pl.pallas_call(
        powers_kernel,
        out_shape=(
            jax.ShapeDtypeStruct((COMP * COLS, (POWERS + 1) * RHS, LANES), jnp.float32),
            jax.ShapeDtypeStruct((RHS, LANES), jnp.float32),
        ),
        in_specs=[VMEM] * 7,
        out_specs=(VMEM,) * 2,
        scratch_shapes=[
            pltpu.VMEM((2, count * COMP, RHS, LANES), jnp.float32),
            pltpu.VMEM((2, count * COMP, RHS, LANES), jnp.float32),
            pltpu.VMEM((count, 24, LANES), jnp.float32),
            pltpu.VMEM((count, 24, LANES), jnp.float32),
            pltpu.VMEM((count * 10, RHS, LANES), jnp.float32),
            pltpu.VMEM((count * 10, RHS, LANES), jnp.float32),
            pltpu.VMEM(((POWERS + 1) * RHS, LANES), jnp.float32),
        ],
        compiler_params=pltpu.CompilerParams(vmem_limit_bytes=48 * 2**20),
    )(own, left, right, front, back, low, high)


def finish_kernel(gram_ref, basis_ref, out_ref, factor_ref, square, upper):
    lane = lane_index()
    order = (POWERS + 1) * RHS
    parts = [gram_ref[i] for i in range(gram_ref.shape[0])]
    while len(parts) > 1:
        parts = [
            parts[i] + parts[i + 1] if i + 1 < len(parts) else parts[i]
            for i in range(0, len(parts), 2)
        ]
    packed = parts[0]
    square[...] = jnp.zeros_like(square)
    start = 0
    for block in range(POWERS + 1):
        width = order - block * RHS
        value = pltpu.roll(packed, (block * RHS - start) % LANES, 1)
        keep = (lane >= block * RHS) & (lane < order)
        square[block * RHS : block * RHS + RHS, :] = jnp.where(keep, value, 0.0)
        start += width
    half = square[...]
    other = half.T
    gram = []
    for block in range(POWERS + 1):
        rows = slice(block * RHS, block * RHS + RHS)
        gram.append(jnp.where(lane < block * RHS, other[rows, :], half[rows, :]))
    summed = [tile + pltpu.roll(tile, LANES - RHS, 1) for tile in gram]
    normal = [summed[i] + summed[i + 1] for i in range(POWERS)] + [summed[0]]

    upper[...] = jnp.zeros_like(upper)
    for step in range(order):
        tile, row = step // RHS, step % RHS
        pick = gram[tile][row : row + 1, :]
        pivot = pick[:, step : step + 1]
        inverse = 1.0 / pivot
        upper[step : step + 1, :] = jnp.where(
            lane[0:1, :] >= step, pick * lax.rsqrt(pivot), 0.0
        )
        scaled = pick * inverse
        for i in range(tile, POWERS + 1):
            gram[i] = gram[i] - gram[i][:, step : step + 1] * scaled
        if step < POWERS * RHS:
            pick = normal[tile][row : row + 1, :]
            inverse = 1.0 / pick[:, step : step + 1]
            scaled = jnp.where(lane[0:1, :] == step, -inverse, pick * inverse)
            for i in range(tile, POWERS + 1):
                kept = jnp.where(lane == step, 0.0, normal[i])
                normal[i] = kept - normal[i][:, step : step + 1] * scaled
    factor_ref[...] = upper[0:order, 0:order]
    answer = normal[POWERS]
    weights = [
        jnp.broadcast_to(answer[:, i : i + 1], (RHS, LANES)) for i in range(POWERS * RHS)
    ]

    def combine(tile, carry):
        sums = [None] * 4
        for i in range(POWERS * RHS):
            term = weights[i] * jnp.broadcast_to(basis_ref[tile, i : i + 1, :], (RHS, LANES))
            sums[i % 4] = term if sums[i % 4] is None else sums[i % 4] + term
        out_ref[pl.ds(tile, RHS, stride=COMP * COLS), :] = (sums[0] + sums[1]) + (
            sums[2] + sums[3]
        )
        return carry

    lax.fori_loop(0, COMP * COLS, combine, 0)


def finish(gram, basis):
    order = (POWERS + 1) * RHS
    return pl.pallas_call(
        finish_kernel,
        out_shape=(
            jax.ShapeDtypeStruct((RHS * COMP * COLS, LANES), jnp.float32),
            jax.ShapeDtypeStruct((order, order), jnp.float32),
        ),
        in_specs=[VMEM] * 2,
        out_specs=(VMEM,) * 2,
        scratch_shapes=[
            pltpu.VMEM((LANES, LANES), jnp.float32),
            pltpu.VMEM((order, LANES), jnp.float32),
        ],
        compiler_params=pltpu.CompilerParams(vmem_limit_bytes=6 * 2**20),
    )(gram, basis)


def moved(block, axis, step):
    count = lax.axis_size(axis)
    pairs = [(i, i + step) for i in range(count) if 0 <= i + step < count]
    return lax.ppermute(block, axis, pairs)


def gathered(tile, axes):
    count = lax.axis_size(axes)
    return lax.all_to_all(jnp.broadcast_to(tile[None], (count,) + tile.shape), axes, 0, 0)


def local(residuals, shear_rate, coupling):
    block, low, high = pack(residuals, shear_rate, coupling)
    ghosts = moved(high, "gz", 1) + moved(low, "gz", -1)
    own = jnp.concatenate([block, ghosts], axis=0)
    left, right = moved(own, "gx", 1), moved(own, "gx", -1)
    front, back = moved(own, "gy", 1), moved(own, "gy", -1)
    down, up = corners(left, right)
    low_corner, high_corner = moved(up, "gy", 1), moved(down, "gy", -1)
    basis, gram = powers(own, left, right, front, back, low_corner, high_corner)
    gram = jnp.sum(gathered(gram, ("gy", "gz")), axis=0)
    correction, factor = finish(gathered(gram, "gx"), basis)
    return correction.reshape(residuals.shape), factor


def solution(mesh):
    in_specs = (
        P(None, None, "gx", "gy", "gz"),
        P("gx", "gy", "gz"),
        P(None, None, "gx", "gy", "gz"),
    )
    out_specs = (P(None, None, "gx", "gy", "gz"), P())
    return jax.shard_map(local, mesh=mesh, in_specs=in_specs, out_specs=out_specs, check_vma=False)
```

```python
import jax
import jax.numpy as jnp
from jax import lax
from jax.experimental import pallas as pl
from jax.experimental.pallas import tpu as pltpu
from jax.sharding import PartitionSpec as P

POWERS = 4
RHS = 8
COMP = 4
BX = 4
BY = 4
LANES = 128
COLS = BX * BY
GRID = BX + 2 * POWERS
HIGHEST = lax.Precision.HIGHEST
VMEM = pl.BlockSpec(memory_space=pltpu.VMEM)

FIELD_ROWS = COMP * COLS * RHS
COUPLE_AT = FIELD_ROWS
ETA_AT = COUPLE_AT + COMP * COMP * COLS
MAIN_ROWS = ETA_AT + COLS
GHOST_ROWS = COMP * RHS + 24
BLOCK_ROWS = MAIN_ROWS + GHOST_ROWS

NEAR = [(1, 1), (1, 2), (2, 1)]
FAR = [(1, 3), (2, 2), (3, 1)]
CORNER = NEAR + FAR
C_COUPLE_AT = len(CORNER) * COMP * RHS
C_ETA_AT = C_COUPLE_AT + len(NEAR) * 16
C_GHOST_AT = C_ETA_AT + 8
CORNER_ROWS = C_GHOST_AT + GHOST_ROWS
SIDES = [(1, 1), (1, -1), (-1, 1), (-1, -1)]


def lane_index():
    return lax.broadcasted_iota(jnp.int32, (RHS, LANES), 1)


def pack_kernel(raw_ref, main_ref, low_ref, high_ref):
    lane = lane_index()
    shear = raw_ref[ETA_AT:MAIN_ROWS, :]
    eta = -0.5 * (0.2 + (1.0 - jnp.exp(-100.0 * shear)) / shear)
    main_ref[ETA_AT:MAIN_ROWS, :] = eta
    main_ref[COUPLE_AT:ETA_AT, :] = raw_ref[COUPLE_AT:ETA_AT, :]

    def pack(group, load):
        low = jnp.zeros((RHS, LANES), jnp.float32)
        high = jnp.zeros((RHS, LANES), jnp.float32)
        for col in range(COLS):
            turned = pltpu.roll(load(col), (8 * col + 4) % LANES, 1)
            here = lane // 4
            high = jnp.where(here == 2 * col, turned, high)
            low = jnp.where(here == 2 * col + 1, turned, low)
        low_ref[group * 8 : group * 8 + 8, :] = low
        high_ref[group * 8 : group * 8 + 8, :] = high

    for comp in range(COMP):

        def load_field(col):
            place = comp * COLS + col
            value = raw_ref[pl.ds(place, RHS, stride=COMP * COLS), :]
            main_ref[place * RHS : place * RHS + RHS, :] = value
            return value

        pack(comp, load_field)
    for half in range(2):
        pack(
            COMP + half,
            lambda col: raw_ref[pl.ds(COUPLE_AT + half * 8 * COLS + col, 8, stride=COLS), :],
        )
    pack(
        COMP + 2,
        lambda col: jnp.broadcast_to(eta[col : col + 1, :], (RHS, LANES)),
    )


def pack(residuals, shear_rate, coupling):
    raw = jnp.concatenate(
        [part.reshape(-1, LANES) for part in (residuals, coupling, shear_rate)], axis=0
    )
    return pl.pallas_call(
        pack_kernel,
        out_shape=(
            jax.ShapeDtypeStruct((MAIN_ROWS, LANES), jnp.float32),
            jax.ShapeDtypeStruct((GHOST_ROWS, LANES), jnp.float32),
            jax.ShapeDtypeStruct((GHOST_ROWS, LANES), jnp.float32),
        ),
        in_specs=[VMEM],
        out_specs=(VMEM,) * 3,
        compiler_params=pltpu.CompilerParams(vmem_limit_bytes=4 * 2**20),
    )(raw)


def corner_kernel(main_ref, ghosts_ref, own_ref, *outs):
    own_ref[0:MAIN_ROWS, :] = main_ref[...]
    ghosts = ghosts_ref[0]
    for i in range(1, ghosts_ref.shape[0]):
        ghosts = ghosts + ghosts_ref[i]
    own_ref[MAIN_ROWS:BLOCK_ROWS, :] = ghosts
    for (side_x, side_y), out_ref in zip(SIDES, outs):
        for place, (a, b) in enumerate(CORNER):
            x = BX - a if side_x > 0 else a - 1
            y = BY - b if side_y > 0 else b - 1
            col = x * BY + y
            for comp in range(COMP):
                start = (comp * COLS + col) * RHS
                row = (place * COMP + comp) * RHS
                out_ref[row : row + RHS, :] = main_ref[start : start + RHS, :]
            if place < len(NEAR):
                for half in range(2):
                    row = C_COUPLE_AT + place * 16 + half * 8
                    out_ref[row : row + 8, :] = main_ref[
                        pl.ds(COUPLE_AT + half * 8 * COLS + col, 8, stride=COLS), :
                    ]
            out_ref[C_ETA_AT + place : C_ETA_AT + place + 1, :] = main_ref[
                ETA_AT + col : ETA_AT + col + 1, :
            ]
        out_ref[C_ETA_AT + len(CORNER) : C_GHOST_AT, :] = jnp.zeros(
            (8 - len(CORNER), LANES), jnp.float32
        )
        out_ref[C_GHOST_AT:CORNER_ROWS, :] = ghosts


def corners(main, ghosts):
    return pl.pallas_call(
        corner_kernel,
        out_shape=(jax.ShapeDtypeStruct((BLOCK_ROWS, LANES), jnp.float32),)
        + (jax.ShapeDtypeStruct((CORNER_ROWS, LANES), jnp.float32),) * 4,
        in_specs=[VMEM] * 2,
        out_specs=(VMEM,) * 5,
        compiler_params=pltpu.CompilerParams(vmem_limit_bytes=4 * 2**20),
    )(main, ghosts)


def distance(place):
    return max(POWERS - place, 0, place - (POWERS + BX - 1))


def powers_kernel(
    own_ref, left_ref, right_ref, front_ref, back_ref, corner_0, corner_1, corner_2, corner_3,
    basis_ref, gram_ref,
    main, ghost, coef, coef_ghost, face, face_ghost, scale, scale_ghost, square,
):
    lane = lane_index()
    first, last = lane == 0, lane == LANES - 1

    def slot(x, y):
        return x * GRID + y

    def place_column(src, x, y, field_at, couple_at, couple_stride, eta_at, ghost_at, col):
        reach = distance(x) + distance(y)
        at = slot(x, y)
        for comp in range(COMP):
            main[0, at * COMP + comp] = src[field_at[comp] : field_at[comp] + RHS, :]
        coef[at, 16:24, :] = jnp.broadcast_to(src[eta_at : eta_at + 1, :], (8, LANES))
        if reach >= POWERS:
            return
        for half in range(2):
            start = couple_at + half * 8 * couple_stride
            coef[at, half * 8 : half * 8 + 8, :] = (
                src[pl.ds(start, 8, stride=couple_stride), :]
                if couple_stride > 1
                else src[start : start + 8, :]
            )
        shift = (-8 * col - 4) % LANES
        for comp in range(COMP):
            row = ghost_at + comp * RHS
            ghost[0, at * COMP + comp] = pltpu.roll(src[row : row + RHS, :], shift, 1)
        for part in range(3):
            row = ghost_at + COMP * RHS + part * 8
            coef_ghost[at, part * 8 : part * 8 + 8, :] = pltpu.roll(
                src[row : row + 8, :], shift, 1
            )

    for src, off_x, off_y in (
        (own_ref, 0, 0), (left_ref, -1, 0), (right_ref, 1, 0), (front_ref, 0, -1), (back_ref, 0, 1)
    ):
        for x in range(BX):
            for y in range(BY):
                col = x * BY + y
                place_column(
                    src, POWERS + off_x * BX + x, POWERS + off_y * BY + y,
                    [(comp * COLS + col) * RHS for comp in range(COMP)],
                    COUPLE_AT + col, COLS, ETA_AT + col, MAIN_ROWS, col,
                )
    for (side_x, side_y), src in zip(SIDES, (corner_0, corner_1, corner_2, corner_3)):
        for place, (a, b) in enumerate(CORNER):
            x = POWERS - a if side_x > 0 else POWERS + BX - 1 + a
            y = POWERS - b if side_y > 0 else POWERS + BY - 1 + b
            col = (BX - a if side_x > 0 else a - 1) * BY + (BY - b if side_y > 0 else b - 1)
            place_column(
                src, x, y, [(place * COMP + comp) * RHS for comp in range(COMP)],
                C_COUPLE_AT + place * 16, 1, C_ETA_AT + place, C_GHOST_AT, col,
            )

    def rows_of(reach):
        for x in range(POWERS - reach, POWERS + BX + reach):
            rest = reach - distance(x)
            yield x, range(POWERS - rest, POWERS + BY + rest)

    def shifted(value, other):
        up, down = pltpu.roll(value, LANES - 1, 1), pltpu.roll(value, 1, 1)
        other_up, other_down = pltpu.roll(other, LANES - 1, 1), pltpu.roll(other, 1, 1)
        return (
            jnp.where(last, other_up, up), jnp.where(first, other_down, down),
            jnp.where(last, up, other_up), jnp.where(first, down, other_down),
        )

    def faces(table, out, inverse, x, y, at, eta, up, down):
        around = [
            table[slot(x - 1, y), 16:24, :], table[slot(x + 1, y), 16:24, :],
            table[slot(x, y - 1), 16:24, :], table[slot(x, y + 1), 16:24, :],
            down, up,
        ]
        kappas = [eta + beside for beside in around]
        for index, kappa in enumerate(kappas):
            out[at * 6 + index] = kappa
        total = (kappas[0] + kappas[1]) + (kappas[2] + kappas[3]) + (kappas[4] + kappas[5])
        diagonal = table[at, pl.ds(0, COMP, stride=COMP + 1), :]
        inverse[at, 0:COMP, :] = jnp.where(
            eta[0:COMP, :] < 0.0, 1.0 / (diagonal - total[0:COMP, :]), 0.0
        )

    for x, ys in rows_of(POWERS - 1):
        for y in ys:
            at = slot(x, y)
            eta, eta_ghost = coef[at, 16:24, :], coef_ghost[at, 16:24, :]
            up, down, ghost_up, ghost_down = shifted(eta, eta_ghost)
            faces(coef, face, scale, x, y, at, eta, up, down)
            if distance(x) + distance(y) < POWERS - 1:
                faces(coef_ghost, face_ghost, scale_ghost, x, y, at, eta_ghost, ghost_up, ghost_down)

    def spread(table, at, row):
        return jnp.broadcast_to(table[at, row : row + 1, :], (RHS, LANES))

    def apply(load, table, faces_of, inverse, x, y, before, centre, after, up, down):
        at = slot(x, y)
        kappa = [faces_of[at * 6 + index] for index in range(6)]
        results = []
        for comp in range(COMP):
            beside = [
                load(x - 1, y, comp), load(x + 1, y, comp), before[comp], after[comp],
                down[comp], up[comp],
            ]
            terms = [k * v for k, v in zip(kappa, beside)]
            terms += [
                spread(table, at, comp * COMP + d) * centre[d] for d in range(COMP) if d != comp
            ]
            while len(terms) > 1:
                terms = [
                    terms[i] + terms[i + 1] if i + 1 < len(terms) else terms[i]
                    for i in range(0, len(terms), 2)
                ]
            results.append(terms[0] * spread(inverse, at, comp))
        return results

    for power in range(1, POWERS + 1):
        limit = POWERS - power
        source, target = (power - 1) % 2, power % 2

        def load_main(x, y, comp, source=source):
            return main[source, slot(x, y) * COMP + comp]

        def load_ghost(x, y, comp, source=source):
            return ghost[source, slot(x, y) * COMP + comp]

        for x, ys in rows_of(limit):
            rows = {}

            def at_row(load, y, x=x, rows=rows):
                if (load, y) not in rows:
                    rows[load, y] = [load(x, y, comp) for comp in range(COMP)]
                return rows[load, y]

            for y in ys:
                at = slot(x, y)
                centre, outer = at_row(load_main, y), at_row(load_ghost, y)
                moved = [shifted(c, o) for c, o in zip(centre, outer)]
                results = apply(
                    load_main, coef, face, scale, x, y,
                    at_row(load_main, y - 1), centre, at_row(load_main, y + 1),
                    [m[0] for m in moved], [m[1] for m in moved],
                )
                for comp in range(COMP):
                    if limit:
                        main[target, at * COMP + comp] = results[comp]
                if distance(x) + distance(y) == 0:
                    for comp in range(COMP):
                        tile = comp * COLS + (x - POWERS) * BY + (y - POWERS)
                        if power == 1:
                            basis_ref[tile, 0:RHS, :] = centre[comp]
                        basis_ref[tile, power * RHS : power * RHS + RHS, :] = results[comp]
                if distance(x) + distance(y) < limit:
                    outside = apply(
                        load_ghost, coef_ghost, face_ghost, scale_ghost, x, y,
                        at_row(load_ghost, y - 1), outer, at_row(load_ghost, y + 1),
                        [m[2] for m in moved], [m[3] for m in moved],
                    )
                    for comp in range(COMP):
                        ghost[target, at * COMP + comp] = outside[comp]

    order = (POWERS + 1) * RHS
    total = jnp.zeros((order, order), jnp.float32)
    for tile in range(0, COMP * COLS, 2):
        both = jnp.concatenate([basis_ref[tile], basis_ref[tile + 1]], axis=1)
        total = total + lax.dot_general(
            both, both, (((1,), (1,)), ((), ())),
            precision=HIGHEST, preferred_element_type=jnp.float32,
        )
    square[...] = jnp.zeros_like(square)
    square[:, 0:order] = total
    packed = jnp.zeros((RHS, LANES), jnp.float32)
    start = 0
    for block in range(POWERS + 1):
        width = order - block * RHS
        value = pltpu.roll(
            square[block * RHS : block * RHS + RHS, :], (start - block * RHS) % LANES, 1
        )
        packed = jnp.where((lane >= start) & (lane < start + width), value, packed)
        start += width
    gram_ref[...] = packed


def powers(own, left, right, front, back, *corner):
    count = GRID * GRID
    return pl.pallas_call(
        powers_kernel,
        out_shape=(
            jax.ShapeDtypeStruct((COMP * COLS, (POWERS + 1) * RHS, LANES), jnp.float32),
            jax.ShapeDtypeStruct((RHS, LANES), jnp.float32),
        ),
        in_specs=[VMEM] * 9,
        out_specs=(VMEM,) * 2,
        scratch_shapes=[
            pltpu.VMEM((2, count * COMP, RHS, LANES), jnp.float32),
            pltpu.VMEM((2, count * COMP, RHS, LANES), jnp.float32),
            pltpu.VMEM((count, 24, LANES), jnp.float32),
            pltpu.VMEM((count, 24, LANES), jnp.float32),
            pltpu.VMEM((count * 6, RHS, LANES), jnp.float32),
            pltpu.VMEM((count * 6, RHS, LANES), jnp.float32),
            pltpu.VMEM((count, RHS, LANES), jnp.float32),
            pltpu.VMEM((count, RHS, LANES), jnp.float32),
            pltpu.VMEM(((POWERS + 1) * RHS, LANES), jnp.float32),
        ],
        compiler_params=pltpu.CompilerParams(vmem_limit_bytes=48 * 2**20),
    )(own, left, right, front, back, *corner)


def finish_kernel(gram_ref, basis_ref, out_ref, factor_ref, square, upper):
    lane = lane_index()
    order = (POWERS + 1) * RHS
    parts = [gram_ref[i] for i in range(gram_ref.shape[0])]
    while len(parts) > 1:
        parts = [
            parts[i] + parts[i + 1] if i + 1 < len(parts) else parts[i]
            for i in range(0, len(parts), 2)
        ]
    packed = parts[0]
    square[...] = jnp.zeros_like(square)
    start = 0
    for block in range(POWERS + 1):
        width = order - block * RHS
        value = pltpu.roll(packed, (block * RHS - start) % LANES, 1)
        keep = (lane >= block * RHS) & (lane < order)
        square[block * RHS : block * RHS + RHS, :] = jnp.where(keep, value, 0.0)
        start += width
    half = square[...]
    other = half.T
    gram = []
    for block in range(POWERS + 1):
        rows = slice(block * RHS, block * RHS + RHS)
        gram.append(jnp.where(lane < block * RHS, other[rows, :], half[rows, :]))
    summed = [tile + pltpu.roll(tile, LANES - RHS, 1) for tile in gram]
    normal = [summed[i] + summed[i + 1] for i in range(POWERS)] + [summed[0]]

    upper[...] = jnp.zeros_like(upper)
    number = lane[0:1, :]

    def pair(matrix, step):
        tile, row = step // RHS, step % RHS
        p, q = matrix[tile][row : row + 1, :], matrix[tile][row + 1 : row + 2, :]
        one = p[:, step : step + 1]
        cross = p[:, step + 1 : step + 2]
        inverse = 1.0 / one
        ratio = cross * inverse
        other = q[:, step + 1 : step + 2] - cross * ratio
        rest = q - ratio * p
        inverse_other = 1.0 / other
        second = rest * inverse_other
        first = p * inverse - ratio * second
        return p, rest, one, other, first, second, inverse, inverse_other, ratio

    for step in range(0, order, 2):
        tile = step // RHS
        p, rest, one, other, first, second, _, _, _ = pair(gram, step)
        upper[step : step + 1, :] = jnp.where(number >= step, p * lax.rsqrt(one), 0.0)
        upper[step + 1 : step + 2, :] = jnp.where(
            number > step, rest * lax.rsqrt(other), 0.0
        )
        low = tile if step % RHS < RHS - 2 else tile + 1
        for i in range(low, POWERS + 1):
            gram[i] = (
                gram[i]
                - gram[i][:, step : step + 1] * first
                - gram[i][:, step + 1 : step + 2] * second
            )
        if step < POWERS * RHS:
            _, _, _, _, first, second, inverse, inverse_other, ratio = pair(normal, step)
            mixed = ratio * inverse_other
            at_one, at_other = number == step, number == step + 1
            first = jnp.where(
                at_one, -(inverse + ratio * mixed), jnp.where(at_other, mixed, first)
            )
            second = jnp.where(at_one, mixed, jnp.where(at_other, -inverse_other, second))
            cleared = (lane == step) | (lane == step + 1)
            for i in range(low, POWERS + 1):
                normal[i] = (
                    jnp.where(cleared, 0.0, normal[i])
                    - normal[i][:, step : step + 1] * first
                    - normal[i][:, step + 1 : step + 2] * second
                )
    factor_ref[...] = upper[0:order, 0:order]
    answer = normal[POWERS]
    weights = [
        jnp.broadcast_to(answer[:, i : i + 1], (RHS, LANES)) for i in range(POWERS * RHS)
    ]

    def combine(tile, carry):
        sums = [None] * 4
        for i in range(POWERS * RHS):
            term = weights[i] * jnp.broadcast_to(basis_ref[tile, i : i + 1, :], (RHS, LANES))
            sums[i % 4] = term if sums[i % 4] is None else sums[i % 4] + term
        out_ref[pl.ds(tile, RHS, stride=COMP * COLS), :] = (sums[0] + sums[1]) + (
            sums[2] + sums[3]
        )
        return carry

    lax.fori_loop(0, COMP * COLS, combine, 0, unroll=4)


def finish(gram, basis):
    order = (POWERS + 1) * RHS
    return pl.pallas_call(
        finish_kernel,
        out_shape=(
            jax.ShapeDtypeStruct((RHS * COMP * COLS, LANES), jnp.float32),
            jax.ShapeDtypeStruct((order, order), jnp.float32),
        ),
        in_specs=[VMEM] * 2,
        out_specs=(VMEM,) * 2,
        scratch_shapes=[
            pltpu.VMEM((LANES, LANES), jnp.float32),
            pltpu.VMEM((order, LANES), jnp.float32),
        ],
        compiler_params=pltpu.CompilerParams(vmem_limit_bytes=6 * 2**20),
    )(gram, basis)


def moved(block, step_x, step_y):
    across, along = lax.axis_size("gx"), lax.axis_size("gy")
    pairs = [
        (x * along + y, (x + step_x) * along + y + step_y)
        for x in range(across)
        for y in range(along)
        if 0 <= x + step_x < across and 0 <= y + step_y < along
    ]
    return lax.ppermute(block, ("gx", "gy"), pairs)


def vertical(low, high):
    count, place = lax.axis_size("gz"), lax.axis_index("gz")
    index = jnp.arange(count)[:, None, None]
    sent = jnp.where(index == place + 1, high[None], jnp.where(index == place - 1, low[None], 0.0))
    return lax.all_to_all(sent, "gz", 0, 0)


def gathered(tile, axes):
    count = lax.axis_size(axes)
    return lax.all_to_all(jnp.broadcast_to(tile[None], (count,) + tile.shape), axes, 0, 0)


def local(residuals, shear_rate, coupling):
    block, low, high = pack(residuals, shear_rate, coupling)
    own, *parts = corners(block, vertical(low, high))
    left, right = moved(own, 1, 0), moved(own, -1, 0)
    corner = [moved(part, *side) for part, side in zip(parts, SIDES)]
    front, back = moved(own, 0, 1), moved(own, 0, -1)
    basis, gram = powers(own, left, right, front, back, *corner)
    gram = jnp.sum(gathered(gram, ("gy", "gz")), axis=0)
    correction, factor = finish(gathered(gram, "gx"), basis)
    return correction.reshape(residuals.shape), factor


def solution(mesh):
    in_specs = (
        P(None, None, "gx", "gy", "gz"),
        P("gx", "gy", "gz"),
        P(None, None, "gx", "gy", "gz"),
    )
    out_specs = (P(None, None, "gx", "gy", "gz"), P())
    return jax.shard_map(local, mesh=mesh, in_specs=in_specs, out_specs=out_specs, check_vma=False)
```

```python
import jax
import jax.numpy as jnp
from jax import lax
from jax.experimental import pallas as pl
from jax.experimental.pallas import tpu as pltpu
from jax.sharding import PartitionSpec as P

POWERS = 4
RHS = 8
COMP = 4
BX = 4
BY = 4
LANES = 128
COLS = BX * BY
GRID = BX + 2 * POWERS
HIGHEST = lax.Precision.HIGHEST
VMEM = pl.BlockSpec(memory_space=pltpu.VMEM)

FIELD_ROWS = COMP * COLS * RHS
LAYER = COMP * COMP * BY
GHOST_ROWS = COMP * RHS + 24
GHOST_AT = LAYER
FIELD_AT = GHOST_AT + GHOST_ROWS
ETA_AT = FIELD_AT + FIELD_ROWS
TAIL_AT = ETA_AT + COLS
BLOCK_ROWS = TAIL_AT + (BX - 1) * LAYER
SIDE_ROWS = BLOCK_ROWS - LAYER

NEAR = [(1, 1), (1, 2), (2, 1)]
FAR = [(1, 3), (2, 2), (3, 1)]
CORNER = [(side, a, b) for a, b in NEAR + FAR for side in (0, 1)]
NEAR_COUNT = 2 * len(NEAR)
C_COUPLE_AT = len(CORNER) * COMP * RHS
C_ETA_AT = C_COUPLE_AT + NEAR_COUNT * 16
C_GHOST_AT = C_ETA_AT + 16
CORNER_ROWS = C_GHOST_AT + GHOST_ROWS


def couple_at(x):
    return TAIL_AT + (x - 1) * LAYER if x else 0


def lane_index():
    return lax.broadcasted_iota(jnp.int32, (RHS, LANES), 1)


def pack_kernel(raw_ref, main_ref, low_ref, high_ref):
    lane = lane_index()
    raw_couple = FIELD_ROWS
    raw_shear = FIELD_ROWS + BX * LAYER
    shear = raw_ref[raw_shear : raw_shear + COLS, :]
    eta = -0.5 * (0.2 + (1.0 - jnp.exp(-100.0 * shear)) / shear)
    main_ref[ETA_AT:TAIL_AT, :] = eta
    main_ref[GHOST_AT:FIELD_AT, :] = jnp.zeros((GHOST_ROWS, LANES), jnp.float32)
    for entry in range(COMP * COMP):
        for x in range(BX):
            start = raw_couple + entry * COLS + x * BY
            row = couple_at(x) + entry * BY
            main_ref[row : row + BY, :] = raw_ref[start : start + BY, :]

    def pack(group, load):
        low = jnp.zeros((RHS, LANES), jnp.float32)
        high = jnp.zeros((RHS, LANES), jnp.float32)
        for col in range(COLS):
            turned = pltpu.roll(load(col), (8 * col + 4) % LANES, 1)
            here = lane // 4
            high = jnp.where(here == 2 * col, turned, high)
            low = jnp.where(here == 2 * col + 1, turned, low)
        low_ref[group * 8 : group * 8 + 8, :] = low
        high_ref[group * 8 : group * 8 + 8, :] = high

    for comp in range(COMP):

        def load_field(col):
            place = comp * COLS + col
            value = raw_ref[pl.ds(place, RHS, stride=COMP * COLS), :]
            row = FIELD_AT + place * RHS
            main_ref[row : row + RHS, :] = value
            return value

        pack(comp, load_field)
    for half in range(2):
        pack(
            COMP + half,
            lambda col: raw_ref[pl.ds(raw_couple + half * 8 * COLS + col, 8, stride=COLS), :],
        )
    pack(
        COMP + 2,
        lambda col: jnp.broadcast_to(eta[col : col + 1, :], (RHS, LANES)),
    )


def pack(residuals, shear_rate, coupling):
    raw = jnp.concatenate(
        [part.reshape(-1, LANES) for part in (residuals, coupling, shear_rate)], axis=0
    )
    return pl.pallas_call(
        pack_kernel,
        out_shape=(
            jax.ShapeDtypeStruct((BLOCK_ROWS, LANES), jnp.float32),
            jax.ShapeDtypeStruct((GHOST_ROWS, LANES), jnp.float32),
            jax.ShapeDtypeStruct((GHOST_ROWS, LANES), jnp.float32),
        ),
        in_specs=[VMEM],
        out_specs=(VMEM,) * 3,
        compiler_params=pltpu.CompilerParams(vmem_limit_bytes=4 * 2**20),
    )(raw)


def corner_kernel(left_ref, right_ref, down_ref, up_ref):
    lane = lane_index()
    for out_ref, top in ((down_ref, False), (up_ref, True)):
        for place, (side, a, b) in enumerate(CORNER):
            src = right_ref if side else left_ref
            base = 0 if side else -LAYER
            x = a - 1 if side else BX - a
            y = BY - b if top else b - 1
            col = x * BY + y
            for comp in range(COMP):
                start = base + FIELD_AT + (comp * COLS + col) * RHS
                row = (place * COMP + comp) * RHS
                out_ref[row : row + RHS, :] = src[start : start + RHS, :]
            if place < NEAR_COUNT:
                for half in range(2):
                    row = C_COUPLE_AT + place * 16 + half * 8
                    start = base + couple_at(x) + half * 8 * BY + y
                    out_ref[row : row + 8, :] = src[pl.ds(start, 8, stride=BY), :]
            start = base + ETA_AT + col
            out_ref[C_ETA_AT + place : C_ETA_AT + place + 1, :] = src[start : start + 1, :]
        out_ref[C_ETA_AT + len(CORNER) : C_GHOST_AT, :] = jnp.zeros(
            (16 - len(CORNER), LANES), jnp.float32
        )
        for row in range(0, GHOST_ROWS, 8):
            right = right_ref[GHOST_AT + row : GHOST_AT + row + 8, :]
            left = left_ref[GHOST_AT - LAYER + row : GHOST_AT - LAYER + row + 8, :]
            out_ref[C_GHOST_AT + row : C_GHOST_AT + row + 8, :] = jnp.where(
                lane < LANES // 2, right, left
            )


def corners(left, right):
    return pl.pallas_call(
        corner_kernel,
        out_shape=(jax.ShapeDtypeStruct((CORNER_ROWS, LANES), jnp.float32),) * 2,
        in_specs=[VMEM] * 2,
        out_specs=(VMEM,) * 2,
        compiler_params=pltpu.CompilerParams(vmem_limit_bytes=4 * 2**20),
    )(left, right)


def distance(place):
    return max(POWERS - place, 0, place - (POWERS + BX - 1))


def powers_kernel(
    own_ref, left_ref, right_ref, front_ref, back_ref, low_ref, high_ref,
    basis_ref, gram_ref,
    main, ghost, coef, coef_ghost, face, face_ghost, scale, scale_ghost, square,
):
    lane = lane_index()
    first, last = lane == 0, lane == LANES - 1

    def slot(x, y):
        return x * GRID + y

    def place_column(src, x, y, field_at, entry_at, couple_stride, eta_at, ghost_at, col):
        reach = distance(x) + distance(y)
        at = slot(x, y)
        for comp in range(COMP):
            main[0, at * COMP + comp] = src[field_at[comp] : field_at[comp] + RHS, :]
        coef[at, 16:24, :] = jnp.broadcast_to(src[eta_at : eta_at + 1, :], (8, LANES))
        if reach >= POWERS:
            return
        for half in range(2):
            start = entry_at + half * 8 * couple_stride
            coef[at, half * 8 : half * 8 + 8, :] = (
                src[pl.ds(start, 8, stride=couple_stride), :]
                if couple_stride > 1
                else src[start : start + 8, :]
            )
        shift = (-8 * col - 4) % LANES
        for comp in range(COMP):
            row = ghost_at + comp * RHS
            ghost[0, at * COMP + comp] = pltpu.roll(src[row : row + RHS, :], shift, 1)
        for part in range(3):
            row = ghost_at + COMP * RHS + part * 8
            coef_ghost[at, part * 8 : part * 8 + 8, :] = pltpu.roll(
                src[row : row + 8, :], shift, 1
            )

    for src, base, off_x, off_y in (
        (own_ref, 0, 0, 0), (left_ref, -LAYER, -1, 0), (right_ref, 0, 1, 0),
        (front_ref, 0, 0, -1), (back_ref, 0, 0, 1),
    ):
        for x in range(BX):
            for y in range(BY):
                col = x * BY + y
                place_column(
                    src, POWERS + off_x * BX + x, POWERS + off_y * BY + y,
                    [base + FIELD_AT + (comp * COLS + col) * RHS for comp in range(COMP)],
                    base + couple_at(x) + y, BY, base + ETA_AT + col, base + GHOST_AT, col,
                )
    for src, top in ((low_ref, True), (high_ref, False)):
        for place, (side, a, b) in enumerate(CORNER):
            x = POWERS + BX - 1 + a if side else POWERS - a
            y = POWERS - b if top else POWERS + BY - 1 + b
            col = (a - 1 if side else BX - a) * BY + (BY - b if top else b - 1)
            place_column(
                src, x, y, [(place * COMP + comp) * RHS for comp in range(COMP)],
                C_COUPLE_AT + place * 16, 1, C_ETA_AT + place, C_GHOST_AT, col,
            )

    def rows_of(reach):
        for x in range(POWERS - reach, POWERS + BX + reach):
            rest = reach - distance(x)
            yield x, range(POWERS - rest, POWERS + BY + rest)

    def shifted(value, other):
        up, down = pltpu.roll(value, LANES - 1, 1), pltpu.roll(value, 1, 1)
        other_up, other_down = pltpu.roll(other, LANES - 1, 1), pltpu.roll(other, 1, 1)
        return (
            jnp.where(last, other_up, up), jnp.where(first, other_down, down),
            jnp.where(last, up, other_up), jnp.where(first, down, other_down),
        )

    def faces(table, out, inverse, x, y, at, eta, up, down):
        around = [
            table[slot(x - 1, y), 16:24, :], table[slot(x + 1, y), 16:24, :],
            table[slot(x, y - 1), 16:24, :], table[slot(x, y + 1), 16:24, :],
            down, up,
        ]
        kappas = [eta + beside for beside in around]
        for index, kappa in enumerate(kappas):
            out[at * 6 + index] = kappa
        total = (kappas[0] + kappas[1]) + (kappas[2] + kappas[3]) + (kappas[4] + kappas[5])
        diagonal = table[at, pl.ds(0, COMP, stride=COMP + 1), :]
        inverse[at, 0:COMP, :] = jnp.where(
            eta[0:COMP, :] < 0.0, 1.0 / (diagonal - total[0:COMP, :]), 0.0
        )

    for x, ys in rows_of(POWERS - 1):
        for y in ys:
            at = slot(x, y)
            eta, eta_ghost = coef[at, 16:24, :], coef_ghost[at, 16:24, :]
            up, down, ghost_up, ghost_down = shifted(eta, eta_ghost)
            faces(coef, face, scale, x, y, at, eta, up, down)
            if distance(x) + distance(y) < POWERS - 1:
                faces(coef_ghost, face_ghost, scale_ghost, x, y, at, eta_ghost, ghost_up, ghost_down)

    def spread(table, at, row):
        return jnp.broadcast_to(table[at, row : row + 1, :], (RHS, LANES))

    def apply(load, table, faces_of, inverse, x, y, before, centre, after, up, down):
        at = slot(x, y)
        kappa = [faces_of[at * 6 + index] for index in range(6)]
        results = []
        for comp in range(COMP):
            beside = [
                load(x - 1, y, comp), load(x + 1, y, comp), before[comp], after[comp],
                down[comp], up[comp],
            ]
            terms = [k * v for k, v in zip(kappa, beside)]
            terms += [
                spread(table, at, comp * COMP + d) * centre[d] for d in range(COMP) if d != comp
            ]
            while len(terms) > 1:
                terms = [
                    terms[i] + terms[i + 1] if i + 1 < len(terms) else terms[i]
                    for i in range(0, len(terms), 2)
                ]
            results.append(terms[0] * spread(inverse, at, comp))
        return results

    for power in range(1, POWERS + 1):
        limit = POWERS - power
        source, target = (power - 1) % 2, power % 2

        def load_main(x, y, comp, source=source):
            return main[source, slot(x, y) * COMP + comp]

        def load_ghost(x, y, comp, source=source):
            return ghost[source, slot(x, y) * COMP + comp]

        for x, ys in rows_of(limit):
            rows = {}

            def at_row(load, y, x=x, rows=rows):
                if (load, y) not in rows:
                    rows[load, y] = [load(x, y, comp) for comp in range(COMP)]
                return rows[load, y]

            for y in ys:
                at = slot(x, y)
                centre, outer = at_row(load_main, y), at_row(load_ghost, y)
                moved = [shifted(c, o) for c, o in zip(centre, outer)]
                results = apply(
                    load_main, coef, face, scale, x, y,
                    at_row(load_main, y - 1), centre, at_row(load_main, y + 1),
                    [m[0] for m in moved], [m[1] for m in moved],
                )
                for comp in range(COMP):
                    if limit:
                        main[target, at * COMP + comp] = results[comp]
                if distance(x) + distance(y) == 0:
                    for comp in range(COMP):
                        tile = comp * COLS + (x - POWERS) * BY + (y - POWERS)
                        if power == 1:
                            basis_ref[tile, 0:RHS, :] = centre[comp]
                        basis_ref[tile, power * RHS : power * RHS + RHS, :] = results[comp]
                if distance(x) + distance(y) < limit:
                    outside = apply(
                        load_ghost, coef_ghost, face_ghost, scale_ghost, x, y,
                        at_row(load_ghost, y - 1), outer, at_row(load_ghost, y + 1),
                        [m[2] for m in moved], [m[3] for m in moved],
                    )
                    for comp in range(COMP):
                        ghost[target, at * COMP + comp] = outside[comp]

    order = (POWERS + 1) * RHS
    total = jnp.zeros((order, order), jnp.float32)
    for tile in range(0, COMP * COLS, 2):
        both = jnp.concatenate([basis_ref[tile], basis_ref[tile + 1]], axis=1)
        total = total + lax.dot_general(
            both, both, (((1,), (1,)), ((), ())),
            precision=HIGHEST, preferred_element_type=jnp.float32,
        )
    square[...] = jnp.zeros_like(square)
    square[:, 0:order] = total
    packed = jnp.zeros((RHS, LANES), jnp.float32)
    start = 0
    for block in range(POWERS + 1):
        width = order - block * RHS
        value = pltpu.roll(
            square[block * RHS : block * RHS + RHS, :], (start - block * RHS) % LANES, 1
        )
        packed = jnp.where((lane >= start) & (lane < start + width), value, packed)
        start += width
    gram_ref[...] = packed


def powers(*parts):
    count = GRID * GRID
    return pl.pallas_call(
        powers_kernel,
        out_shape=(
            jax.ShapeDtypeStruct((COMP * COLS, (POWERS + 1) * RHS, LANES), jnp.float32),
            jax.ShapeDtypeStruct((RHS, LANES), jnp.float32),
        ),
        in_specs=[VMEM] * 7,
        out_specs=(VMEM,) * 2,
        scratch_shapes=[
            pltpu.VMEM((2, count * COMP, RHS, LANES), jnp.float32),
            pltpu.VMEM((2, count * COMP, RHS, LANES), jnp.float32),
            pltpu.VMEM((count, 24, LANES), jnp.float32),
            pltpu.VMEM((count, 24, LANES), jnp.float32),
            pltpu.VMEM((count * 6, RHS, LANES), jnp.float32),
            pltpu.VMEM((count * 6, RHS, LANES), jnp.float32),
            pltpu.VMEM((count, RHS, LANES), jnp.float32),
            pltpu.VMEM((count, RHS, LANES), jnp.float32),
            pltpu.VMEM(((POWERS + 1) * RHS, LANES), jnp.float32),
        ],
        compiler_params=pltpu.CompilerParams(vmem_limit_bytes=48 * 2**20),
    )(*parts)


def finish_kernel(gram_ref, basis_ref, out_ref, factor_ref, square, upper):
    lane = lane_index()
    order = (POWERS + 1) * RHS
    parts = [gram_ref[i] for i in range(gram_ref.shape[0])]
    while len(parts) > 1:
        parts = [
            parts[i] + parts[i + 1] if i + 1 < len(parts) else parts[i]
            for i in range(0, len(parts), 2)
        ]
    packed = parts[0]
    square[...] = jnp.zeros_like(square)
    start = 0
    for block in range(POWERS + 1):
        width = order - block * RHS
        value = pltpu.roll(packed, (block * RHS - start) % LANES, 1)
        keep = (lane >= block * RHS) & (lane < order)
        square[block * RHS : block * RHS + RHS, :] = jnp.where(keep, value, 0.0)
        start += width
    half = square[...]
    other = half.T
    gram = []
    for block in range(POWERS + 1):
        rows = slice(block * RHS, block * RHS + RHS)
        gram.append(jnp.where(lane < block * RHS, other[rows, :], half[rows, :]))
    summed = [tile + pltpu.roll(tile, LANES - RHS, 1) for tile in gram]
    normal = [summed[i] + summed[i + 1] for i in range(POWERS)] + [summed[0]]

    upper[...] = jnp.zeros_like(upper)
    number = lane[0:1, :]

    def wide(value, column):
        return jnp.broadcast_to(value[:, column : column + 1], value.shape)

    def pair(matrix, step):
        tile, row = step // RHS, step % RHS
        p, q = matrix[tile][row : row + 1, :], matrix[tile][row + 1 : row + 2, :]
        one, cross, far = wide(p, step), wide(p, step + 1), wide(q, step + 1)
        inverse = 1.0 / one
        ratio = cross * inverse
        other = far - cross * ratio
        rest = q - ratio * p
        inverse_other = 1.0 / other
        second = rest * inverse_other
        first = p * inverse - ratio * second
        return p, rest, one, other, first, second, inverse, inverse_other, ratio

    for step in range(0, order, 2):
        tile = step // RHS
        low = tile if step % RHS < RHS - 2 else tile + 1
        p, rest, one, other, first, second, _, _, _ = pair(gram, step)
        top = jnp.where(number >= step, p * lax.rsqrt(one), 0.0)
        bottom = jnp.where(number > step, rest * lax.rsqrt(other), 0.0)
        upper[step : step + 1, :] = top[0:1, :]
        upper[step + 1 : step + 2, :] = bottom[0:1, :]
        for i in range(low, POWERS + 1):
            gram[i] = gram[i] - wide(gram[i], step) * first - wide(gram[i], step + 1) * second
        if step < POWERS * RHS:
            _, _, _, _, first, second, inverse, inverse_other, ratio = pair(normal, step)
            mixed = ratio * inverse_other
            at_one, at_other = number == step, number == step + 1
            cleared = (lane == step) | (lane == step + 1)
            first = jnp.where(
                at_one, -(inverse + ratio * mixed), jnp.where(at_other, mixed, first)
            )
            second = jnp.where(at_one, mixed, jnp.where(at_other, -inverse_other, second))
            for i in range(low, POWERS + 1):
                normal[i] = (
                    jnp.where(cleared, 0.0, normal[i])
                    - wide(normal[i], step) * first
                    - wide(normal[i], step + 1) * second
                )
    factor_ref[...] = upper[0:order, 0:order]
    answer = normal[POWERS]
    weights = [
        jnp.broadcast_to(answer[:, i : i + 1], (RHS, LANES)) for i in range(POWERS * RHS)
    ]

    def combine(tile, carry):
        sums = [None] * 4
        for i in range(POWERS * RHS):
            term = weights[i] * jnp.broadcast_to(basis_ref[tile, i : i + 1, :], (RHS, LANES))
            sums[i % 4] = term if sums[i % 4] is None else sums[i % 4] + term
        out_ref[pl.ds(tile, RHS, stride=COMP * COLS), :] = (sums[0] + sums[1]) + (
            sums[2] + sums[3]
        )
        return carry

    lax.fori_loop(0, COMP * COLS, combine, 0, unroll=4)


def finish(gram, basis):
    order = (POWERS + 1) * RHS
    return pl.pallas_call(
        finish_kernel,
        out_shape=(
            jax.ShapeDtypeStruct((RHS * COMP * COLS, LANES), jnp.float32),
            jax.ShapeDtypeStruct((order, order), jnp.float32),
        ),
        in_specs=[VMEM] * 2,
        out_specs=(VMEM,) * 2,
        scratch_shapes=[
            pltpu.VMEM((LANES, LANES), jnp.float32),
            pltpu.VMEM((order, LANES), jnp.float32),
        ],
        compiler_params=pltpu.CompilerParams(vmem_limit_bytes=6 * 2**20),
    )(gram, basis)


def moved(block, axis, step):
    count = lax.axis_size(axis)
    pairs = [(i, i + step) for i in range(count) if 0 <= i + step < count]
    return lax.ppermute(block, axis, pairs)


def vertical(low, high):
    count, place = lax.axis_size("gz"), lax.axis_index("gz")
    index = jnp.arange(count)[:, None, None]
    sent = jnp.where(index == place + 1, high[None], jnp.where(index == place - 1, low[None], 0.0))
    return lax.all_to_all(sent, "gz", 0, 0)


def gathered(tile, axes):
    count = lax.axis_size(axes)
    return lax.all_to_all(jnp.broadcast_to(tile[None], (count,) + tile.shape), axes, 0, 0)


def local(residuals, shear_rate, coupling):
    block, low, high = pack(residuals, shear_rate, coupling)
    ghosts = jnp.sum(vertical(low, high), axis=0)
    own = lax.dynamic_update_slice(block, ghosts, (GHOST_AT, 0))
    left, right = moved(own[LAYER:], "gx", 1), moved(own[:SIDE_ROWS], "gx", -1)
    front, back = moved(own, "gy", 1), moved(own, "gy", -1)
    down, up = corners(left, right)
    low_corner, high_corner = moved(up, "gy", 1), moved(down, "gy", -1)
    basis, gram = powers(own, left, right, front, back, low_corner, high_corner)
    gram = jnp.sum(gathered(gram, ("gy", "gz")), axis=0)
    correction, factor = finish(gathered(gram, "gx"), basis)
    return correction.reshape(residuals.shape), factor


def solution(mesh):
    in_specs = (
        P(None, None, "gx", "gy", "gz"),
        P("gx", "gy", "gz"),
        P(None, None, "gx", "gy", "gz"),
    )
    out_specs = (P(None, None, "gx", "gy", "gz"), P())
    return jax.shard_map(local, mesh=mesh, in_specs=in_specs, out_specs=out_specs, check_vma=False)
```

```python
import jax
import jax.numpy as jnp
from jax import lax
from jax.experimental import pallas as pl
from jax.experimental.pallas import tpu as pltpu
from jax.sharding import PartitionSpec as P

POWERS = 4
RHS = 8
COMP = 4
BX = 4
BY = 4
LANES = 128
COLS = BX * BY
GRID = BX + 2 * POWERS
HIGHEST = lax.Precision.HIGHEST
VMEM = pl.BlockSpec(memory_space=pltpu.VMEM)

FIELD_ROWS = COMP * COLS * RHS
LAYER = COMP * COMP * BY
GHOST_ROWS = COMP * RHS + 24
GHOST_AT = LAYER
FIELD_AT = GHOST_AT + GHOST_ROWS
ETA_AT = FIELD_AT + FIELD_ROWS
TAIL_AT = ETA_AT + COLS
BLOCK_ROWS = TAIL_AT + (BX - 1) * LAYER
SIDE_ROWS = BLOCK_ROWS - LAYER

NEAR = [(1, 1), (1, 2), (2, 1)]
FAR = [(1, 3), (2, 2), (3, 1)]
CORNER = [(side, a, b) for a, b in NEAR + FAR for side in (0, 1)]
NEAR_COUNT = 2 * len(NEAR)
C_COUPLE_AT = len(CORNER) * COMP * RHS
C_ETA_AT = C_COUPLE_AT + NEAR_COUNT * 16
C_GHOST_AT = C_ETA_AT + 16
CORNER_ROWS = C_GHOST_AT + GHOST_ROWS


def couple_at(x):
    return TAIL_AT + (x - 1) * LAYER if x else 0


def lane_index():
    return lax.broadcasted_iota(jnp.int32, (RHS, LANES), 1)


def pack_kernel(raw_ref, main_ref, low_ref, high_ref):
    lane = lane_index()
    raw_couple = FIELD_ROWS
    raw_shear = FIELD_ROWS + BX * LAYER
    shear = raw_ref[raw_shear : raw_shear + COLS, :]
    eta = -0.5 * (0.2 + (1.0 - jnp.exp(-100.0 * shear)) / shear)
    main_ref[ETA_AT:TAIL_AT, :] = eta
    main_ref[GHOST_AT:FIELD_AT, :] = jnp.zeros((GHOST_ROWS, LANES), jnp.float32)
    for entry in range(COMP * COMP):
        for x in range(BX):
            start = raw_couple + entry * COLS + x * BY
            row = couple_at(x) + entry * BY
            main_ref[row : row + BY, :] = raw_ref[start : start + BY, :]

    def pack(group, load):
        low = jnp.zeros((RHS, LANES), jnp.float32)
        high = jnp.zeros((RHS, LANES), jnp.float32)
        for col in range(COLS):
            turned = pltpu.roll(load(col), (8 * col + 4) % LANES, 1)
            here = lane // 4
            high = jnp.where(here == 2 * col, turned, high)
            low = jnp.where(here == 2 * col + 1, turned, low)
        low_ref[group * 8 : group * 8 + 8, :] = low
        high_ref[group * 8 : group * 8 + 8, :] = high

    for comp in range(COMP):

        def load_field(col):
            place = comp * COLS + col
            value = raw_ref[pl.ds(place, RHS, stride=COMP * COLS), :]
            row = FIELD_AT + place * RHS
            main_ref[row : row + RHS, :] = value
            return value

        pack(comp, load_field)
    for half in range(2):
        pack(
            COMP + half,
            lambda col: raw_ref[pl.ds(raw_couple + half * 8 * COLS + col, 8, stride=COLS), :],
        )
    pack(
        COMP + 2,
        lambda col: jnp.broadcast_to(eta[col : col + 1, :], (RHS, LANES)),
    )


def pack(residuals, shear_rate, coupling):
    raw = jnp.concatenate(
        [part.reshape(-1, LANES) for part in (residuals, coupling, shear_rate)], axis=0
    )
    return pl.pallas_call(
        pack_kernel,
        out_shape=(
            jax.ShapeDtypeStruct((BLOCK_ROWS, LANES), jnp.float32),
            jax.ShapeDtypeStruct((GHOST_ROWS, LANES), jnp.float32),
            jax.ShapeDtypeStruct((GHOST_ROWS, LANES), jnp.float32),
        ),
        in_specs=[VMEM],
        out_specs=(VMEM,) * 3,
        compiler_params=pltpu.CompilerParams(vmem_limit_bytes=4 * 2**20),
    )(raw)


def corner_kernel(left_ref, right_ref, down_ref, up_ref):
    lane = lane_index()
    for out_ref, top in ((down_ref, False), (up_ref, True)):
        for place, (side, a, b) in enumerate(CORNER):
            src = right_ref if side else left_ref
            base = 0 if side else -LAYER
            x = a - 1 if side else BX - a
            y = BY - b if top else b - 1
            col = x * BY + y
            for comp in range(COMP):
                start = base + FIELD_AT + (comp * COLS + col) * RHS
                row = (place * COMP + comp) * RHS
                out_ref[row : row + RHS, :] = src[start : start + RHS, :]
            if place < NEAR_COUNT:
                for half in range(2):
                    row = C_COUPLE_AT + place * 16 + half * 8
                    start = base + couple_at(x) + half * 8 * BY + y
                    out_ref[row : row + 8, :] = src[pl.ds(start, 8, stride=BY), :]
            start = base + ETA_AT + col
            out_ref[C_ETA_AT + place : C_ETA_AT + place + 1, :] = src[start : start + 1, :]
        out_ref[C_ETA_AT + len(CORNER) : C_GHOST_AT, :] = jnp.zeros(
            (16 - len(CORNER), LANES), jnp.float32
        )
        for row in range(0, GHOST_ROWS, 8):
            right = right_ref[GHOST_AT + row : GHOST_AT + row + 8, :]
            left = left_ref[GHOST_AT - LAYER + row : GHOST_AT - LAYER + row + 8, :]
            out_ref[C_GHOST_AT + row : C_GHOST_AT + row + 8, :] = jnp.where(
                lane < LANES // 2, right, left
            )


def corners(left, right):
    return pl.pallas_call(
        corner_kernel,
        out_shape=(jax.ShapeDtypeStruct((CORNER_ROWS, LANES), jnp.float32),) * 2,
        in_specs=[VMEM] * 2,
        out_specs=(VMEM,) * 2,
        compiler_params=pltpu.CompilerParams(vmem_limit_bytes=4 * 2**20),
    )(left, right)


def distance(place):
    return max(POWERS - place, 0, place - (POWERS + BX - 1))


def corner(x, y):
    return distance(x) > 0 and distance(y) > 0


def rows_of(reach):
    for x in range(POWERS - reach, POWERS + BX + reach):
        rest = reach - distance(x)
        yield x, range(POWERS - rest, POWERS + BY + rest)


PLACES = [(x, y) for x, ys in rows_of(POWERS) for y in ys]
SLOT = {place: i for i, place in enumerate(sorted(PLACES, key=lambda place: corner(*place)))}
EARLY = sum(not corner(*place) for place in PLACES)


def ready(x, y, power):
    if power == 0:
        return not corner(x, y)
    around = ((x, y), (x - 1, y), (x + 1, y), (x, y - 1), (x, y + 1))
    return all(ready(i, j, power - 1) for i, j in around)


def state_shapes(count):
    field = (count * COMP, RHS, LANES)
    return (
        [field] * 4 + [(count, 24, LANES)] * 2 + [(count * 6, RHS, LANES)] * 2
        + [(count, RHS, LANES)] * 2
    )


def powers_part(early, blocks, first_state, mine, basis_ref):
    lane = lane_index()
    first, last = lane == 0, lane == LANES - 1
    MAIN, GHOST, COEF, FACE, SCALE = 0, 2, 4, 6, 8

    def held(kind, x, y, power):
        return first_state[kind] if early or ready(x, y, power) else mine[kind]

    def place_column(src, x, y, field_at, entry_at, stride, eta_at, ghost_at, col):
        at = SLOT[x, y]
        for comp in range(COMP):
            mine[MAIN][at * COMP + comp] = src[field_at[comp] : field_at[comp] + RHS, :]
        mine[COEF][at, 16:24, :] = jnp.broadcast_to(src[eta_at : eta_at + 1, :], (8, LANES))
        if distance(x) + distance(y) >= POWERS:
            return
        for half in range(2):
            start = entry_at + half * 8 * stride
            mine[COEF][at, half * 8 : half * 8 + 8, :] = (
                src[pl.ds(start, 8, stride=stride), :] if stride > 1 else src[start : start + 8, :]
            )
        shift = (-8 * col - 4) % LANES
        for comp in range(COMP):
            row = ghost_at + comp * RHS
            mine[GHOST][at * COMP + comp] = pltpu.roll(src[row : row + RHS, :], shift, 1)
        for part in range(3):
            row = ghost_at + COMP * RHS + part * 8
            mine[COEF + 1][at, part * 8 : part * 8 + 8, :] = pltpu.roll(
                src[row : row + 8, :], shift, 1
            )

    if early:
        own_ref, left_ref, right_ref, front_ref, back_ref = blocks
        for src, base, off_x, off_y in (
            (own_ref, 0, 0, 0), (left_ref, -LAYER, -1, 0), (right_ref, 0, 1, 0),
            (front_ref, 0, 0, -1), (back_ref, 0, 0, 1),
        ):
            for x in range(BX):
                for y in range(BY):
                    col = x * BY + y
                    place_column(
                        src, POWERS + off_x * BX + x, POWERS + off_y * BY + y,
                        [base + FIELD_AT + (comp * COLS + col) * RHS for comp in range(COMP)],
                        base + couple_at(x) + y, BY, base + ETA_AT + col, base + GHOST_AT, col,
                    )
    else:
        low_ref, high_ref = blocks
        for src, top in ((low_ref, True), (high_ref, False)):
            for place, (side, a, b) in enumerate(CORNER):
                x = POWERS + BX - 1 + a if side else POWERS - a
                y = POWERS - b if top else POWERS + BY - 1 + b
                col = (a - 1 if side else BX - a) * BY + (BY - b if top else b - 1)
                place_column(
                    src, x, y, [(place * COMP + comp) * RHS for comp in range(COMP)],
                    C_COUPLE_AT + place * 16, 1, C_ETA_AT + place, C_GHOST_AT, col,
                )

    def shifted(value, other):
        up, down = pltpu.roll(value, LANES - 1, 1), pltpu.roll(value, 1, 1)
        other_up, other_down = pltpu.roll(other, LANES - 1, 1), pltpu.roll(other, 1, 1)
        return (
            jnp.where(last, other_up, up), jnp.where(first, other_down, down),
            jnp.where(last, up, other_up), jnp.where(first, down, other_down),
        )

    def eta_at(kind, x, y):
        return held(kind, x, y, 0)[SLOT[x, y], 16:24, :]

    def faces(outer, x, y, eta, up, down):
        kind, at = COEF + outer, SLOT[x, y]
        around = [
            eta_at(kind, x - 1, y), eta_at(kind, x + 1, y),
            eta_at(kind, x, y - 1), eta_at(kind, x, y + 1), down, up,
        ]
        kappas = [eta + beside for beside in around]
        for index, kappa in enumerate(kappas):
            mine[FACE + outer][at * 6 + index] = kappa
        total = (kappas[0] + kappas[1]) + (kappas[2] + kappas[3]) + (kappas[4] + kappas[5])
        diagonal = held(kind, x, y, 0)[at, pl.ds(0, COMP, stride=COMP + 1), :]
        mine[SCALE + outer][at, 0:COMP, :] = jnp.where(
            eta[0:COMP, :] < 0.0, 1.0 / (diagonal - total[0:COMP, :]), 0.0
        )

    for x, ys in rows_of(POWERS - 1):
        for y in ys:
            if ready(x, y, 1) != early:
                continue
            eta, eta_ghost = eta_at(COEF, x, y), eta_at(COEF + 1, x, y)
            up, down, ghost_up, ghost_down = shifted(eta, eta_ghost)
            faces(0, x, y, eta, up, down)
            if distance(x) + distance(y) < POWERS - 1:
                faces(1, x, y, eta_ghost, ghost_up, ghost_down)

    def spread(ref, at, row):
        return jnp.broadcast_to(ref[at, row : row + 1, :], (RHS, LANES))

    def apply(outer, power, x, y, before, centre, after, up, down):
        at = SLOT[x, y]
        table = held(COEF + outer, x, y, 0)
        faces_of, inverse = held(FACE + outer, x, y, 1), held(SCALE + outer, x, y, 1)
        kappa = [faces_of[at * 6 + index] for index in range(6)]
        results = []
        for comp in range(COMP):
            beside = [
                load(outer, power, x - 1, y, comp), load(outer, power, x + 1, y, comp),
                before[comp], after[comp], down[comp], up[comp],
            ]
            terms = [k * v for k, v in zip(kappa, beside)]
            terms += [
                spread(table, at, comp * COMP + d) * centre[d] for d in range(COMP) if d != comp
            ]
            while len(terms) > 1:
                terms = [
                    terms[i] + terms[i + 1] if i + 1 < len(terms) else terms[i]
                    for i in range(0, len(terms), 2)
                ]
            results.append(terms[0] * spread(inverse, at, comp))
        return results

    def load(outer, power, x, y, comp):
        kind = (GHOST if outer else MAIN) + power % 2
        return held(kind, x, y, power)[SLOT[x, y] * COMP + comp]

    for power in range(1, POWERS + 1):
        limit = POWERS - power
        for x, ys in rows_of(limit):
            rows = {}

            def at_row(outer, y, x=x, rows=rows, power=power):
                if (outer, y) not in rows:
                    rows[outer, y] = [load(outer, power - 1, x, y, comp) for comp in range(COMP)]
                return rows[outer, y]

            for y in ys:
                if ready(x, y, power) != early:
                    continue
                at = SLOT[x, y]
                reach = distance(x) + distance(y)
                centre, outer = at_row(0, y), at_row(1, y)
                moves = [shifted(c, o) for c, o in zip(centre, outer)]
                results = apply(
                    0, power - 1, x, y, at_row(0, y - 1), centre, at_row(0, y + 1),
                    [m[0] for m in moves], [m[1] for m in moves],
                )
                for comp in range(COMP):
                    if limit:
                        mine[MAIN + power % 2][at * COMP + comp] = results[comp]
                if reach == 0:
                    for comp in range(COMP):
                        tile = comp * COLS + (x - POWERS) * BY + (y - POWERS)
                        if power == 1:
                            basis_ref[tile, 0:RHS, :] = centre[comp]
                        basis_ref[tile, power * RHS : power * RHS + RHS, :] = results[comp]
                if reach < limit:
                    outside = apply(
                        1, power - 1, x, y, at_row(1, y - 1), outer, at_row(1, y + 1),
                        [m[2] for m in moves], [m[3] for m in moves],
                    )
                    for comp in range(COMP):
                        mine[GHOST + power % 2][at * COMP + comp] = outside[comp]


def early_kernel(*refs):
    powers_part(True, refs[:5], refs[5:15], refs[5:15], refs[15])


def late_kernel(*refs):
    blocks, first_state, early_basis = refs[:2], refs[2:12], refs[12]
    basis_ref, gram_ref, mine, square = refs[13], refs[14], refs[15:25], refs[25]
    for x in range(BX):
        for y in range(BY):
            for power in range(1, POWERS + 1):
                if ready(POWERS + x, POWERS + y, power):
                    start = 0 if power == 1 else power * RHS
                    stop = power * RHS + RHS
                    for comp in range(COMP):
                        tile = comp * COLS + x * BY + y
                        basis_ref[tile, start:stop, :] = early_basis[tile, start:stop, :]
    powers_part(False, blocks, first_state, mine, basis_ref)
    lane = lane_index()
    order = (POWERS + 1) * RHS
    total = jnp.zeros((order, order), jnp.float32)
    for tile in range(0, COMP * COLS, 2):
        both = jnp.concatenate([basis_ref[tile], basis_ref[tile + 1]], axis=1)
        total = total + lax.dot_general(
            both, both, (((1,), (1,)), ((), ())),
            precision=HIGHEST, preferred_element_type=jnp.float32,
        )
    square[...] = jnp.zeros_like(square)
    square[:, 0:order] = total
    packed = jnp.zeros((RHS, LANES), jnp.float32)
    start = 0
    for block in range(POWERS + 1):
        width = order - block * RHS
        value = pltpu.roll(
            square[block * RHS : block * RHS + RHS, :], (start - block * RHS) % LANES, 1
        )
        packed = jnp.where((lane >= start) & (lane < start + width), value, packed)
        start += width
    gram_ref[...] = packed


def early_powers(*blocks):
    basis = (COMP * COLS, (POWERS + 1) * RHS, LANES)
    return pl.pallas_call(
        early_kernel,
        out_shape=[
            jax.ShapeDtypeStruct(shape, jnp.float32) for shape in state_shapes(EARLY) + [basis]
        ],
        in_specs=[VMEM] * 5,
        out_specs=[VMEM] * 11,
        compiler_params=pltpu.CompilerParams(vmem_limit_bytes=20 * 2**20),
        cost_estimate=pl.CostEstimate(flops=5_000_000, bytes_accessed=8_000_000, transcendentals=0),
    )(*blocks)


def late_powers(low, high, state):
    basis = (COMP * COLS, (POWERS + 1) * RHS, LANES)
    return pl.pallas_call(
        late_kernel,
        out_shape=(
            jax.ShapeDtypeStruct(basis, jnp.float32),
            jax.ShapeDtypeStruct((RHS, LANES), jnp.float32),
        ),
        in_specs=[VMEM] * 13,
        out_specs=(VMEM,) * 2,
        scratch_shapes=[pltpu.VMEM(shape, jnp.float32) for shape in state_shapes(len(PLACES))]
        + [pltpu.VMEM(((POWERS + 1) * RHS, LANES), jnp.float32)],
        compiler_params=pltpu.CompilerParams(vmem_limit_bytes=36 * 2**20),
    )(low, high, *state)


def finish_kernel(gram_ref, basis_ref, out_ref, factor_ref, square, upper):
    lane = lane_index()
    order = (POWERS + 1) * RHS
    parts = [gram_ref[i] for i in range(gram_ref.shape[0])]
    while len(parts) > 1:
        parts = [
            parts[i] + parts[i + 1] if i + 1 < len(parts) else parts[i]
            for i in range(0, len(parts), 2)
        ]
    packed = parts[0]
    square[...] = jnp.zeros_like(square)
    start = 0
    for block in range(POWERS + 1):
        width = order - block * RHS
        value = pltpu.roll(packed, (block * RHS - start) % LANES, 1)
        keep = (lane >= block * RHS) & (lane < order)
        square[block * RHS : block * RHS + RHS, :] = jnp.where(keep, value, 0.0)
        start += width
    half = square[...]
    other = half.T
    gram = []
    for block in range(POWERS + 1):
        rows = slice(block * RHS, block * RHS + RHS)
        gram.append(jnp.where(lane < block * RHS, other[rows, :], half[rows, :]))
    summed = [tile + pltpu.roll(tile, LANES - RHS, 1) for tile in gram]
    normal = [summed[i] + summed[i + 1] for i in range(POWERS)] + [summed[0]]

    upper[...] = jnp.zeros_like(upper)
    number = lane[0:1, :]

    def wide(value, column):
        return jnp.broadcast_to(value[:, column : column + 1], value.shape)

    def pair(matrix, step):
        tile, row = step // RHS, step % RHS
        p, q = matrix[tile][row : row + 1, :], matrix[tile][row + 1 : row + 2, :]
        one, cross, far = wide(p, step), wide(p, step + 1), wide(q, step + 1)
        inverse = 1.0 / one
        ratio = cross * inverse
        other = far - cross * ratio
        rest = q - ratio * p
        inverse_other = 1.0 / other
        second = rest * inverse_other
        first = p * inverse - ratio * second
        return p, rest, one, other, first, second, inverse, inverse_other, ratio

    for step in range(0, order, 2):
        tile = step // RHS
        low = tile if step % RHS < RHS - 2 else tile + 1
        p, rest, one, other, first, second, _, _, _ = pair(gram, step)
        top = jnp.where(number >= step, p * lax.rsqrt(one), 0.0)
        bottom = jnp.where(number > step, rest * lax.rsqrt(other), 0.0)
        upper[step : step + 1, :] = top[0:1, :]
        upper[step + 1 : step + 2, :] = bottom[0:1, :]
        for i in range(low, POWERS + 1):
            gram[i] = gram[i] - wide(gram[i], step) * first - wide(gram[i], step + 1) * second
        if step < POWERS * RHS:
            _, _, _, _, first, second, inverse, inverse_other, ratio = pair(normal, step)
            mixed = ratio * inverse_other
            at_one, at_other = number == step, number == step + 1
            cleared = (lane == step) | (lane == step + 1)
            first = jnp.where(
                at_one, -(inverse + ratio * mixed), jnp.where(at_other, mixed, first)
            )
            second = jnp.where(at_one, mixed, jnp.where(at_other, -inverse_other, second))
            for i in range(low, POWERS + 1):
                normal[i] = (
                    jnp.where(cleared, 0.0, normal[i])
                    - wide(normal[i], step) * first
                    - wide(normal[i], step + 1) * second
                )
    factor_ref[...] = upper[0:order, 0:order]
    answer = normal[POWERS]
    weights = [
        jnp.broadcast_to(answer[:, i : i + 1], (RHS, LANES)) for i in range(POWERS * RHS)
    ]

    def combine(tile, carry):
        sums = [None] * 4
        for i in range(POWERS * RHS):
            term = weights[i] * jnp.broadcast_to(basis_ref[tile, i : i + 1, :], (RHS, LANES))
            sums[i % 4] = term if sums[i % 4] is None else sums[i % 4] + term
        out_ref[pl.ds(tile, RHS, stride=COMP * COLS), :] = (sums[0] + sums[1]) + (
            sums[2] + sums[3]
        )
        return carry

    lax.fori_loop(0, COMP * COLS, combine, 0, unroll=4)


def finish(gram, basis):
    order = (POWERS + 1) * RHS
    return pl.pallas_call(
        finish_kernel,
        out_shape=(
            jax.ShapeDtypeStruct((RHS * COMP * COLS, LANES), jnp.float32),
            jax.ShapeDtypeStruct((order, order), jnp.float32),
        ),
        in_specs=[VMEM] * 2,
        out_specs=(VMEM,) * 2,
        scratch_shapes=[
            pltpu.VMEM((LANES, LANES), jnp.float32),
            pltpu.VMEM((order, LANES), jnp.float32),
        ],
        compiler_params=pltpu.CompilerParams(vmem_limit_bytes=6 * 2**20),
    )(gram, basis)


def moved(block, axis, step):
    count = lax.axis_size(axis)
    pairs = [(i, i + step) for i in range(count) if 0 <= i + step < count]
    return lax.ppermute(block, axis, pairs)


def vertical(low, high):
    count, place = lax.axis_size("gz"), lax.axis_index("gz")
    index = jnp.arange(count)[:, None, None]
    sent = jnp.where(index == place + 1, high[None], jnp.where(index == place - 1, low[None], 0.0))
    return lax.all_to_all(sent, "gz", 0, 0)


def gathered(tile, axes):
    count = lax.axis_size(axes)
    return lax.all_to_all(jnp.broadcast_to(tile[None], (count,) + tile.shape), axes, 0, 0)


def local(residuals, shear_rate, coupling):
    block, low, high = pack(residuals, shear_rate, coupling)
    ghosts = jnp.sum(vertical(low, high), axis=0)
    own = lax.dynamic_update_slice(block, ghosts, (GHOST_AT, 0))
    left, right = moved(own[LAYER:], "gx", 1), moved(own[:SIDE_ROWS], "gx", -1)
    front, back = moved(own, "gy", 1), moved(own, "gy", -1)
    down, up = corners(left, right)
    low_corner, high_corner = moved(up, "gy", 1), moved(down, "gy", -1)
    state = early_powers(own, left, right, front, back)
    basis, gram = late_powers(low_corner, high_corner, state)
    gram = jnp.sum(gathered(gram, ("gy", "gz")), axis=0)
    correction, factor = finish(gathered(gram, "gx"), basis)
    return correction.reshape(residuals.shape), factor


def solution(mesh):
    in_specs = (
        P(None, None, "gx", "gy", "gz"),
        P("gx", "gy", "gz"),
        P(None, None, "gx", "gy", "gz"),
    )
    out_specs = (P(None, None, "gx", "gy", "gz"), P())
    return jax.shard_map(local, mesh=mesh, in_specs=in_specs, out_specs=out_specs, check_vma=False)
```

```python
import jax
import jax.numpy as jnp
from jax import lax
from jax.experimental import pallas as pl
from jax.experimental.pallas import tpu as pltpu
from jax.sharding import PartitionSpec as P

POWERS = 4
RHS = 8
COMP = 4
BX = 4
BY = 4
LANES = 128
COLS = BX * BY
GRID = BX + 2 * POWERS
HIGHEST = lax.Precision.HIGHEST
VMEM = pl.BlockSpec(memory_space=pltpu.VMEM)

FIELD_ROWS = COMP * COLS * RHS
LAYER = COMP * COMP * BY
GHOST_ROWS = COMP * RHS + 24
GHOST_AT = LAYER
FIELD_AT = GHOST_AT + GHOST_ROWS
ETA_AT = FIELD_AT + FIELD_ROWS
TAIL_AT = ETA_AT + COLS
BLOCK_ROWS = TAIL_AT + (BX - 1) * LAYER
SIDE_ROWS = BLOCK_ROWS - LAYER

NEAR = [(1, 1), (1, 2), (2, 1)]
FAR = [(1, 3), (2, 2), (3, 1)]
CORNER = [(side, a, b) for a, b in NEAR + FAR for side in (0, 1)]
NEAR_COUNT = 2 * len(NEAR)
C_COUPLE_AT = len(CORNER) * COMP * RHS
C_ETA_AT = C_COUPLE_AT + NEAR_COUNT * 16
C_GHOST_AT = C_ETA_AT + 16
CORNER_ROWS = C_GHOST_AT + GHOST_ROWS


def couple_at(x):
    return TAIL_AT + (x - 1) * LAYER if x else 0


def lane_index():
    return lax.broadcasted_iota(jnp.int32, (RHS, LANES), 1)


def pack_kernel(raw_ref, main_ref, low_ref, high_ref):
    lane = lane_index()
    raw_couple = FIELD_ROWS
    raw_shear = FIELD_ROWS + BX * LAYER
    shear = raw_ref[raw_shear : raw_shear + COLS, :]
    eta = -0.5 * (0.2 + (1.0 - jnp.exp(-100.0 * shear)) / shear)
    main_ref[ETA_AT:TAIL_AT, :] = eta
    main_ref[GHOST_AT:FIELD_AT, :] = jnp.zeros((GHOST_ROWS, LANES), jnp.float32)
    for entry in range(COMP * COMP):
        for x in range(BX):
            start = raw_couple + entry * COLS + x * BY
            row = couple_at(x) + entry * BY
            main_ref[row : row + BY, :] = raw_ref[start : start + BY, :]

    def pack(group, load):
        low = jnp.zeros((RHS, LANES), jnp.float32)
        high = jnp.zeros((RHS, LANES), jnp.float32)
        for col in range(COLS):
            turned = pltpu.roll(load(col), (8 * col + 4) % LANES, 1)
            here = lane // 4
            high = jnp.where(here == 2 * col, turned, high)
            low = jnp.where(here == 2 * col + 1, turned, low)
        low_ref[group * 8 : group * 8 + 8, :] = low
        high_ref[group * 8 : group * 8 + 8, :] = high

    for comp in range(COMP):

        def load_field(col):
            place = comp * COLS + col
            value = raw_ref[pl.ds(place, RHS, stride=COMP * COLS), :]
            row = FIELD_AT + place * RHS
            main_ref[row : row + RHS, :] = value
            return value

        pack(comp, load_field)
    for half in range(2):
        pack(
            COMP + half,
            lambda col: raw_ref[pl.ds(raw_couple + half * 8 * COLS + col, 8, stride=COLS), :],
        )
    pack(
        COMP + 2,
        lambda col: jnp.broadcast_to(eta[col : col + 1, :], (RHS, LANES)),
    )


def pack(residuals, shear_rate, coupling):
    raw = jnp.concatenate(
        [part.reshape(-1, LANES) for part in (residuals, coupling, shear_rate)], axis=0
    )
    return pl.pallas_call(
        pack_kernel,
        out_shape=(
            jax.ShapeDtypeStruct((BLOCK_ROWS, LANES), jnp.float32),
            jax.ShapeDtypeStruct((GHOST_ROWS, LANES), jnp.float32),
            jax.ShapeDtypeStruct((GHOST_ROWS, LANES), jnp.float32),
        ),
        in_specs=[VMEM],
        out_specs=(VMEM,) * 3,
        compiler_params=pltpu.CompilerParams(vmem_limit_bytes=4 * 2**20),
    )(raw)


def corner_kernel(left_ref, right_ref, down_ref, up_ref):
    lane = lane_index()
    for out_ref, top in ((down_ref, False), (up_ref, True)):
        for place, (side, a, b) in enumerate(CORNER):
            src = right_ref if side else left_ref
            base = 0 if side else -LAYER
            x = a - 1 if side else BX - a
            y = BY - b if top else b - 1
            col = x * BY + y
            for comp in range(COMP):
                start = base + FIELD_AT + (comp * COLS + col) * RHS
                row = (place * COMP + comp) * RHS
                out_ref[row : row + RHS, :] = src[start : start + RHS, :]
            if place < NEAR_COUNT:
                for half in range(2):
                    row = C_COUPLE_AT + place * 16 + half * 8
                    start = base + couple_at(x) + half * 8 * BY + y
                    out_ref[row : row + 8, :] = src[pl.ds(start, 8, stride=BY), :]
            start = base + ETA_AT + col
            out_ref[C_ETA_AT + place : C_ETA_AT + place + 1, :] = src[start : start + 1, :]
        out_ref[C_ETA_AT + len(CORNER) : C_GHOST_AT, :] = jnp.zeros(
            (16 - len(CORNER), LANES), jnp.float32
        )
        for row in range(0, GHOST_ROWS, 8):
            right = right_ref[GHOST_AT + row : GHOST_AT + row + 8, :]
            left = left_ref[GHOST_AT - LAYER + row : GHOST_AT - LAYER + row + 8, :]
            out_ref[C_GHOST_AT + row : C_GHOST_AT + row + 8, :] = jnp.where(
                lane < LANES // 2, right, left
            )


def corners(left, right):
    return pl.pallas_call(
        corner_kernel,
        out_shape=(jax.ShapeDtypeStruct((CORNER_ROWS, LANES), jnp.float32),) * 2,
        in_specs=[VMEM] * 2,
        out_specs=(VMEM,) * 2,
        compiler_params=pltpu.CompilerParams(vmem_limit_bytes=4 * 2**20),
    )(left, right)


def distance(place):
    return max(POWERS - place, 0, place - (POWERS + BX - 1))


def corner(x, y):
    return distance(x) > 0 and distance(y) > 0


def rows_of(reach):
    for x in range(POWERS - reach, POWERS + BX + reach):
        rest = reach - distance(x)
        yield x, range(POWERS - rest, POWERS + BY + rest)


PLACES = [(x, y) for x, ys in rows_of(POWERS) for y in ys]
SLOT = {place: i for i, place in enumerate(sorted(PLACES, key=lambda place: corner(*place)))}
EARLY = sum(not corner(*place) for place in PLACES)


def ready(x, y, power):
    if power == 0:
        return not corner(x, y)
    around = ((x, y), (x - 1, y), (x + 1, y), (x, y - 1), (x, y + 1))
    return all(ready(i, j, power - 1) for i, j in around)


def state_shapes(count):
    field = (count * COMP, RHS, LANES)
    return (
        [field] * 4 + [(count, 24, LANES)] * 2 + [(count * 6, RHS, LANES)] * 2
        + [(count, RHS, LANES)] * 2
    )


def powers_part(early, blocks, first_state, mine, basis_ref):
    lane = lane_index()
    first, last = lane == 0, lane == LANES - 1
    MAIN, GHOST, COEF, FACE, SCALE = 0, 2, 4, 6, 8

    def held(kind, x, y, power):
        return first_state[kind] if early or ready(x, y, power) else mine[kind]

    def place_column(src, x, y, field_at, entry_at, stride, eta_at, ghost_at, col):
        at = SLOT[x, y]
        for comp in range(COMP):
            mine[MAIN][at * COMP + comp] = src[field_at[comp] : field_at[comp] + RHS, :]
        mine[COEF][at, 16:24, :] = jnp.broadcast_to(src[eta_at : eta_at + 1, :], (8, LANES))
        if distance(x) + distance(y) >= POWERS:
            return
        for half in range(2):
            start = entry_at + half * 8 * stride
            mine[COEF][at, half * 8 : half * 8 + 8, :] = (
                src[pl.ds(start, 8, stride=stride), :] if stride > 1 else src[start : start + 8, :]
            )
        shift = (-8 * col - 4) % LANES
        for comp in range(COMP):
            row = ghost_at + comp * RHS
            mine[GHOST][at * COMP + comp] = pltpu.roll(src[row : row + RHS, :], shift, 1)
        for part in range(3):
            row = ghost_at + COMP * RHS + part * 8
            mine[COEF + 1][at, part * 8 : part * 8 + 8, :] = pltpu.roll(
                src[row : row + 8, :], shift, 1
            )

    if early:
        own_ref, left_ref, right_ref, front_ref, back_ref = blocks
        for src, base, off_x, off_y in (
            (own_ref, 0, 0, 0), (left_ref, -LAYER, -1, 0), (right_ref, 0, 1, 0),
            (front_ref, 0, 0, -1), (back_ref, 0, 0, 1),
        ):
            for x in range(BX):
                for y in range(BY):
                    col = x * BY + y
                    place_column(
                        src, POWERS + off_x * BX + x, POWERS + off_y * BY + y,
                        [base + FIELD_AT + (comp * COLS + col) * RHS for comp in range(COMP)],
                        base + couple_at(x) + y, BY, base + ETA_AT + col, base + GHOST_AT, col,
                    )
    else:
        low_ref, high_ref = blocks
        for src, top in ((low_ref, True), (high_ref, False)):
            for place, (side, a, b) in enumerate(CORNER):
                x = POWERS + BX - 1 + a if side else POWERS - a
                y = POWERS - b if top else POWERS + BY - 1 + b
                col = (a - 1 if side else BX - a) * BY + (BY - b if top else b - 1)
                place_column(
                    src, x, y, [(place * COMP + comp) * RHS for comp in range(COMP)],
                    C_COUPLE_AT + place * 16, 1, C_ETA_AT + place, C_GHOST_AT, col,
                )

    def shifted(value, other):
        up, down = pltpu.roll(value, LANES - 1, 1), pltpu.roll(value, 1, 1)
        other_up, other_down = pltpu.roll(other, LANES - 1, 1), pltpu.roll(other, 1, 1)
        return (
            jnp.where(last, other_up, up), jnp.where(first, other_down, down),
            jnp.where(last, up, other_up), jnp.where(first, down, other_down),
        )

    def eta_at(kind, x, y):
        return held(kind, x, y, 0)[SLOT[x, y], 16:24, :]

    def faces(outer, x, y, eta, up, down):
        kind, at = COEF + outer, SLOT[x, y]
        around = [
            eta_at(kind, x - 1, y), eta_at(kind, x + 1, y),
            eta_at(kind, x, y - 1), eta_at(kind, x, y + 1), down, up,
        ]
        kappas = [eta + beside for beside in around]
        for index, kappa in enumerate(kappas):
            mine[FACE + outer][at * 6 + index] = kappa
        total = (kappas[0] + kappas[1]) + (kappas[2] + kappas[3]) + (kappas[4] + kappas[5])
        diagonal = held(kind, x, y, 0)[at, pl.ds(0, COMP, stride=COMP + 1), :]
        mine[SCALE + outer][at, 0:COMP, :] = jnp.where(
            eta[0:COMP, :] < 0.0, 1.0 / (diagonal - total[0:COMP, :]), 0.0
        )

    for x, ys in rows_of(POWERS - 1):
        for y in ys:
            if ready(x, y, 1) != early:
                continue
            eta, eta_ghost = eta_at(COEF, x, y), eta_at(COEF + 1, x, y)
            up, down, ghost_up, ghost_down = shifted(eta, eta_ghost)
            faces(0, x, y, eta, up, down)
            if distance(x) + distance(y) < POWERS - 1:
                faces(1, x, y, eta_ghost, ghost_up, ghost_down)

    def spread(ref, at, row):
        return jnp.broadcast_to(ref[at, row : row + 1, :], (RHS, LANES))

    def apply(outer, power, x, y, before, centre, after, up, down):
        at = SLOT[x, y]
        table = held(COEF + outer, x, y, 0)
        faces_of, inverse = held(FACE + outer, x, y, 1), held(SCALE + outer, x, y, 1)
        kappa = [faces_of[at * 6 + index] for index in range(6)]
        results = []
        for comp in range(COMP):
            beside = [
                load(outer, power, x - 1, y, comp), load(outer, power, x + 1, y, comp),
                before[comp], after[comp], down[comp], up[comp],
            ]
            terms = [k * v for k, v in zip(kappa, beside)]
            terms += [
                spread(table, at, comp * COMP + d) * centre[d] for d in range(COMP) if d != comp
            ]
            while len(terms) > 1:
                terms = [
                    terms[i] + terms[i + 1] if i + 1 < len(terms) else terms[i]
                    for i in range(0, len(terms), 2)
                ]
            results.append(terms[0] * spread(inverse, at, comp))
        return results

    def load(outer, power, x, y, comp):
        kind = (GHOST if outer else MAIN) + power % 2
        return held(kind, x, y, power)[SLOT[x, y] * COMP + comp]

    for power in range(1, POWERS + 1):
        limit = POWERS - power
        for x, ys in rows_of(limit):
            rows = {}

            def at_row(outer, y, x=x, rows=rows, power=power):
                if (outer, y) not in rows:
                    rows[outer, y] = [load(outer, power - 1, x, y, comp) for comp in range(COMP)]
                return rows[outer, y]

            for y in ys:
                if ready(x, y, power) != early:
                    continue
                at = SLOT[x, y]
                reach = distance(x) + distance(y)
                centre, outer = at_row(0, y), at_row(1, y)
                moves = [shifted(c, o) for c, o in zip(centre, outer)]
                results = apply(
                    0, power - 1, x, y, at_row(0, y - 1), centre, at_row(0, y + 1),
                    [m[0] for m in moves], [m[1] for m in moves],
                )
                for comp in range(COMP):
                    if limit:
                        mine[MAIN + power % 2][at * COMP + comp] = results[comp]
                if reach == 0:
                    for comp in range(COMP):
                        tile = comp * COLS + (x - POWERS) * BY + (y - POWERS)
                        if power == 1:
                            basis_ref[tile, 0:RHS, :] = centre[comp]
                        basis_ref[tile, power * RHS : power * RHS + RHS, :] = results[comp]
                if reach < limit:
                    outside = apply(
                        1, power - 1, x, y, at_row(1, y - 1), outer, at_row(1, y + 1),
                        [m[2] for m in moves], [m[3] for m in moves],
                    )
                    for comp in range(COMP):
                        mine[GHOST + power % 2][at * COMP + comp] = outside[comp]


def early_kernel(*refs):
    powers_part(True, refs[:5], refs[5:15], refs[5:15], refs[15])


def late_kernel(*refs):
    blocks, first_state, early_basis = refs[:2], refs[2:12], refs[12]
    basis_ref, gram_ref, mine, square = refs[13], refs[14], refs[15:25], refs[25]
    for x in range(BX):
        for y in range(BY):
            for power in range(1, POWERS + 1):
                if ready(POWERS + x, POWERS + y, power):
                    start = 0 if power == 1 else power * RHS
                    stop = power * RHS + RHS
                    for comp in range(COMP):
                        tile = comp * COLS + x * BY + y
                        basis_ref[tile, start:stop, :] = early_basis[tile, start:stop, :]
    powers_part(False, blocks, first_state, mine, basis_ref)
    lane = lane_index()
    order = (POWERS + 1) * RHS
    total = jnp.zeros((order, order), jnp.float32)
    for tile in range(0, COMP * COLS, 2):
        both = jnp.concatenate([basis_ref[tile], basis_ref[tile + 1]], axis=1)
        total = total + lax.dot_general(
            both, both, (((1,), (1,)), ((), ())),
            precision=HIGHEST, preferred_element_type=jnp.float32,
        )
    square[...] = jnp.zeros_like(square)
    square[:, 0:order] = total
    packed = jnp.zeros((RHS, LANES), jnp.float32)
    start = 0
    for block in range(POWERS + 1):
        width = order - block * RHS
        value = pltpu.roll(
            square[block * RHS : block * RHS + RHS, :], (start - block * RHS) % LANES, 1
        )
        packed = jnp.where((lane >= start) & (lane < start + width), value, packed)
        start += width
    gram_ref[...] = packed


def early_powers(*blocks):
    basis = (COMP * COLS, (POWERS + 1) * RHS, LANES)
    return pl.pallas_call(
        early_kernel,
        out_shape=[
            jax.ShapeDtypeStruct(shape, jnp.float32) for shape in state_shapes(EARLY) + [basis]
        ],
        in_specs=[VMEM] * 5,
        out_specs=[VMEM] * 11,
        compiler_params=pltpu.CompilerParams(vmem_limit_bytes=20 * 2**20),
        cost_estimate=pl.CostEstimate(flops=5_000_000, bytes_accessed=8_000_000, transcendentals=0),
    )(*blocks)


def late_powers(low, high, state):
    basis = (COMP * COLS, (POWERS + 1) * RHS, LANES)
    return pl.pallas_call(
        late_kernel,
        out_shape=(
            jax.ShapeDtypeStruct(basis, jnp.float32),
            jax.ShapeDtypeStruct((RHS, LANES), jnp.float32),
        ),
        in_specs=[VMEM] * 13,
        out_specs=(VMEM,) * 2,
        scratch_shapes=[pltpu.VMEM(shape, jnp.float32) for shape in state_shapes(len(PLACES))]
        + [pltpu.VMEM(((POWERS + 1) * RHS, LANES), jnp.float32)],
        compiler_params=pltpu.CompilerParams(vmem_limit_bytes=36 * 2**20),
    )(low, high, *state)


def finish_kernel(gram_ref, basis_ref, out_ref, factor_ref, square, upper):
    lane = lane_index()
    order = (POWERS + 1) * RHS
    parts = [gram_ref[i] for i in range(gram_ref.shape[0])]
    while len(parts) > 1:
        parts = [
            parts[i] + parts[i + 1] if i + 1 < len(parts) else parts[i]
            for i in range(0, len(parts), 2)
        ]
    packed = parts[0]
    square[...] = jnp.zeros_like(square)
    start = 0
    for block in range(POWERS + 1):
        width = order - block * RHS
        value = pltpu.roll(packed, (block * RHS - start) % LANES, 1)
        keep = (lane >= block * RHS) & (lane < order)
        square[block * RHS : block * RHS + RHS, :] = jnp.where(keep, value, 0.0)
        start += width
    half = square[...]
    other = half.T
    gram = []
    for block in range(POWERS + 1):
        rows = slice(block * RHS, block * RHS + RHS)
        gram.append(jnp.where(lane < block * RHS, other[rows, :], half[rows, :]))
    summed = [tile + pltpu.roll(tile, LANES - RHS, 1) for tile in gram]
    normal = [summed[i] + summed[i + 1] for i in range(POWERS)] + [summed[0]]

    upper[...] = jnp.zeros_like(upper)
    number = lane[0:1, :]

    def wide(value, column):
        return jnp.broadcast_to(value[:, column : column + 1], value.shape)

    def pair(matrix, step):
        tile, row = step // RHS, step % RHS
        p, q = matrix[tile][row : row + 1, :], matrix[tile][row + 1 : row + 2, :]
        one, cross, far = wide(p, step), wide(p, step + 1), wide(q, step + 1)
        inverse = 1.0 / one
        ratio = cross * inverse
        other = far - cross * ratio
        rest = q - ratio * p
        inverse_other = 1.0 / other
        second = rest * inverse_other
        first = p * inverse - ratio * second
        return p, rest, one, other, first, second, inverse, inverse_other, ratio

    for step in range(0, order, 2):
        tile = step // RHS
        low = tile if step % RHS < RHS - 2 else tile + 1
        p, rest, one, other, first, second, _, _, _ = pair(gram, step)
        top = jnp.where(number >= step, p * lax.rsqrt(one), 0.0)
        bottom = jnp.where(number > step, rest * lax.rsqrt(other), 0.0)
        upper[step : step + 1, :] = top[0:1, :]
        upper[step + 1 : step + 2, :] = bottom[0:1, :]
        for i in range(low, POWERS + 1):
            gram[i] = gram[i] - wide(gram[i], step) * first - wide(gram[i], step + 1) * second
        if step < POWERS * RHS:
            _, _, _, _, first, second, inverse, inverse_other, ratio = pair(normal, step)
            mixed = ratio * inverse_other
            at_one, at_other = number == step, number == step + 1
            cleared = (lane == step) | (lane == step + 1)
            first = jnp.where(
                at_one, -(inverse + ratio * mixed), jnp.where(at_other, mixed, first)
            )
            second = jnp.where(at_one, mixed, jnp.where(at_other, -inverse_other, second))
            for i in range(low, POWERS + 1):
                normal[i] = (
                    jnp.where(cleared, 0.0, normal[i])
                    - wide(normal[i], step) * first
                    - wide(normal[i], step + 1) * second
                )
    factor_ref[...] = upper[0:order, 0:order]
    answer = normal[POWERS]
    weights = [
        jnp.broadcast_to(answer[:, i : i + 1], (RHS, LANES)) for i in range(POWERS * RHS)
    ]

    def combine(tile, carry):
        sums = [None] * 4
        for i in range(POWERS * RHS):
            term = weights[i] * jnp.broadcast_to(basis_ref[tile, i : i + 1, :], (RHS, LANES))
            sums[i % 4] = term if sums[i % 4] is None else sums[i % 4] + term
        out_ref[pl.ds(tile, RHS, stride=COMP * COLS), :] = (sums[0] + sums[1]) + (
            sums[2] + sums[3]
        )
        return carry

    lax.fori_loop(0, COMP * COLS, combine, 0, unroll=4)


def finish(gram, basis):
    order = (POWERS + 1) * RHS
    return pl.pallas_call(
        finish_kernel,
        out_shape=(
            jax.ShapeDtypeStruct((RHS * COMP * COLS, LANES), jnp.float32),
            jax.ShapeDtypeStruct((order, order), jnp.float32),
        ),
        in_specs=[VMEM] * 2,
        out_specs=(VMEM,) * 2,
        scratch_shapes=[
            pltpu.VMEM((LANES, LANES), jnp.float32),
            pltpu.VMEM((order, LANES), jnp.float32),
        ],
        compiler_params=pltpu.CompilerParams(vmem_limit_bytes=6 * 2**20),
    )(gram, basis)


def swapped(first, second, axis):
    count = lax.axis_size(axis)
    odd = lax.axis_index(axis) % 2 == 1
    inner = [(i, i ^ 1) for i in range(count)]
    outer = [(i, ((i + 1) ^ 1) - 1) for i in range(1, count - 1)]
    one = lax.ppermute(first(odd), axis, inner)
    two = lax.ppermute(second(odd), axis, outer)
    return jnp.where(odd, one, two), jnp.where(odd, two, one)


def vertical(low, high):
    count, place = lax.axis_size("gz"), lax.axis_index("gz")
    index = jnp.arange(count)[:, None, None]
    sent = jnp.where(index == place + 1, high[None], jnp.where(index == place - 1, low[None], 0.0))
    return lax.all_to_all(sent, "gz", 0, 0)


def gathered(tile, axes):
    count = lax.axis_size(axes)
    return lax.all_to_all(jnp.broadcast_to(tile[None], (count,) + tile.shape), axes, 0, 0)


def local(residuals, shear_rate, coupling):
    block, low, high = pack(residuals, shear_rate, coupling)
    ghosts = jnp.sum(vertical(low, high), axis=0)
    own = lax.dynamic_update_slice(block, ghosts, (GHOST_AT, 0))
    left, right = swapped(
        lambda odd: jnp.where(odd, own[:SIDE_ROWS], own[LAYER:]),
        lambda odd: jnp.where(odd, own[LAYER:], own[:SIDE_ROWS]),
        "gx",
    )
    front, back = swapped(lambda odd: own, lambda odd: own, "gy")
    down, up = corners(left, right)
    low_corner, high_corner = swapped(
        lambda odd: jnp.where(odd, down, up), lambda odd: jnp.where(odd, up, down), "gy"
    )
    state = early_powers(own, left, right, front, back)
    basis, gram = late_powers(low_corner, high_corner, state)
    gram = jnp.sum(gathered(gram, ("gy", "gz")), axis=0)
    correction, factor = finish(gathered(gram, "gx"), basis)
    return correction.reshape(residuals.shape), factor


def solution(mesh):
    in_specs = (
        P(None, None, "gx", "gy", "gz"),
        P("gx", "gy", "gz"),
        P(None, None, "gx", "gy", "gz"),
    )
    out_specs = (P(None, None, "gx", "gy", "gz"), P())
    return jax.shard_map(local, mesh=mesh, in_specs=in_specs, out_specs=out_specs, check_vma=False)
```

```python
import jax
import jax.numpy as jnp
from jax import lax
from jax.experimental import pallas as pl
from jax.experimental.pallas import tpu as pltpu
from jax.sharding import PartitionSpec as P

POWERS = 4
RHS = 8
COMP = 4
BX = 4
BY = 4
LANES = 128
COLS = BX * BY
GRID = BX + 2 * POWERS
HIGHEST = lax.Precision.HIGHEST
VMEM = pl.BlockSpec(memory_space=pltpu.VMEM)

FIELD_ROWS = COMP * COLS * RHS
LAYER = COMP * COMP * BY
GHOST_ROWS = COMP * RHS + 24
GHOST_AT = LAYER
FIELD_AT = GHOST_AT + GHOST_ROWS
ETA_AT = FIELD_AT + FIELD_ROWS
TAIL_AT = ETA_AT + COLS
BLOCK_ROWS = TAIL_AT + (BX - 1) * LAYER
SIDE_ROWS = BLOCK_ROWS - LAYER

NEAR = [(1, 1), (1, 2), (2, 1)]
FAR = [(1, 3), (2, 2), (3, 1)]
CORNER = [(side, a, b) for a, b in NEAR + FAR for side in (0, 1)]
NEAR_COUNT = 2 * len(NEAR)
C_COUPLE_AT = len(CORNER) * COMP * RHS
C_ETA_AT = C_COUPLE_AT + NEAR_COUNT * 16
C_GHOST_AT = C_ETA_AT + 16
CORNER_ROWS = C_GHOST_AT + GHOST_ROWS


def couple_at(x):
    return TAIL_AT + (x - 1) * LAYER if x else 0


def lane_index():
    return lax.broadcasted_iota(jnp.int32, (RHS, LANES), 1)


def pack_kernel(raw_ref, main_ref, low_ref, high_ref):
    lane = lane_index()
    raw_couple = FIELD_ROWS
    raw_shear = FIELD_ROWS + BX * LAYER
    shear = raw_ref[raw_shear : raw_shear + COLS, :]
    eta = -0.5 * (0.2 + (1.0 - jnp.exp(-100.0 * shear)) / shear)
    main_ref[ETA_AT:TAIL_AT, :] = eta
    main_ref[GHOST_AT:FIELD_AT, :] = jnp.zeros((GHOST_ROWS, LANES), jnp.float32)
    for entry in range(COMP * COMP):
        for x in range(BX):
            start = raw_couple + entry * COLS + x * BY
            row = couple_at(x) + entry * BY
            main_ref[row : row + BY, :] = raw_ref[start : start + BY, :]

    def pack(group, load):
        low = jnp.zeros((RHS, LANES), jnp.float32)
        high = jnp.zeros((RHS, LANES), jnp.float32)
        for col in range(COLS):
            turned = pltpu.roll(load(col), (8 * col + 4) % LANES, 1)
            here = lane // 4
            high = jnp.where(here == 2 * col, turned, high)
            low = jnp.where(here == 2 * col + 1, turned, low)
        low_ref[group * 8 : group * 8 + 8, :] = low
        high_ref[group * 8 : group * 8 + 8, :] = high

    for comp in range(COMP):

        def load_field(col):
            place = comp * COLS + col
            value = raw_ref[pl.ds(place, RHS, stride=COMP * COLS), :]
            row = FIELD_AT + place * RHS
            main_ref[row : row + RHS, :] = value
            return value

        pack(comp, load_field)
    for half in range(2):
        pack(
            COMP + half,
            lambda col: raw_ref[pl.ds(raw_couple + half * 8 * COLS + col, 8, stride=COLS), :],
        )
    pack(
        COMP + 2,
        lambda col: jnp.broadcast_to(eta[col : col + 1, :], (RHS, LANES)),
    )


def pack(residuals, shear_rate, coupling):
    raw = jnp.concatenate(
        [part.reshape(-1, LANES) for part in (residuals, coupling, shear_rate)], axis=0
    )
    return pl.pallas_call(
        pack_kernel,
        out_shape=(
            jax.ShapeDtypeStruct((BLOCK_ROWS, LANES), jnp.float32),
            jax.ShapeDtypeStruct((GHOST_ROWS, LANES), jnp.float32),
            jax.ShapeDtypeStruct((GHOST_ROWS, LANES), jnp.float32),
        ),
        in_specs=[VMEM],
        out_specs=(VMEM,) * 3,
        compiler_params=pltpu.CompilerParams(vmem_limit_bytes=4 * 2**20),
    )(raw)


def corner_kernel(left_ref, right_ref, down_ref, up_ref):
    lane = lane_index()
    for out_ref, top in ((down_ref, False), (up_ref, True)):
        for place, (side, a, b) in enumerate(CORNER):
            src = right_ref if side else left_ref
            base = 0 if side else -LAYER
            x = a - 1 if side else BX - a
            y = BY - b if top else b - 1
            col = x * BY + y
            for comp in range(COMP):
                start = base + FIELD_AT + (comp * COLS + col) * RHS
                row = (place * COMP + comp) * RHS
                out_ref[row : row + RHS, :] = src[start : start + RHS, :]
            if place < NEAR_COUNT:
                for half in range(2):
                    row = C_COUPLE_AT + place * 16 + half * 8
                    start = base + couple_at(x) + half * 8 * BY + y
                    out_ref[row : row + 8, :] = src[pl.ds(start, 8, stride=BY), :]
            start = base + ETA_AT + col
            out_ref[C_ETA_AT + place : C_ETA_AT + place + 1, :] = src[start : start + 1, :]
        out_ref[C_ETA_AT + len(CORNER) : C_GHOST_AT, :] = jnp.zeros(
            (16 - len(CORNER), LANES), jnp.float32
        )
        for row in range(0, GHOST_ROWS, 8):
            right = right_ref[GHOST_AT + row : GHOST_AT + row + 8, :]
            left = left_ref[GHOST_AT - LAYER + row : GHOST_AT - LAYER + row + 8, :]
            out_ref[C_GHOST_AT + row : C_GHOST_AT + row + 8, :] = jnp.where(
                lane < LANES // 2, right, left
            )


def corners(left, right):
    return pl.pallas_call(
        corner_kernel,
        out_shape=(jax.ShapeDtypeStruct((CORNER_ROWS, LANES), jnp.float32),) * 2,
        in_specs=[VMEM] * 2,
        out_specs=(VMEM,) * 2,
        compiler_params=pltpu.CompilerParams(vmem_limit_bytes=4 * 2**20),
    )(left, right)


def distance(place):
    return max(POWERS - place, 0, place - (POWERS + BX - 1))


def corner(x, y):
    return distance(x) > 0 and distance(y) > 0


def rows_of(reach):
    for x in range(POWERS - reach, POWERS + BX + reach):
        rest = reach - distance(x)
        yield x, range(POWERS - rest, POWERS + BY + rest)


PLACES = [(x, y) for x, ys in rows_of(POWERS) for y in ys]
SLOT = {place: i for i, place in enumerate(sorted(PLACES, key=lambda place: corner(*place)))}
EARLY = sum(not corner(*place) for place in PLACES)


def ready(x, y, power):
    if power == 0:
        return not corner(x, y)
    around = ((x, y), (x - 1, y), (x + 1, y), (x, y - 1), (x, y + 1))
    return all(ready(i, j, power - 1) for i, j in around)


def state_shapes(count):
    field = (count * COMP, RHS, LANES)
    return (
        [field] * 4 + [(count, 24, LANES)] * 2 + [(count * 6, RHS, LANES)] * 2
        + [(count, RHS, LANES)] * 2
    )


def powers_part(early, blocks, first_state, mine, basis_ref):
    lane = lane_index()
    first, last = lane == 0, lane == LANES - 1
    MAIN, GHOST, COEF, FACE, SCALE = 0, 2, 4, 6, 8

    def held(kind, x, y, power):
        return first_state[kind] if early or ready(x, y, power) else mine[kind]

    def place_column(src, x, y, field_at, entry_at, stride, eta_at, ghost_at, col):
        at = SLOT[x, y]
        for comp in range(COMP):
            mine[MAIN][at * COMP + comp] = src[field_at[comp] : field_at[comp] + RHS, :]
        mine[COEF][at, 16:24, :] = jnp.broadcast_to(src[eta_at : eta_at + 1, :], (8, LANES))
        if distance(x) + distance(y) >= POWERS:
            return
        for half in range(2):
            start = entry_at + half * 8 * stride
            mine[COEF][at, half * 8 : half * 8 + 8, :] = (
                src[pl.ds(start, 8, stride=stride), :] if stride > 1 else src[start : start + 8, :]
            )
        shift = (-8 * col - 4) % LANES
        for comp in range(COMP):
            row = ghost_at + comp * RHS
            mine[GHOST][at * COMP + comp] = pltpu.roll(src[row : row + RHS, :], shift, 1)
        for part in range(3):
            row = ghost_at + COMP * RHS + part * 8
            mine[COEF + 1][at, part * 8 : part * 8 + 8, :] = pltpu.roll(
                src[row : row + 8, :], shift, 1
            )

    if early:
        own_ref, left_ref, right_ref, front_ref, back_ref = blocks
        for src, base, off_x, off_y in (
            (own_ref, 0, 0, 0), (left_ref, -LAYER, -1, 0), (right_ref, 0, 1, 0),
            (front_ref, 0, 0, -1), (back_ref, 0, 0, 1),
        ):
            for x in range(BX):
                for y in range(BY):
                    col = x * BY + y
                    place_column(
                        src, POWERS + off_x * BX + x, POWERS + off_y * BY + y,
                        [base + FIELD_AT + (comp * COLS + col) * RHS for comp in range(COMP)],
                        base + couple_at(x) + y, BY, base + ETA_AT + col, base + GHOST_AT, col,
                    )
    else:
        low_ref, high_ref = blocks
        for src, top in ((low_ref, True), (high_ref, False)):
            for place, (side, a, b) in enumerate(CORNER):
                x = POWERS + BX - 1 + a if side else POWERS - a
                y = POWERS - b if top else POWERS + BY - 1 + b
                col = (a - 1 if side else BX - a) * BY + (BY - b if top else b - 1)
                place_column(
                    src, x, y, [(place * COMP + comp) * RHS for comp in range(COMP)],
                    C_COUPLE_AT + place * 16, 1, C_ETA_AT + place, C_GHOST_AT, col,
                )

    def shifted(value, other):
        up, down = pltpu.roll(value, LANES - 1, 1), pltpu.roll(value, 1, 1)
        other_up, other_down = pltpu.roll(other, LANES - 1, 1), pltpu.roll(other, 1, 1)
        return (
            jnp.where(last, other_up, up), jnp.where(first, other_down, down),
            jnp.where(last, up, other_up), jnp.where(first, down, other_down),
        )

    def eta_at(kind, x, y):
        return held(kind, x, y, 0)[SLOT[x, y], 16:24, :]

    def faces(outer, x, y, eta, up, down):
        kind, at = COEF + outer, SLOT[x, y]
        around = [
            eta_at(kind, x - 1, y), eta_at(kind, x + 1, y),
            eta_at(kind, x, y - 1), eta_at(kind, x, y + 1), down, up,
        ]
        kappas = [eta + beside for beside in around]
        for index, kappa in enumerate(kappas):
            mine[FACE + outer][at * 6 + index] = kappa
        total = (kappas[0] + kappas[1]) + (kappas[2] + kappas[3]) + (kappas[4] + kappas[5])
        diagonal = held(kind, x, y, 0)[at, pl.ds(0, COMP, stride=COMP + 1), :]
        mine[SCALE + outer][at, 0:COMP, :] = jnp.where(
            eta[0:COMP, :] < 0.0, 1.0 / (diagonal - total[0:COMP, :]), 0.0
        )

    for x, ys in rows_of(POWERS - 1):
        for y in ys:
            if ready(x, y, 1) != early:
                continue
            eta, eta_ghost = eta_at(COEF, x, y), eta_at(COEF + 1, x, y)
            up, down, ghost_up, ghost_down = shifted(eta, eta_ghost)
            faces(0, x, y, eta, up, down)
            if distance(x) + distance(y) < POWERS - 1:
                faces(1, x, y, eta_ghost, ghost_up, ghost_down)

    def spread(ref, at, row):
        return jnp.broadcast_to(ref[at, row : row + 1, :], (RHS, LANES))

    def apply(outer, power, x, y, before, centre, after, up, down):
        at = SLOT[x, y]
        table = held(COEF + outer, x, y, 0)
        faces_of, inverse = held(FACE + outer, x, y, 1), held(SCALE + outer, x, y, 1)
        kappa = [faces_of[at * 6 + index] for index in range(6)]
        results = []
        for comp in range(COMP):
            beside = [
                load(outer, power, x - 1, y, comp), load(outer, power, x + 1, y, comp),
                before[comp], after[comp], down[comp], up[comp],
            ]
            terms = [k * v for k, v in zip(kappa, beside)]
            terms += [
                spread(table, at, comp * COMP + d) * centre[d] for d in range(COMP) if d != comp
            ]
            while len(terms) > 1:
                terms = [
                    terms[i] + terms[i + 1] if i + 1 < len(terms) else terms[i]
                    for i in range(0, len(terms), 2)
                ]
            results.append(terms[0] * spread(inverse, at, comp))
        return results

    def load(outer, power, x, y, comp):
        kind = (GHOST if outer else MAIN) + power % 2
        return held(kind, x, y, power)[SLOT[x, y] * COMP + comp]

    for power in range(1, POWERS + 1):
        limit = POWERS - power
        for x, ys in rows_of(limit):
            rows = {}

            def at_row(outer, y, x=x, rows=rows, power=power):
                if (outer, y) not in rows:
                    rows[outer, y] = [load(outer, power - 1, x, y, comp) for comp in range(COMP)]
                return rows[outer, y]

            for y in ys:
                if ready(x, y, power) != early:
                    continue
                at = SLOT[x, y]
                reach = distance(x) + distance(y)
                centre, outer = at_row(0, y), at_row(1, y)
                moves = [shifted(c, o) for c, o in zip(centre, outer)]
                results = apply(
                    0, power - 1, x, y, at_row(0, y - 1), centre, at_row(0, y + 1),
                    [m[0] for m in moves], [m[1] for m in moves],
                )
                for comp in range(COMP):
                    if limit:
                        mine[MAIN + power % 2][at * COMP + comp] = results[comp]
                if reach == 0:
                    for comp in range(COMP):
                        tile = comp * COLS + (x - POWERS) * BY + (y - POWERS)
                        if power == 1:
                            basis_ref[tile, 0:RHS, :] = centre[comp]
                        basis_ref[tile, power * RHS : power * RHS + RHS, :] = results[comp]
                if reach < limit:
                    outside = apply(
                        1, power - 1, x, y, at_row(1, y - 1), outer, at_row(1, y + 1),
                        [m[2] for m in moves], [m[3] for m in moves],
                    )
                    for comp in range(COMP):
                        mine[GHOST + power % 2][at * COMP + comp] = outside[comp]


def early_kernel(*refs):
    powers_part(True, refs[:5], refs[5:15], refs[5:15], refs[15])


def late_kernel(*refs):
    blocks, first_state, early_basis = refs[:2], refs[2:12], refs[12]
    basis_ref, gram_ref, mine, square = refs[13], refs[14], refs[15:25], refs[25]
    for x in range(BX):
        for y in range(BY):
            for power in range(1, POWERS + 1):
                if ready(POWERS + x, POWERS + y, power):
                    start = 0 if power == 1 else power * RHS
                    stop = power * RHS + RHS
                    for comp in range(COMP):
                        tile = comp * COLS + x * BY + y
                        basis_ref[tile, start:stop, :] = early_basis[tile, start:stop, :]
    powers_part(False, blocks, first_state, mine, basis_ref)
    lane = lane_index()
    order = (POWERS + 1) * RHS
    total = jnp.zeros((order, order), jnp.float32)
    for tile in range(0, COMP * COLS, 2):
        both = jnp.concatenate([basis_ref[tile], basis_ref[tile + 1]], axis=1)
        total = total + lax.dot_general(
            both, both, (((1,), (1,)), ((), ())),
            precision=HIGHEST, preferred_element_type=jnp.float32,
        )
    square[...] = jnp.zeros_like(square)
    square[:, 0:order] = total
    packed = jnp.zeros((RHS, LANES), jnp.float32)
    start = 0
    for block in range(POWERS + 1):
        width = order - block * RHS
        value = pltpu.roll(
            square[block * RHS : block * RHS + RHS, :], (start - block * RHS) % LANES, 1
        )
        packed = jnp.where((lane >= start) & (lane < start + width), value, packed)
        start += width
    gram_ref[...] = packed


def early_powers(*blocks):
    basis = (COMP * COLS, (POWERS + 1) * RHS, LANES)
    return pl.pallas_call(
        early_kernel,
        out_shape=[
            jax.ShapeDtypeStruct(shape, jnp.float32) for shape in state_shapes(EARLY) + [basis]
        ],
        in_specs=[VMEM] * 5,
        out_specs=[VMEM] * 11,
        compiler_params=pltpu.CompilerParams(vmem_limit_bytes=20 * 2**20),
        cost_estimate=pl.CostEstimate(flops=5_000_000, bytes_accessed=8_000_000, transcendentals=0),
    )(*blocks)


def late_powers(low, high, state):
    basis = (COMP * COLS, (POWERS + 1) * RHS, LANES)
    return pl.pallas_call(
        late_kernel,
        out_shape=(
            jax.ShapeDtypeStruct(basis, jnp.float32),
            jax.ShapeDtypeStruct((RHS, LANES), jnp.float32),
        ),
        in_specs=[VMEM] * 13,
        out_specs=(VMEM,) * 2,
        scratch_shapes=[pltpu.VMEM(shape, jnp.float32) for shape in state_shapes(len(PLACES))]
        + [pltpu.VMEM(((POWERS + 1) * RHS, LANES), jnp.float32)],
        compiler_params=pltpu.CompilerParams(vmem_limit_bytes=36 * 2**20),
    )(low, high, *state)


def finish_kernel(gram_ref, basis_ref, out_ref, factor_ref, square, upper):
    lane = lane_index()
    order = (POWERS + 1) * RHS
    parts = [gram_ref[i] for i in range(gram_ref.shape[0])]
    while len(parts) > 1:
        parts = [
            parts[i] + parts[i + 1] if i + 1 < len(parts) else parts[i]
            for i in range(0, len(parts), 2)
        ]
    packed = parts[0]
    square[...] = jnp.zeros_like(square)
    start = 0
    for block in range(POWERS + 1):
        width = order - block * RHS
        value = pltpu.roll(packed, (block * RHS - start) % LANES, 1)
        keep = (lane >= block * RHS) & (lane < order)
        square[block * RHS : block * RHS + RHS, :] = jnp.where(keep, value, 0.0)
        start += width
    half = square[...]
    other = half.T
    gram = []
    for block in range(POWERS + 1):
        rows = slice(block * RHS, block * RHS + RHS)
        gram.append(jnp.where(lane < block * RHS, other[rows, :], half[rows, :]))
    summed = [tile + pltpu.roll(tile, LANES - RHS, 1) for tile in gram]
    normal = [summed[i] + summed[i + 1] for i in range(POWERS)] + [summed[0]]

    upper[...] = jnp.zeros_like(upper)
    number = lane[0:1, :]

    def wide(value, column):
        return jnp.broadcast_to(value[:, column : column + 1], value.shape)

    def pair(matrix, step):
        tile, row = step // RHS, step % RHS
        p, q = matrix[tile][row : row + 1, :], matrix[tile][row + 1 : row + 2, :]
        one, cross, far = wide(p, step), wide(p, step + 1), wide(q, step + 1)
        inverse = 1.0 / one
        ratio = cross * inverse
        other = far - cross * ratio
        rest = q - ratio * p
        inverse_other = 1.0 / other
        second = rest * inverse_other
        first = p * inverse - ratio * second
        return p, rest, one, other, first, second, inverse, inverse_other, ratio

    for step in range(0, order, 2):
        tile = step // RHS
        low = tile if step % RHS < RHS - 2 else tile + 1
        p, rest, one, other, first, second, _, _, _ = pair(gram, step)
        top = jnp.where(number >= step, p * lax.rsqrt(one), 0.0)
        bottom = jnp.where(number > step, rest * lax.rsqrt(other), 0.0)
        upper[step : step + 1, :] = top[0:1, :]
        upper[step + 1 : step + 2, :] = bottom[0:1, :]
        for i in range(low, POWERS + 1):
            gram[i] = gram[i] - wide(gram[i], step) * first - wide(gram[i], step + 1) * second
        if step < POWERS * RHS:
            _, _, _, _, first, second, inverse, inverse_other, ratio = pair(normal, step)
            mixed = ratio * inverse_other
            at_one, at_other = number == step, number == step + 1
            cleared = (lane == step) | (lane == step + 1)
            first = jnp.where(
                at_one, -(inverse + ratio * mixed), jnp.where(at_other, mixed, first)
            )
            second = jnp.where(at_one, mixed, jnp.where(at_other, -inverse_other, second))
            for i in range(low, POWERS + 1):
                normal[i] = (
                    jnp.where(cleared, 0.0, normal[i])
                    - wide(normal[i], step) * first
                    - wide(normal[i], step + 1) * second
                )
    factor_ref[...] = upper[0:order, 0:order]
    answer = normal[POWERS]
    weights = [
        jnp.broadcast_to(answer[:, i : i + 1], (RHS, LANES)) for i in range(POWERS * RHS)
    ]

    def combine(tile, carry):
        sums = [None] * 4
        for i in range(POWERS * RHS):
            term = weights[i] * jnp.broadcast_to(basis_ref[tile, i : i + 1, :], (RHS, LANES))
            sums[i % 4] = term if sums[i % 4] is None else sums[i % 4] + term
        out_ref[pl.ds(tile, RHS, stride=COMP * COLS), :] = (sums[0] + sums[1]) + (
            sums[2] + sums[3]
        )
        return carry

    lax.fori_loop(0, COMP * COLS, combine, 0, unroll=4)


def finish(gram, basis):
    order = (POWERS + 1) * RHS
    return pl.pallas_call(
        finish_kernel,
        out_shape=(
            jax.ShapeDtypeStruct((RHS * COMP * COLS, LANES), jnp.float32),
            jax.ShapeDtypeStruct((order, order), jnp.float32),
        ),
        in_specs=[VMEM] * 2,
        out_specs=(VMEM,) * 2,
        scratch_shapes=[
            pltpu.VMEM((LANES, LANES), jnp.float32),
            pltpu.VMEM((order, LANES), jnp.float32),
        ],
        compiler_params=pltpu.CompilerParams(vmem_limit_bytes=6 * 2**20),
    )(gram, basis)


def moved(block, axis, step):
    count = lax.axis_size(axis)
    pairs = [(i, i + step) for i in range(count) if 0 <= i + step < count]
    return lax.ppermute(block, axis, pairs)


def swapped(to_low, to_high, axis, even):
    count = lax.axis_size(axis)
    inner = [(i, i ^ 1) for i in range(count)]
    outer = [(i, ((i + 1) ^ 1) - 1) for i in range(1, count - 1)]
    two = lax.ppermute(jnp.where(even, to_low, to_high), axis, outer)
    one = lax.ppermute(jnp.where(even, to_high, to_low), axis, inner)
    return jnp.where(even, two, one), jnp.where(even, one, two)


def vertical(low, high):
    count, place = lax.axis_size("gz"), lax.axis_index("gz")
    index = jnp.arange(count)[:, None, None]
    sent = jnp.where(index == place + 1, high[None], jnp.where(index == place - 1, low[None], 0.0))
    even = [lax.axis_index(axis) % 2 == 0 for axis in ("gx", "gy")]
    sent, even = lax.optimization_barrier((sent, even))
    return lax.all_to_all(sent, "gz", 0, 0), even


def gathered(tile, axes):
    count = lax.axis_size(axes)
    return lax.all_to_all(jnp.broadcast_to(tile[None], (count,) + tile.shape), axes, 0, 0)


def local(residuals, shear_rate, coupling):
    block, low, high = pack(residuals, shear_rate, coupling)
    received, (even_x, even_y) = vertical(low, high)
    own = lax.dynamic_update_slice(block, jnp.sum(received, axis=0), (GHOST_AT, 0))
    left, right = swapped(own[:SIDE_ROWS], own[LAYER:], "gx", even_x)
    front, back = moved(own, "gy", 1), moved(own, "gy", -1)
    down, up = corners(left, right)
    low_corner, high_corner = swapped(down, up, "gy", even_y)
    state = early_powers(own, left, right, front, back)
    basis, gram = late_powers(low_corner, high_corner, state)
    gram = jnp.sum(gathered(gram, ("gy", "gz")), axis=0)
    correction, factor = finish(gathered(gram, "gx"), basis)
    return correction.reshape(residuals.shape), factor


def solution(mesh):
    in_specs = (
        P(None, None, "gx", "gy", "gz"),
        P("gx", "gy", "gz"),
        P(None, None, "gx", "gy", "gz"),
    )
    out_specs = (P(None, None, "gx", "gy", "gz"), P())
    return jax.shard_map(local, mesh=mesh, in_specs=in_specs, out_specs=out_specs, check_vma=False)
```

```python
import jax
import jax.numpy as jnp
from jax import lax
from jax.experimental import pallas as pl
from jax.experimental.pallas import tpu as pltpu
from jax.sharding import PartitionSpec as P

POWERS = 4
RHS = 8
COMP = 4
BX = 4
BY = 4
LANES = 128
COLS = BX * BY
GRID = BX + 2 * POWERS
HIGHEST = lax.Precision.HIGHEST
VMEM = pl.BlockSpec(memory_space=pltpu.VMEM)

FIELD_ROWS = COMP * COLS * RHS
LAYER = COMP * COMP * BY
GHOST_ROWS = COMP * RHS + 24
GHOST_AT = LAYER
FIELD_AT = GHOST_AT + GHOST_ROWS
ETA_AT = FIELD_AT + FIELD_ROWS
TAIL_AT = ETA_AT + COLS
BLOCK_ROWS = TAIL_AT + (BX - 1) * LAYER
SIDE_ROWS = BLOCK_ROWS - LAYER

NEAR = [(1, 1), (1, 2), (2, 1)]
FAR = [(1, 3), (2, 2), (3, 1)]
CORNER = [(side, a, b) for a, b in NEAR + FAR for side in (0, 1)]
NEAR_COUNT = 2 * len(NEAR)
C_COUPLE_AT = len(CORNER) * COMP * RHS
C_ETA_AT = C_COUPLE_AT + NEAR_COUNT * 16
C_GHOST_AT = C_ETA_AT + 16
CORNER_ROWS = C_GHOST_AT + GHOST_ROWS


def couple_at(x):
    return TAIL_AT + (x - 1) * LAYER if x else 0


def lane_index():
    return lax.broadcasted_iota(jnp.int32, (RHS, LANES), 1)


def pack_kernel(raw_ref, main_ref, low_ref, high_ref):
    lane = lane_index()
    raw_couple = FIELD_ROWS
    raw_shear = FIELD_ROWS + BX * LAYER
    shear = raw_ref[raw_shear : raw_shear + COLS, :]
    eta = -0.5 * (0.2 + (1.0 - jnp.exp(-100.0 * shear)) / shear)
    main_ref[ETA_AT:TAIL_AT, :] = eta
    main_ref[GHOST_AT:FIELD_AT, :] = jnp.zeros((GHOST_ROWS, LANES), jnp.float32)
    for entry in range(COMP * COMP):
        for x in range(BX):
            start = raw_couple + entry * COLS + x * BY
            row = couple_at(x) + entry * BY
            main_ref[row : row + BY, :] = raw_ref[start : start + BY, :]

    def pack(group, load):
        low = jnp.zeros((RHS, LANES), jnp.float32)
        high = jnp.zeros((RHS, LANES), jnp.float32)
        for col in range(COLS):
            turned = pltpu.roll(load(col), (8 * col + 4) % LANES, 1)
            here = lane // 4
            high = jnp.where(here == 2 * col, turned, high)
            low = jnp.where(here == 2 * col + 1, turned, low)
        low_ref[group * 8 : group * 8 + 8, :] = low
        high_ref[group * 8 : group * 8 + 8, :] = high

    for comp in range(COMP):

        def load_field(col):
            place = comp * COLS + col
            value = raw_ref[pl.ds(place, RHS, stride=COMP * COLS), :]
            row = FIELD_AT + place * RHS
            main_ref[row : row + RHS, :] = value
            return value

        pack(comp, load_field)
    for half in range(2):
        pack(
            COMP + half,
            lambda col: raw_ref[pl.ds(raw_couple + half * 8 * COLS + col, 8, stride=COLS), :],
        )
    pack(
        COMP + 2,
        lambda col: jnp.broadcast_to(eta[col : col + 1, :], (RHS, LANES)),
    )


def pack(residuals, shear_rate, coupling):
    raw = jnp.concatenate(
        [part.reshape(-1, LANES) for part in (residuals, coupling, shear_rate)], axis=0
    )
    return pl.pallas_call(
        pack_kernel,
        out_shape=(
            jax.ShapeDtypeStruct((BLOCK_ROWS, LANES), jnp.float32),
            jax.ShapeDtypeStruct((GHOST_ROWS, LANES), jnp.float32),
            jax.ShapeDtypeStruct((GHOST_ROWS, LANES), jnp.float32),
        ),
        in_specs=[VMEM],
        out_specs=(VMEM,) * 3,
        compiler_params=pltpu.CompilerParams(vmem_limit_bytes=4 * 2**20),
    )(raw)


def corner_kernel(left_ref, right_ref, down_ref, up_ref):
    lane = lane_index()
    for out_ref, top in ((down_ref, False), (up_ref, True)):
        for place, (side, a, b) in enumerate(CORNER):
            src = right_ref if side else left_ref
            base = 0 if side else -LAYER
            x = a - 1 if side else BX - a
            y = BY - b if top else b - 1
            col = x * BY + y
            for comp in range(COMP):
                start = base + FIELD_AT + (comp * COLS + col) * RHS
                row = (place * COMP + comp) * RHS
                out_ref[row : row + RHS, :] = src[start : start + RHS, :]
            if place < NEAR_COUNT:
                for half in range(2):
                    row = C_COUPLE_AT + place * 16 + half * 8
                    start = base + couple_at(x) + half * 8 * BY + y
                    out_ref[row : row + 8, :] = src[pl.ds(start, 8, stride=BY), :]
            start = base + ETA_AT + col
            out_ref[C_ETA_AT + place : C_ETA_AT + place + 1, :] = src[start : start + 1, :]
        out_ref[C_ETA_AT + len(CORNER) : C_GHOST_AT, :] = jnp.zeros(
            (16 - len(CORNER), LANES), jnp.float32
        )
        for row in range(0, GHOST_ROWS, 8):
            right = right_ref[GHOST_AT + row : GHOST_AT + row + 8, :]
            left = left_ref[GHOST_AT - LAYER + row : GHOST_AT - LAYER + row + 8, :]
            out_ref[C_GHOST_AT + row : C_GHOST_AT + row + 8, :] = jnp.where(
                lane < LANES // 2, right, left
            )


def corners(left, right):
    return pl.pallas_call(
        corner_kernel,
        out_shape=(jax.ShapeDtypeStruct((CORNER_ROWS, LANES), jnp.float32),) * 2,
        in_specs=[VMEM] * 2,
        out_specs=(VMEM,) * 2,
        compiler_params=pltpu.CompilerParams(vmem_limit_bytes=4 * 2**20),
    )(left, right)


def distance(place):
    return max(POWERS - place, 0, place - (POWERS + BX - 1))


def corner(x, y):
    return distance(x) > 0 and distance(y) > 0


def rows_of(reach):
    for x in range(POWERS - reach, POWERS + BX + reach):
        rest = reach - distance(x)
        yield x, range(POWERS - rest, POWERS + BY + rest)


PLACES = [(x, y) for x, ys in rows_of(POWERS) for y in ys]
SLOT = {place: i for i, place in enumerate(sorted(PLACES, key=lambda place: corner(*place)))}
EARLY = sum(not corner(*place) for place in PLACES)


def ready(x, y, power):
    if power == 0:
        return not corner(x, y)
    around = ((x, y), (x - 1, y), (x + 1, y), (x, y - 1), (x, y + 1))
    return all(ready(i, j, power - 1) for i, j in around)


def state_shapes(count):
    field = (count * COMP, RHS, LANES)
    return (
        [field] * 4 + [(count, 24, LANES)] * 2 + [(count * 6, RHS, LANES)] * 2
        + [(count, RHS, LANES)] * 2
    )


def powers_part(early, blocks, first_state, mine, basis_ref):
    lane = lane_index()
    first, last = lane == 0, lane == LANES - 1
    MAIN, GHOST, COEF, FACE, SCALE = 0, 2, 4, 6, 8

    def held(kind, x, y, power):
        return first_state[kind] if early or ready(x, y, power) else mine[kind]

    def place_column(src, x, y, field_at, entry_at, stride, eta_at, ghost_at, col):
        at = SLOT[x, y]
        for comp in range(COMP):
            mine[MAIN][at * COMP + comp] = src[field_at[comp] : field_at[comp] + RHS, :]
        mine[COEF][at, 16:24, :] = jnp.broadcast_to(src[eta_at : eta_at + 1, :], (8, LANES))
        if distance(x) + distance(y) >= POWERS:
            return
        for half in range(2):
            start = entry_at + half * 8 * stride
            mine[COEF][at, half * 8 : half * 8 + 8, :] = (
                src[pl.ds(start, 8, stride=stride), :] if stride > 1 else src[start : start + 8, :]
            )
        shift = (-8 * col - 4) % LANES
        for comp in range(COMP):
            row = ghost_at + comp * RHS
            mine[GHOST][at * COMP + comp] = pltpu.roll(src[row : row + RHS, :], shift, 1)
        for part in range(3):
            row = ghost_at + COMP * RHS + part * 8
            mine[COEF + 1][at, part * 8 : part * 8 + 8, :] = pltpu.roll(
                src[row : row + 8, :], shift, 1
            )

    if early:
        own_ref, left_ref, right_ref, front_ref, back_ref = blocks
        for src, base, off_x, off_y in (
            (own_ref, 0, 0, 0), (left_ref, -LAYER, -1, 0), (right_ref, 0, 1, 0),
            (front_ref, 0, 0, -1), (back_ref, 0, 0, 1),
        ):
            for x in range(BX):
                for y in range(BY):
                    col = x * BY + y
                    place_column(
                        src, POWERS + off_x * BX + x, POWERS + off_y * BY + y,
                        [base + FIELD_AT + (comp * COLS + col) * RHS for comp in range(COMP)],
                        base + couple_at(x) + y, BY, base + ETA_AT + col, base + GHOST_AT, col,
                    )
    else:
        low_ref, high_ref = blocks
        for src, top in ((low_ref, True), (high_ref, False)):
            for place, (side, a, b) in enumerate(CORNER):
                x = POWERS + BX - 1 + a if side else POWERS - a
                y = POWERS - b if top else POWERS + BY - 1 + b
                col = (a - 1 if side else BX - a) * BY + (BY - b if top else b - 1)
                place_column(
                    src, x, y, [(place * COMP + comp) * RHS for comp in range(COMP)],
                    C_COUPLE_AT + place * 16, 1, C_ETA_AT + place, C_GHOST_AT, col,
                )

    def shifted(value, other):
        up, down = pltpu.roll(value, LANES - 1, 1), pltpu.roll(value, 1, 1)
        other_up, other_down = pltpu.roll(other, LANES - 1, 1), pltpu.roll(other, 1, 1)
        return (
            jnp.where(last, other_up, up), jnp.where(first, other_down, down),
            jnp.where(last, up, other_up), jnp.where(first, down, other_down),
        )

    def eta_at(kind, x, y):
        return held(kind, x, y, 0)[SLOT[x, y], 16:24, :]

    def faces(outer, x, y, eta, up, down):
        kind, at = COEF + outer, SLOT[x, y]
        around = [
            eta_at(kind, x - 1, y), eta_at(kind, x + 1, y),
            eta_at(kind, x, y - 1), eta_at(kind, x, y + 1), down, up,
        ]
        kappas = [eta + beside for beside in around]
        for index, kappa in enumerate(kappas):
            mine[FACE + outer][at * 6 + index] = kappa
        total = (kappas[0] + kappas[1]) + (kappas[2] + kappas[3]) + (kappas[4] + kappas[5])
        diagonal = held(kind, x, y, 0)[at, pl.ds(0, COMP, stride=COMP + 1), :]
        mine[SCALE + outer][at, 0:COMP, :] = jnp.where(
            eta[0:COMP, :] < 0.0, 1.0 / (diagonal - total[0:COMP, :]), 0.0
        )

    for x, ys in rows_of(POWERS - 1):
        for y in ys:
            if ready(x, y, 1) != early:
                continue
            eta, eta_ghost = eta_at(COEF, x, y), eta_at(COEF + 1, x, y)
            up, down, ghost_up, ghost_down = shifted(eta, eta_ghost)
            faces(0, x, y, eta, up, down)
            if distance(x) + distance(y) < POWERS - 1:
                faces(1, x, y, eta_ghost, ghost_up, ghost_down)

    def spread(ref, at, row):
        return jnp.broadcast_to(ref[at, row : row + 1, :], (RHS, LANES))

    def apply(outer, power, x, y, before, centre, after, up, down):
        at = SLOT[x, y]
        table = held(COEF + outer, x, y, 0)
        faces_of, inverse = held(FACE + outer, x, y, 1), held(SCALE + outer, x, y, 1)
        kappa = [faces_of[at * 6 + index] for index in range(6)]
        results = []
        for comp in range(COMP):
            beside = [
                load(outer, power, x - 1, y, comp), load(outer, power, x + 1, y, comp),
                before[comp], after[comp], down[comp], up[comp],
            ]
            terms = [k * v for k, v in zip(kappa, beside)]
            terms += [
                spread(table, at, comp * COMP + d) * centre[d] for d in range(COMP) if d != comp
            ]
            while len(terms) > 1:
                terms = [
                    terms[i] + terms[i + 1] if i + 1 < len(terms) else terms[i]
                    for i in range(0, len(terms), 2)
                ]
            results.append(terms[0] * spread(inverse, at, comp))
        return results

    def load(outer, power, x, y, comp):
        kind = (GHOST if outer else MAIN) + power % 2
        return held(kind, x, y, power)[SLOT[x, y] * COMP + comp]

    for power in range(1, POWERS + 1):
        limit = POWERS - power
        for x, ys in rows_of(limit):
            rows = {}

            def at_row(outer, y, x=x, rows=rows, power=power):
                if (outer, y) not in rows:
                    rows[outer, y] = [load(outer, power - 1, x, y, comp) for comp in range(COMP)]
                return rows[outer, y]

            for y in ys:
                if ready(x, y, power) != early:
                    continue
                at = SLOT[x, y]
                reach = distance(x) + distance(y)
                centre, outer = at_row(0, y), at_row(1, y)
                moves = [shifted(c, o) for c, o in zip(centre, outer)]
                results = apply(
                    0, power - 1, x, y, at_row(0, y - 1), centre, at_row(0, y + 1),
                    [m[0] for m in moves], [m[1] for m in moves],
                )
                for comp in range(COMP):
                    if limit:
                        mine[MAIN + power % 2][at * COMP + comp] = results[comp]
                if reach == 0:
                    for comp in range(COMP):
                        tile = comp * COLS + (x - POWERS) * BY + (y - POWERS)
                        if power == 1:
                            basis_ref[tile, 0:RHS, :] = centre[comp]
                        basis_ref[tile, power * RHS : power * RHS + RHS, :] = results[comp]
                if reach < limit:
                    outside = apply(
                        1, power - 1, x, y, at_row(1, y - 1), outer, at_row(1, y + 1),
                        [m[2] for m in moves], [m[3] for m in moves],
                    )
                    for comp in range(COMP):
                        mine[GHOST + power % 2][at * COMP + comp] = outside[comp]


def early_kernel(*refs):
    powers_part(True, refs[:5], refs[5:15], refs[5:15], refs[15])


def late_kernel(*refs):
    blocks, first_state, early_basis = refs[:2], refs[2:12], refs[12]
    basis_ref, gram_ref, mine, square = refs[13], refs[14], refs[15:25], refs[25]
    for x in range(BX):
        for y in range(BY):
            for power in range(1, POWERS + 1):
                if ready(POWERS + x, POWERS + y, power):
                    start = 0 if power == 1 else power * RHS
                    stop = power * RHS + RHS
                    for comp in range(COMP):
                        tile = comp * COLS + x * BY + y
                        basis_ref[tile, start:stop, :] = early_basis[tile, start:stop, :]
    powers_part(False, blocks, first_state, mine, basis_ref)
    lane = lane_index()
    order = (POWERS + 1) * RHS
    total = jnp.zeros((order, order), jnp.float32)
    for tile in range(0, COMP * COLS, 2):
        both = jnp.concatenate([basis_ref[tile], basis_ref[tile + 1]], axis=1)
        total = total + lax.dot_general(
            both, both, (((1,), (1,)), ((), ())),
            precision=HIGHEST, preferred_element_type=jnp.float32,
        )
    square[...] = jnp.zeros_like(square)
    square[:, 0:order] = total
    packed = jnp.zeros((RHS, LANES), jnp.float32)
    start = 0
    for block in range(POWERS + 1):
        width = order - block * RHS
        value = pltpu.roll(
            square[block * RHS : block * RHS + RHS, :], (start - block * RHS) % LANES, 1
        )
        packed = jnp.where((lane >= start) & (lane < start + width), value, packed)
        start += width
    gram_ref[...] = packed


def early_powers(*blocks):
    basis = (COMP * COLS, (POWERS + 1) * RHS, LANES)
    return pl.pallas_call(
        early_kernel,
        out_shape=[
            jax.ShapeDtypeStruct(shape, jnp.float32) for shape in state_shapes(EARLY) + [basis]
        ],
        in_specs=[VMEM] * 5,
        out_specs=[VMEM] * 11,
        compiler_params=pltpu.CompilerParams(vmem_limit_bytes=20 * 2**20),
        cost_estimate=pl.CostEstimate(flops=5_000_000, bytes_accessed=8_000_000, transcendentals=0),
    )(*blocks)


def late_powers(low, high, state):
    basis = (COMP * COLS, (POWERS + 1) * RHS, LANES)
    return pl.pallas_call(
        late_kernel,
        out_shape=(
            jax.ShapeDtypeStruct(basis, jnp.float32),
            jax.ShapeDtypeStruct((RHS, LANES), jnp.float32),
        ),
        in_specs=[VMEM] * 13,
        out_specs=(VMEM,) * 2,
        scratch_shapes=[pltpu.VMEM(shape, jnp.float32) for shape in state_shapes(len(PLACES))]
        + [pltpu.VMEM(((POWERS + 1) * RHS, LANES), jnp.float32)],
        compiler_params=pltpu.CompilerParams(vmem_limit_bytes=36 * 2**20),
    )(low, high, *state)


def finish_kernel(gram_ref, basis_ref, out_ref, factor_ref, square, upper):
    lane = lane_index()
    order = (POWERS + 1) * RHS
    parts = [gram_ref[i] for i in range(gram_ref.shape[0])]
    while len(parts) > 1:
        parts = [
            parts[i] + parts[i + 1] if i + 1 < len(parts) else parts[i]
            for i in range(0, len(parts), 2)
        ]
    packed = parts[0]
    square[...] = jnp.zeros_like(square)
    start = 0
    for block in range(POWERS + 1):
        width = order - block * RHS
        value = pltpu.roll(packed, (block * RHS - start) % LANES, 1)
        keep = (lane >= block * RHS) & (lane < order)
        square[block * RHS : block * RHS + RHS, :] = jnp.where(keep, value, 0.0)
        start += width
    half = square[...]
    other = half.T
    gram = []
    for block in range(POWERS + 1):
        rows = slice(block * RHS, block * RHS + RHS)
        gram.append(jnp.where(lane < block * RHS, other[rows, :], half[rows, :]))
    summed = [tile + pltpu.roll(tile, LANES - RHS, 1) for tile in gram]
    normal = [summed[i] + summed[i + 1] for i in range(POWERS)] + [summed[0]]

    upper[...] = jnp.zeros_like(upper)
    number = lane[0:1, :]

    def wide(value, column):
        return jnp.broadcast_to(value[:, column : column + 1], value.shape)

    def pair(matrix, step):
        tile, row = step // RHS, step % RHS
        p, q = matrix[tile][row : row + 1, :], matrix[tile][row + 1 : row + 2, :]
        one, cross, far = wide(p, step), wide(p, step + 1), wide(q, step + 1)
        inverse = 1.0 / one
        ratio = cross * inverse
        other = far - cross * ratio
        rest = q - ratio * p
        inverse_other = 1.0 / other
        second = rest * inverse_other
        first = p * inverse - ratio * second
        return p, rest, one, other, first, second, inverse, inverse_other, ratio

    for step in range(0, order, 2):
        tile = step // RHS
        low = tile if step % RHS < RHS - 2 else tile + 1
        p, rest, one, other, first, second, _, _, _ = pair(gram, step)
        top = jnp.where(number >= step, p * lax.rsqrt(one), 0.0)
        bottom = jnp.where(number > step, rest * lax.rsqrt(other), 0.0)
        upper[step : step + 1, :] = top[0:1, :]
        upper[step + 1 : step + 2, :] = bottom[0:1, :]
        for i in range(low, POWERS + 1):
            gram[i] = gram[i] - wide(gram[i], step) * first - wide(gram[i], step + 1) * second
        if step < POWERS * RHS:
            _, _, _, _, first, second, inverse, inverse_other, ratio = pair(normal, step)
            mixed = ratio * inverse_other
            at_one, at_other = number == step, number == step + 1
            cleared = (lane == step) | (lane == step + 1)
            first = jnp.where(
                at_one, -(inverse + ratio * mixed), jnp.where(at_other, mixed, first)
            )
            second = jnp.where(at_one, mixed, jnp.where(at_other, -inverse_other, second))
            for i in range(low, POWERS + 1):
                normal[i] = (
                    jnp.where(cleared, 0.0, normal[i])
                    - wide(normal[i], step) * first
                    - wide(normal[i], step + 1) * second
                )
    factor_ref[...] = upper[0:order, 0:order]
    answer = normal[POWERS]
    weights = [
        jnp.broadcast_to(answer[:, i : i + 1], (RHS, LANES)) for i in range(POWERS * RHS)
    ]

    def combine(tile, carry):
        sums = [None] * 4
        for i in range(POWERS * RHS):
            term = weights[i] * jnp.broadcast_to(basis_ref[tile, i : i + 1, :], (RHS, LANES))
            sums[i % 4] = term if sums[i % 4] is None else sums[i % 4] + term
        out_ref[pl.ds(tile, RHS, stride=COMP * COLS), :] = (sums[0] + sums[1]) + (
            sums[2] + sums[3]
        )
        return carry

    lax.fori_loop(0, COMP * COLS, combine, 0, unroll=4)


def finish(gram, basis):
    order = (POWERS + 1) * RHS
    return pl.pallas_call(
        finish_kernel,
        out_shape=(
            jax.ShapeDtypeStruct((RHS * COMP * COLS, LANES), jnp.float32),
            jax.ShapeDtypeStruct((order, order), jnp.float32),
        ),
        in_specs=[VMEM] * 2,
        out_specs=(VMEM,) * 2,
        scratch_shapes=[
            pltpu.VMEM((LANES, LANES), jnp.float32),
            pltpu.VMEM((order, LANES), jnp.float32),
        ],
        compiler_params=pltpu.CompilerParams(vmem_limit_bytes=6 * 2**20),
    )(gram, basis)


def moved(block, axis, step):
    count = lax.axis_size(axis)
    pairs = [(i, i + step) for i in range(count) if 0 <= i + step < count]
    return lax.ppermute(block, axis, pairs)


def swapped(to_low, to_high, axis, even):
    count = lax.axis_size(axis)
    inner = [(i, i ^ 1) for i in range(count)]
    outer = [(i, ((i + 1) ^ 1) - 1) for i in range(1, count - 1)]
    two = lax.ppermute(jnp.where(even, to_low, to_high), axis, outer)
    one = lax.ppermute(jnp.where(even, to_high, to_low), axis, inner)
    return two, one


def sorted_pair(two, one, even):
    return jnp.where(even, two, one), jnp.where(even, one, two)


def gathered(tile, axes):
    count = lax.axis_size(axes)
    return lax.all_to_all(jnp.broadcast_to(tile[None], (count,) + tile.shape), axes, 0, 0)


def local(residuals, shear_rate, coupling):
    block, low, high = pack(residuals, shear_rate, coupling)
    even_x, even_y, even_z = (lax.axis_index(axis) % 2 == 0 for axis in ("gx", "gy", "gz"))
    two, one = swapped(low, high, "gz", even_z)
    own = lax.dynamic_update_slice(block, two + one, (GHOST_AT, 0))
    left, right = sorted_pair(*swapped(own[:SIDE_ROWS], own[LAYER:], "gx", even_x), even_x)
    front, back = moved(own, "gy", 1), moved(own, "gy", -1)
    down, up = corners(left, right)
    low_corner, high_corner = sorted_pair(*swapped(down, up, "gy", even_y), even_y)
    state = early_powers(own, left, right, front, back)
    basis, gram = late_powers(low_corner, high_corner, state)
    gram = jnp.sum(gathered(gram, ("gy", "gz")), axis=0)
    correction, factor = finish(gathered(gram, "gx"), basis)
    return correction.reshape(residuals.shape), factor


def solution(mesh):
    in_specs = (
        P(None, None, "gx", "gy", "gz"),
        P("gx", "gy", "gz"),
        P(None, None, "gx", "gy", "gz"),
    )
    out_specs = (P(None, None, "gx", "gy", "gz"), P())
    return jax.shard_map(local, mesh=mesh, in_specs=in_specs, out_specs=out_specs, check_vma=False)
```

```python
import jax
import jax.numpy as jnp
from jax import lax
from jax.experimental import pallas as pl
from jax.experimental.pallas import tpu as pltpu
from jax.sharding import PartitionSpec as P

POWERS = 4
RHS = 8
COMP = 4
BX = 4
BY = 4
LANES = 128
COLS = BX * BY
GRID = BX + 2 * POWERS
HIGHEST = lax.Precision.HIGHEST
VMEM = pl.BlockSpec(memory_space=pltpu.VMEM)

FIELD_ROWS = COMP * COLS * RHS
LAYER = COMP * COMP * BY
GHOST_ROWS = COMP * RHS + 24
FIELD_AT = GHOST_ROWS + LAYER
ETA_AT = FIELD_AT + FIELD_ROWS
TAIL_AT = ETA_AT + COLS
BLOCK_ROWS = TAIL_AT + (BX - 1) * LAYER
SIDE_ROWS = BLOCK_ROWS - LAYER - GHOST_ROWS
LOW_BASE = -GHOST_ROWS - LAYER
HIGH_BASE = -GHOST_ROWS

NEAR = [(1, 1), (1, 2), (2, 1)]
FAR = [(1, 3), (2, 2), (3, 1)]
CORNER = [(side, a, b) for a, b in NEAR + FAR for side in (0, 1)]
NEAR_COUNT = 2 * len(NEAR)
C_COUPLE_AT = len(CORNER) * COMP * RHS
C_ETA_AT = C_COUPLE_AT + NEAR_COUNT * 16
C_GHOST_AT = C_ETA_AT + 16
CORNER_ROWS = C_GHOST_AT + GHOST_ROWS


def couple_at(x):
    return TAIL_AT + (x - 1) * LAYER if x else GHOST_ROWS


def lane_index():
    return lax.broadcasted_iota(jnp.int32, (RHS, LANES), 1)


def pack_kernel(raw_ref, main_ref, low_ref, high_ref):
    lane = lane_index()
    raw_couple = FIELD_ROWS
    raw_shear = FIELD_ROWS + BX * LAYER
    shear = raw_ref[raw_shear : raw_shear + COLS, :]
    eta = -0.5 * (0.2 + (1.0 - jnp.exp(-100.0 * shear)) / shear)
    main_ref[ETA_AT:TAIL_AT, :] = eta
    main_ref[0:GHOST_ROWS, :] = jnp.zeros((GHOST_ROWS, LANES), jnp.float32)
    for entry in range(COMP * COMP):
        for x in range(BX):
            start = raw_couple + entry * COLS + x * BY
            row = couple_at(x) + entry * BY
            main_ref[row : row + BY, :] = raw_ref[start : start + BY, :]

    def pack(group, load):
        low = jnp.zeros((RHS, LANES), jnp.float32)
        high = jnp.zeros((RHS, LANES), jnp.float32)
        for col in range(COLS):
            turned = pltpu.roll(load(col), (8 * col + 4) % LANES, 1)
            here = lane // 4
            high = jnp.where(here == 2 * col, turned, high)
            low = jnp.where(here == 2 * col + 1, turned, low)
        low_ref[group * 8 : group * 8 + 8, :] = low
        high_ref[group * 8 : group * 8 + 8, :] = high

    for comp in range(COMP):

        def load_field(col):
            place = comp * COLS + col
            value = raw_ref[pl.ds(place, RHS, stride=COMP * COLS), :]
            row = FIELD_AT + place * RHS
            main_ref[row : row + RHS, :] = value
            return value

        pack(comp, load_field)
    for half in range(2):
        pack(
            COMP + half,
            lambda col: raw_ref[pl.ds(raw_couple + half * 8 * COLS + col, 8, stride=COLS), :],
        )
    pack(
        COMP + 2,
        lambda col: jnp.broadcast_to(eta[col : col + 1, :], (RHS, LANES)),
    )


def pack(residuals, shear_rate, coupling):
    raw = jnp.concatenate(
        [part.reshape(-1, LANES) for part in (residuals, coupling, shear_rate)], axis=0
    )
    return pl.pallas_call(
        pack_kernel,
        out_shape=(
            jax.ShapeDtypeStruct((BLOCK_ROWS, LANES), jnp.float32),
            jax.ShapeDtypeStruct((GHOST_ROWS, LANES), jnp.float32),
            jax.ShapeDtypeStruct((GHOST_ROWS, LANES), jnp.float32),
        ),
        in_specs=[VMEM],
        out_specs=(VMEM,) * 3,
        compiler_params=pltpu.CompilerParams(vmem_limit_bytes=4 * 2**20),
    )(raw)


def corner_kernel(left_ref, right_ref, left_ghost, right_ghost, down_ref, up_ref):
    lane = lane_index()
    for out_ref, top in ((down_ref, False), (up_ref, True)):
        for place, (side, a, b) in enumerate(CORNER):
            src = right_ref if side else left_ref
            base = HIGH_BASE if side else LOW_BASE
            x = a - 1 if side else BX - a
            y = BY - b if top else b - 1
            col = x * BY + y
            for comp in range(COMP):
                start = base + FIELD_AT + (comp * COLS + col) * RHS
                row = (place * COMP + comp) * RHS
                out_ref[row : row + RHS, :] = src[start : start + RHS, :]
            if place < NEAR_COUNT:
                for half in range(2):
                    row = C_COUPLE_AT + place * 16 + half * 8
                    start = base + couple_at(x) + half * 8 * BY + y
                    out_ref[row : row + 8, :] = src[pl.ds(start, 8, stride=BY), :]
            start = base + ETA_AT + col
            out_ref[C_ETA_AT + place : C_ETA_AT + place + 1, :] = src[start : start + 1, :]
        out_ref[C_ETA_AT + len(CORNER) : C_GHOST_AT, :] = jnp.zeros(
            (16 - len(CORNER), LANES), jnp.float32
        )
        for row in range(0, GHOST_ROWS, 8):
            right, left = right_ghost[row : row + 8, :], left_ghost[row : row + 8, :]
            out_ref[C_GHOST_AT + row : C_GHOST_AT + row + 8, :] = jnp.where(
                lane < LANES // 2, right, left
            )


def corners(*parts):
    return pl.pallas_call(
        corner_kernel,
        out_shape=(jax.ShapeDtypeStruct((CORNER_ROWS, LANES), jnp.float32),) * 2,
        in_specs=[VMEM] * 4,
        out_specs=(VMEM,) * 2,
        compiler_params=pltpu.CompilerParams(vmem_limit_bytes=4 * 2**20),
    )(*parts)


def distance(place):
    return max(POWERS - place, 0, place - (POWERS + BX - 1))


def corner(x, y):
    return distance(x) > 0 and distance(y) > 0


def rows_of(reach):
    for x in range(POWERS - reach, POWERS + BX + reach):
        rest = reach - distance(x)
        yield x, range(POWERS - rest, POWERS + BY + rest)


PLACES = [(x, y) for x, ys in rows_of(POWERS) for y in ys]
SLOT = {place: i for i, place in enumerate(sorted(PLACES, key=lambda place: corner(*place)))}
EARLY = sum(not corner(*place) for place in PLACES)


def ready(x, y, power):
    if power == 0:
        return not corner(x, y)
    around = ((x, y), (x - 1, y), (x + 1, y), (x, y - 1), (x, y + 1))
    return all(ready(i, j, power - 1) for i, j in around)


def state_shapes(count):
    field = (count * COMP, RHS, LANES)
    return (
        [field] * 4 + [(count, 24, LANES)] * 2 + [(count * 6, RHS, LANES)] * 2
        + [(count, RHS, LANES)] * 2
    )


def powers_part(early, blocks, first_state, mine, basis_ref):
    lane = lane_index()
    first, last = lane == 0, lane == LANES - 1
    MAIN, GHOST, COEF, FACE, SCALE = 0, 2, 4, 6, 8

    def held(kind, x, y, power):
        return first_state[kind] if early or ready(x, y, power) else mine[kind]

    def place_column(src, x, y, field_at, entry_at, stride, eta_at, ghosts, ghost_at, col):
        at = SLOT[x, y]
        for comp in range(COMP):
            mine[MAIN][at * COMP + comp] = src[field_at[comp] : field_at[comp] + RHS, :]
        mine[COEF][at, 16:24, :] = jnp.broadcast_to(src[eta_at : eta_at + 1, :], (8, LANES))
        if distance(x) + distance(y) >= POWERS:
            return
        for half in range(2):
            start = entry_at + half * 8 * stride
            mine[COEF][at, half * 8 : half * 8 + 8, :] = (
                src[pl.ds(start, 8, stride=stride), :] if stride > 1 else src[start : start + 8, :]
            )
        shift = (-8 * col - 4) % LANES
        for comp in range(COMP):
            row = ghost_at + comp * RHS
            mine[GHOST][at * COMP + comp] = pltpu.roll(ghosts[row : row + RHS, :], shift, 1)
        for part in range(3):
            row = ghost_at + COMP * RHS + part * 8
            mine[COEF + 1][at, part * 8 : part * 8 + 8, :] = pltpu.roll(
                ghosts[row : row + 8, :], shift, 1
            )

    if early:
        own_ref, left_ref, right_ref, front_ref, back_ref, left_ghost, right_ghost = blocks
        for src, base, ghosts, off_x, off_y in (
            (own_ref, 0, own_ref, 0, 0), (left_ref, LOW_BASE, left_ghost, -1, 0),
            (right_ref, HIGH_BASE, right_ghost, 1, 0),
            (front_ref, 0, front_ref, 0, -1), (back_ref, 0, back_ref, 0, 1),
        ):
            for x in range(BX):
                for y in range(BY):
                    col = x * BY + y
                    place_column(
                        src, POWERS + off_x * BX + x, POWERS + off_y * BY + y,
                        [base + FIELD_AT + (comp * COLS + col) * RHS for comp in range(COMP)],
                        base + couple_at(x) + y, BY, base + ETA_AT + col, ghosts, 0, col,
                    )
    else:
        low_ref, high_ref = blocks
        for src, top in ((low_ref, True), (high_ref, False)):
            for place, (side, a, b) in enumerate(CORNER):
                x = POWERS + BX - 1 + a if side else POWERS - a
                y = POWERS - b if top else POWERS + BY - 1 + b
                col = (a - 1 if side else BX - a) * BY + (BY - b if top else b - 1)
                place_column(
                    src, x, y, [(place * COMP + comp) * RHS for comp in range(COMP)],
                    C_COUPLE_AT + place * 16, 1, C_ETA_AT + place, src, C_GHOST_AT, col,
                )

    def shifted(value, other):
        up, down = pltpu.roll(value, LANES - 1, 1), pltpu.roll(value, 1, 1)
        other_up, other_down = pltpu.roll(other, LANES - 1, 1), pltpu.roll(other, 1, 1)
        return (
            jnp.where(last, other_up, up), jnp.where(first, other_down, down),
            jnp.where(last, up, other_up), jnp.where(first, down, other_down),
        )

    def eta_at(kind, x, y):
        return held(kind, x, y, 0)[SLOT[x, y], 16:24, :]

    def faces(outer, x, y, eta, up, down):
        kind, at = COEF + outer, SLOT[x, y]
        around = [
            eta_at(kind, x - 1, y), eta_at(kind, x + 1, y),
            eta_at(kind, x, y - 1), eta_at(kind, x, y + 1), down, up,
        ]
        kappas = [eta + beside for beside in around]
        for index, kappa in enumerate(kappas):
            mine[FACE + outer][at * 6 + index] = kappa
        total = (kappas[0] + kappas[1]) + (kappas[2] + kappas[3]) + (kappas[4] + kappas[5])
        diagonal = held(kind, x, y, 0)[at, pl.ds(0, COMP, stride=COMP + 1), :]
        mine[SCALE + outer][at, 0:COMP, :] = jnp.where(
            eta[0:COMP, :] < 0.0, 1.0 / (diagonal - total[0:COMP, :]), 0.0
        )

    for x, ys in rows_of(POWERS - 1):
        for y in ys:
            if ready(x, y, 1) != early:
                continue
            eta, eta_ghost = eta_at(COEF, x, y), eta_at(COEF + 1, x, y)
            up, down, ghost_up, ghost_down = shifted(eta, eta_ghost)
            faces(0, x, y, eta, up, down)
            if distance(x) + distance(y) < POWERS - 1:
                faces(1, x, y, eta_ghost, ghost_up, ghost_down)

    def spread(ref, at, row):
        return jnp.broadcast_to(ref[at, row : row + 1, :], (RHS, LANES))

    def apply(outer, power, x, y, before, centre, after, up, down):
        at = SLOT[x, y]
        table = held(COEF + outer, x, y, 0)
        faces_of, inverse = held(FACE + outer, x, y, 1), held(SCALE + outer, x, y, 1)
        kappa = [faces_of[at * 6 + index] for index in range(6)]
        results = []
        for comp in range(COMP):
            beside = [
                load(outer, power, x - 1, y, comp), load(outer, power, x + 1, y, comp),
                before[comp], after[comp], down[comp], up[comp],
            ]
            terms = [k * v for k, v in zip(kappa, beside)]
            terms += [
                spread(table, at, comp * COMP + d) * centre[d] for d in range(COMP) if d != comp
            ]
            while len(terms) > 1:
                terms = [
                    terms[i] + terms[i + 1] if i + 1 < len(terms) else terms[i]
                    for i in range(0, len(terms), 2)
                ]
            results.append(terms[0] * spread(inverse, at, comp))
        return results

    def load(outer, power, x, y, comp):
        kind = (GHOST if outer else MAIN) + power % 2
        return held(kind, x, y, power)[SLOT[x, y] * COMP + comp]

    for power in range(1, POWERS + 1):
        limit = POWERS - power
        for x, ys in rows_of(limit):
            rows = {}

            def at_row(outer, y, x=x, rows=rows, power=power):
                if (outer, y) not in rows:
                    rows[outer, y] = [load(outer, power - 1, x, y, comp) for comp in range(COMP)]
                return rows[outer, y]

            for y in ys:
                if ready(x, y, power) != early:
                    continue
                at = SLOT[x, y]
                reach = distance(x) + distance(y)
                centre, outer = at_row(0, y), at_row(1, y)
                moves = [shifted(c, o) for c, o in zip(centre, outer)]
                results = apply(
                    0, power - 1, x, y, at_row(0, y - 1), centre, at_row(0, y + 1),
                    [m[0] for m in moves], [m[1] for m in moves],
                )
                for comp in range(COMP):
                    if limit:
                        mine[MAIN + power % 2][at * COMP + comp] = results[comp]
                if reach == 0:
                    for comp in range(COMP):
                        tile = comp * COLS + (x - POWERS) * BY + (y - POWERS)
                        if power == 1:
                            basis_ref[tile, 0:RHS, :] = centre[comp]
                        basis_ref[tile, power * RHS : power * RHS + RHS, :] = results[comp]
                if reach < limit:
                    outside = apply(
                        1, power - 1, x, y, at_row(1, y - 1), outer, at_row(1, y + 1),
                        [m[2] for m in moves], [m[3] for m in moves],
                    )
                    for comp in range(COMP):
                        mine[GHOST + power % 2][at * COMP + comp] = outside[comp]


def early_kernel(*refs):
    powers_part(True, refs[:7], refs[7:17], refs[7:17], refs[17])


def late_kernel(*refs):
    blocks, first_state, early_basis = refs[:2], refs[2:12], refs[12]
    basis_ref, gram_ref, mine, square = refs[13], refs[14], refs[15:25], refs[25]
    for x in range(BX):
        for y in range(BY):
            for power in range(1, POWERS + 1):
                if ready(POWERS + x, POWERS + y, power):
                    start = 0 if power == 1 else power * RHS
                    stop = power * RHS + RHS
                    for comp in range(COMP):
                        tile = comp * COLS + x * BY + y
                        basis_ref[tile, start:stop, :] = early_basis[tile, start:stop, :]
    powers_part(False, blocks, first_state, mine, basis_ref)
    lane = lane_index()
    order = (POWERS + 1) * RHS
    total = jnp.zeros((order, order), jnp.float32)
    for tile in range(0, COMP * COLS, 2):
        both = jnp.concatenate([basis_ref[tile], basis_ref[tile + 1]], axis=1)
        total = total + lax.dot_general(
            both, both, (((1,), (1,)), ((), ())),
            precision=HIGHEST, preferred_element_type=jnp.float32,
        )
    square[...] = jnp.zeros_like(square)
    square[:, 0:order] = total
    packed = jnp.zeros((RHS, LANES), jnp.float32)
    start = 0
    for block in range(POWERS + 1):
        width = order - block * RHS
        value = pltpu.roll(
            square[block * RHS : block * RHS + RHS, :], (start - block * RHS) % LANES, 1
        )
        packed = jnp.where((lane >= start) & (lane < start + width), value, packed)
        start += width
    gram_ref[...] = packed


def early_powers(*blocks):
    basis = (COMP * COLS, (POWERS + 1) * RHS, LANES)
    return pl.pallas_call(
        early_kernel,
        out_shape=[
            jax.ShapeDtypeStruct(shape, jnp.float32) for shape in state_shapes(EARLY) + [basis]
        ],
        in_specs=[VMEM] * 7,
        out_specs=[VMEM] * 11,
        compiler_params=pltpu.CompilerParams(vmem_limit_bytes=20 * 2**20),
        cost_estimate=pl.CostEstimate(flops=5_000_000, bytes_accessed=8_000_000, transcendentals=0),
    )(*blocks)


def late_powers(low, high, state):
    basis = (COMP * COLS, (POWERS + 1) * RHS, LANES)
    return pl.pallas_call(
        late_kernel,
        out_shape=(
            jax.ShapeDtypeStruct(basis, jnp.float32),
            jax.ShapeDtypeStruct((RHS, LANES), jnp.float32),
        ),
        in_specs=[VMEM] * 13,
        out_specs=(VMEM,) * 2,
        scratch_shapes=[pltpu.VMEM(shape, jnp.float32) for shape in state_shapes(len(PLACES))]
        + [pltpu.VMEM(((POWERS + 1) * RHS, LANES), jnp.float32)],
        compiler_params=pltpu.CompilerParams(vmem_limit_bytes=36 * 2**20),
    )(low, high, *state)


def finish_kernel(gram_ref, basis_ref, out_ref, factor_ref, square, upper):
    lane = lane_index()
    order = (POWERS + 1) * RHS
    parts = [gram_ref[i] for i in range(gram_ref.shape[0])]
    while len(parts) > 1:
        parts = [
            parts[i] + parts[i + 1] if i + 1 < len(parts) else parts[i]
            for i in range(0, len(parts), 2)
        ]
    packed = parts[0]
    square[...] = jnp.zeros_like(square)
    start = 0
    for block in range(POWERS + 1):
        width = order - block * RHS
        value = pltpu.roll(packed, (block * RHS - start) % LANES, 1)
        keep = (lane >= block * RHS) & (lane < order)
        square[block * RHS : block * RHS + RHS, :] = jnp.where(keep, value, 0.0)
        start += width
    half = square[...]
    other = half.T
    gram = []
    for block in range(POWERS + 1):
        rows = slice(block * RHS, block * RHS + RHS)
        gram.append(jnp.where(lane < block * RHS, other[rows, :], half[rows, :]))
    summed = [tile + pltpu.roll(tile, LANES - RHS, 1) for tile in gram]
    normal = [summed[i] + summed[i + 1] for i in range(POWERS)] + [summed[0]]

    upper[...] = jnp.zeros_like(upper)
    number = lane[0:1, :]

    def wide(value, column):
        return jnp.broadcast_to(value[:, column : column + 1], value.shape)

    def pair(matrix, step):
        tile, row = step // RHS, step % RHS
        p, q = matrix[tile][row : row + 1, :], matrix[tile][row + 1 : row + 2, :]
        one, cross, far = wide(p, step), wide(p, step + 1), wide(q, step + 1)
        inverse = 1.0 / one
        ratio = cross * inverse
        other = far - cross * ratio
        rest = q - ratio * p
        inverse_other = 1.0 / other
        second = rest * inverse_other
        first = p * inverse - ratio * second
        return p, rest, one, other, first, second, inverse, inverse_other, ratio

    for step in range(0, order, 2):
        tile = step // RHS
        low = tile if step % RHS < RHS - 2 else tile + 1
        p, rest, one, other, first, second, _, _, _ = pair(gram, step)
        top = jnp.where(number >= step, p * lax.rsqrt(one), 0.0)
        bottom = jnp.where(number > step, rest * lax.rsqrt(other), 0.0)
        upper[step : step + 1, :] = top[0:1, :]
        upper[step + 1 : step + 2, :] = bottom[0:1, :]
        for i in range(low, POWERS + 1):
            gram[i] = gram[i] - wide(gram[i], step) * first - wide(gram[i], step + 1) * second
        if step < POWERS * RHS:
            _, _, _, _, first, second, inverse, inverse_other, ratio = pair(normal, step)
            mixed = ratio * inverse_other
            at_one, at_other = number == step, number == step + 1
            cleared = (lane == step) | (lane == step + 1)
            first = jnp.where(
                at_one, -(inverse + ratio * mixed), jnp.where(at_other, mixed, first)
            )
            second = jnp.where(at_one, mixed, jnp.where(at_other, -inverse_other, second))
            for i in range(low, POWERS + 1):
                normal[i] = (
                    jnp.where(cleared, 0.0, normal[i])
                    - wide(normal[i], step) * first
                    - wide(normal[i], step + 1) * second
                )
    factor_ref[...] = upper[0:order, 0:order]
    answer = normal[POWERS]
    weights = [
        jnp.broadcast_to(answer[:, i : i + 1], (RHS, LANES)) for i in range(POWERS * RHS)
    ]

    def combine(tile, carry):
        sums = [None] * 4
        for i in range(POWERS * RHS):
            term = weights[i] * jnp.broadcast_to(basis_ref[tile, i : i + 1, :], (RHS, LANES))
            sums[i % 4] = term if sums[i % 4] is None else sums[i % 4] + term
        out_ref[pl.ds(tile, RHS, stride=COMP * COLS), :] = (sums[0] + sums[1]) + (
            sums[2] + sums[3]
        )
        return carry

    lax.fori_loop(0, COMP * COLS, combine, 0, unroll=4)


def finish(gram, basis):
    order = (POWERS + 1) * RHS
    return pl.pallas_call(
        finish_kernel,
        out_shape=(
            jax.ShapeDtypeStruct((RHS * COMP * COLS, LANES), jnp.float32),
            jax.ShapeDtypeStruct((order, order), jnp.float32),
        ),
        in_specs=[VMEM] * 2,
        out_specs=(VMEM,) * 2,
        scratch_shapes=[
            pltpu.VMEM((LANES, LANES), jnp.float32),
            pltpu.VMEM((order, LANES), jnp.float32),
        ],
        compiler_params=pltpu.CompilerParams(vmem_limit_bytes=6 * 2**20),
    )(gram, basis)


def moved(block, axis, step):
    count = lax.axis_size(axis)
    pairs = [(i, i + step) for i in range(count) if 0 <= i + step < count]
    return lax.ppermute(block, axis, pairs)


def swapped(to_low, to_high, axis, even):
    count = lax.axis_size(axis)
    inner = [(i, i ^ 1) for i in range(count)]
    outer = [(i, ((i + 1) ^ 1) - 1) for i in range(1, count - 1)]
    two = lax.ppermute(jnp.where(even, to_low, to_high), axis, outer)
    one = lax.ppermute(jnp.where(even, to_high, to_low), axis, inner)
    return two, one


def sorted_pair(two, one, even):
    return jnp.where(even, two, one), jnp.where(even, one, two)


def gathered(tile, axes):
    count = lax.axis_size(axes)
    return lax.all_to_all(jnp.broadcast_to(tile[None], (count,) + tile.shape), axes, 0, 0)


def local(residuals, shear_rate, coupling):
    block, low, high = pack(residuals, shear_rate, coupling)
    even_x, even_y, even_z = (lax.axis_index(axis) % 2 == 0 for axis in ("gx", "gy", "gz"))
    two, one = swapped(low, high, "gz", even_z)
    to_low, to_high = block[GHOST_ROWS : GHOST_ROWS + SIDE_ROWS], block[GHOST_ROWS + LAYER :]
    left, right = sorted_pair(*swapped(to_low, to_high, "gx", even_x), even_x)
    ghosts = two + one
    left_ghost, right_ghost = sorted_pair(*swapped(ghosts, ghosts, "gx", even_x), even_x)
    own = lax.dynamic_update_slice(block, ghosts, (0, 0))
    front, back = moved(own, "gy", 1), moved(own, "gy", -1)
    down, up = corners(left, right, left_ghost, right_ghost)
    low_corner, high_corner = sorted_pair(*swapped(down, up, "gy", even_y), even_y)
    state = early_powers(own, left, right, front, back, left_ghost, right_ghost)
    basis, gram = late_powers(low_corner, high_corner, state)
    gram = jnp.sum(gathered(gram, ("gy", "gz")), axis=0)
    correction, factor = finish(gathered(gram, "gx"), basis)
    return correction.reshape(residuals.shape), factor


def solution(mesh):
    in_specs = (
        P(None, None, "gx", "gy", "gz"),
        P("gx", "gy", "gz"),
        P(None, None, "gx", "gy", "gz"),
    )
    out_specs = (P(None, None, "gx", "gy", "gz"), P())
    return jax.shard_map(local, mesh=mesh, in_specs=in_specs, out_specs=out_specs, check_vma=False)
```

```python
import jax
import jax.numpy as jnp
from jax import lax
from jax.experimental import pallas as pl
from jax.experimental.pallas import tpu as pltpu
from jax.sharding import PartitionSpec as P

POWERS = 4
RHS = 8
COMP = 4
BX = 4
BY = 4
LANES = 128
COLS = BX * BY
GRID = BX + 2 * POWERS
HIGHEST = lax.Precision.HIGHEST
VMEM = pl.BlockSpec(memory_space=pltpu.VMEM)

FIELD_ROWS = COMP * COLS * RHS
LAYER = COMP * COMP * BY
GHOST_ROWS = COMP * RHS + 24
FIELD_AT = GHOST_ROWS + LAYER
ETA_AT = FIELD_AT + FIELD_ROWS
TAIL_AT = ETA_AT + COLS
BLOCK_ROWS = TAIL_AT + (BX - 1) * LAYER
SIDE_ROWS = BLOCK_ROWS - LAYER - GHOST_ROWS
LOW_BASE = -GHOST_ROWS - LAYER
HIGH_BASE = -GHOST_ROWS

NEAR = [(1, 1), (1, 2), (2, 1)]
FAR = [(1, 3), (2, 2), (3, 1)]
CORNER = [(side, a, b) for a, b in NEAR + FAR for side in (0, 1)]
NEAR_COUNT = 2 * len(NEAR)
C_COUPLE_AT = len(CORNER) * COMP * RHS
C_ETA_AT = C_COUPLE_AT + NEAR_COUNT * 16
C_GHOST_AT = C_ETA_AT + 16
CORNER_ROWS = C_GHOST_AT + GHOST_ROWS


def couple_at(x):
    return TAIL_AT + (x - 1) * LAYER if x else GHOST_ROWS


def lane_index():
    return lax.broadcasted_iota(jnp.int32, (RHS, LANES), 1)


def pack_kernel(raw_ref, main_ref, low_ref, high_ref):
    lane = lane_index()
    raw_couple = FIELD_ROWS
    raw_shear = FIELD_ROWS + BX * LAYER
    shear = raw_ref[raw_shear : raw_shear + COLS, :]
    eta = -0.5 * (0.2 + (1.0 - jnp.exp(-100.0 * shear)) / shear)
    main_ref[ETA_AT:TAIL_AT, :] = eta
    main_ref[0:GHOST_ROWS, :] = jnp.zeros((GHOST_ROWS, LANES), jnp.float32)
    for entry in range(COMP * COMP):
        for x in range(BX):
            start = raw_couple + entry * COLS + x * BY
            row = couple_at(x) + entry * BY
            main_ref[row : row + BY, :] = raw_ref[start : start + BY, :]

    def pack(group, load):
        low = jnp.zeros((RHS, LANES), jnp.float32)
        high = jnp.zeros((RHS, LANES), jnp.float32)
        for col in range(COLS):
            turned = pltpu.roll(load(col), (8 * col + 4) % LANES, 1)
            here = lane // 4
            high = jnp.where(here == 2 * col, turned, high)
            low = jnp.where(here == 2 * col + 1, turned, low)
        low_ref[group * 8 : group * 8 + 8, :] = low
        high_ref[group * 8 : group * 8 + 8, :] = high

    for comp in range(COMP):

        def load_field(col):
            place = comp * COLS + col
            value = raw_ref[pl.ds(place, RHS, stride=COMP * COLS), :]
            row = FIELD_AT + place * RHS
            main_ref[row : row + RHS, :] = value
            return value

        pack(comp, load_field)
    for half in range(2):
        pack(
            COMP + half,
            lambda col: raw_ref[pl.ds(raw_couple + half * 8 * COLS + col, 8, stride=COLS), :],
        )
    pack(
        COMP + 2,
        lambda col: jnp.broadcast_to(eta[col : col + 1, :], (RHS, LANES)),
    )


def pack(residuals, shear_rate, coupling):
    raw = jnp.concatenate(
        [part.reshape(-1, LANES) for part in (residuals, coupling, shear_rate)], axis=0
    )
    return pl.pallas_call(
        pack_kernel,
        out_shape=(
            jax.ShapeDtypeStruct((BLOCK_ROWS, LANES), jnp.float32),
            jax.ShapeDtypeStruct((GHOST_ROWS, LANES), jnp.float32),
            jax.ShapeDtypeStruct((GHOST_ROWS, LANES), jnp.float32),
        ),
        in_specs=[VMEM],
        out_specs=(VMEM,) * 3,
        compiler_params=pltpu.CompilerParams(vmem_limit_bytes=4 * 2**20),
    )(raw)


def corner_kernel(left_ref, right_ref, left_ghost, right_ghost, down_ref, up_ref):
    lane = lane_index()
    for out_ref, top in ((down_ref, False), (up_ref, True)):
        for place, (side, a, b) in enumerate(CORNER):
            src = right_ref if side else left_ref
            base = HIGH_BASE if side else LOW_BASE
            x = a - 1 if side else BX - a
            y = BY - b if top else b - 1
            col = x * BY + y
            for comp in range(COMP):
                start = base + FIELD_AT + (comp * COLS + col) * RHS
                row = (place * COMP + comp) * RHS
                out_ref[row : row + RHS, :] = src[start : start + RHS, :]
            if place < NEAR_COUNT:
                for half in range(2):
                    row = C_COUPLE_AT + place * 16 + half * 8
                    start = base + couple_at(x) + half * 8 * BY + y
                    out_ref[row : row + 8, :] = src[pl.ds(start, 8, stride=BY), :]
            start = base + ETA_AT + col
            out_ref[C_ETA_AT + place : C_ETA_AT + place + 1, :] = src[start : start + 1, :]
        out_ref[C_ETA_AT + len(CORNER) : C_GHOST_AT, :] = jnp.zeros(
            (16 - len(CORNER), LANES), jnp.float32
        )
        for row in range(0, GHOST_ROWS, 8):
            right, left = right_ghost[row : row + 8, :], left_ghost[row : row + 8, :]
            out_ref[C_GHOST_AT + row : C_GHOST_AT + row + 8, :] = jnp.where(
                lane < LANES // 2, right, left
            )


def corners(*parts):
    return pl.pallas_call(
        corner_kernel,
        out_shape=(jax.ShapeDtypeStruct((CORNER_ROWS, LANES), jnp.float32),) * 2,
        in_specs=[VMEM] * 4,
        out_specs=(VMEM,) * 2,
        compiler_params=pltpu.CompilerParams(vmem_limit_bytes=4 * 2**20),
    )(*parts)


def distance(place):
    return max(POWERS - place, 0, place - (POWERS + BX - 1))


def corner(x, y):
    return distance(x) > 0 and distance(y) > 0


def rows_of(reach):
    for x in range(POWERS - reach, POWERS + BX + reach):
        rest = reach - distance(x)
        yield x, range(POWERS - rest, POWERS + BY + rest)


PLACES = [(x, y) for x, ys in rows_of(POWERS) for y in ys]
SLOT = {place: i for i, place in enumerate(sorted(PLACES, key=lambda place: corner(*place)))}
EARLY = sum(not corner(*place) for place in PLACES)


def ready(x, y, power):
    if power == 0:
        return not corner(x, y)
    around = ((x, y), (x - 1, y), (x + 1, y), (x, y - 1), (x, y + 1))
    return all(ready(i, j, power - 1) for i, j in around)


def state_shapes(count):
    field = (count * COMP, RHS, LANES)
    return (
        [field] * 4 + [(count, 24, LANES)] * 2 + [(count * 6, RHS, LANES)] * 2
        + [(count, RHS, LANES)] * 2
    )


def powers_part(early, blocks, first_state, mine, basis_ref):
    lane = lane_index()
    first, last = lane == 0, lane == LANES - 1
    MAIN, GHOST, COEF, FACE, SCALE = 0, 2, 4, 6, 8

    def held(kind, x, y, power):
        return first_state[kind] if early or ready(x, y, power) else mine[kind]

    def place_column(src, x, y, field_at, entry_at, stride, eta_at, ghosts, ghost_at, col):
        at = SLOT[x, y]
        for comp in range(COMP):
            mine[MAIN][at * COMP + comp] = src[field_at[comp] : field_at[comp] + RHS, :]
        mine[COEF][at, 16:24, :] = jnp.broadcast_to(src[eta_at : eta_at + 1, :], (8, LANES))
        if distance(x) + distance(y) >= POWERS:
            return
        for half in range(2):
            start = entry_at + half * 8 * stride
            mine[COEF][at, half * 8 : half * 8 + 8, :] = (
                src[pl.ds(start, 8, stride=stride), :] if stride > 1 else src[start : start + 8, :]
            )
        shift = (-8 * col - 4) % LANES
        for comp in range(COMP):
            row = ghost_at + comp * RHS
            mine[GHOST][at * COMP + comp] = pltpu.roll(ghosts[row : row + RHS, :], shift, 1)
        for part in range(3):
            row = ghost_at + COMP * RHS + part * 8
            mine[COEF + 1][at, part * 8 : part * 8 + 8, :] = pltpu.roll(
                ghosts[row : row + 8, :], shift, 1
            )

    if early:
        own_ref, left_ref, right_ref, front_ref, back_ref, left_ghost, right_ghost = blocks
        for src, base, ghosts, off_x, off_y in (
            (own_ref, 0, own_ref, 0, 0), (left_ref, LOW_BASE, left_ghost, -1, 0),
            (right_ref, HIGH_BASE, right_ghost, 1, 0),
            (front_ref, 0, front_ref, 0, -1), (back_ref, 0, back_ref, 0, 1),
        ):
            for x in range(BX):
                for y in range(BY):
                    col = x * BY + y
                    place_column(
                        src, POWERS + off_x * BX + x, POWERS + off_y * BY + y,
                        [base + FIELD_AT + (comp * COLS + col) * RHS for comp in range(COMP)],
                        base + couple_at(x) + y, BY, base + ETA_AT + col, ghosts, 0, col,
                    )
    else:
        low_ref, high_ref = blocks
        for src, top in ((low_ref, True), (high_ref, False)):
            for place, (side, a, b) in enumerate(CORNER):
                x = POWERS + BX - 1 + a if side else POWERS - a
                y = POWERS - b if top else POWERS + BY - 1 + b
                col = (a - 1 if side else BX - a) * BY + (BY - b if top else b - 1)
                place_column(
                    src, x, y, [(place * COMP + comp) * RHS for comp in range(COMP)],
                    C_COUPLE_AT + place * 16, 1, C_ETA_AT + place, src, C_GHOST_AT, col,
                )

    def shifted(value, other):
        up, down = pltpu.roll(value, LANES - 1, 1), pltpu.roll(value, 1, 1)
        other_up, other_down = pltpu.roll(other, LANES - 1, 1), pltpu.roll(other, 1, 1)
        return (
            jnp.where(last, other_up, up), jnp.where(first, other_down, down),
            jnp.where(last, up, other_up), jnp.where(first, down, other_down),
        )

    def eta_at(kind, x, y):
        return held(kind, x, y, 0)[SLOT[x, y], 16:24, :]

    def faces(outer, x, y, eta, up, down):
        kind, at = COEF + outer, SLOT[x, y]
        around = [
            eta_at(kind, x - 1, y), eta_at(kind, x + 1, y),
            eta_at(kind, x, y - 1), eta_at(kind, x, y + 1), down, up,
        ]
        kappas = [eta + beside for beside in around]
        for index, kappa in enumerate(kappas):
            mine[FACE + outer][at * 6 + index] = kappa
        total = (kappas[0] + kappas[1]) + (kappas[2] + kappas[3]) + (kappas[4] + kappas[5])
        diagonal = held(kind, x, y, 0)[at, pl.ds(0, COMP, stride=COMP + 1), :]
        mine[SCALE + outer][at, 0:COMP, :] = jnp.where(
            eta[0:COMP, :] < 0.0, 1.0 / (diagonal - total[0:COMP, :]), 0.0
        )

    for x, ys in rows_of(POWERS - 1):
        for y in ys:
            if ready(x, y, 1) != early:
                continue
            eta, eta_ghost = eta_at(COEF, x, y), eta_at(COEF + 1, x, y)
            up, down, ghost_up, ghost_down = shifted(eta, eta_ghost)
            faces(0, x, y, eta, up, down)
            if distance(x) + distance(y) < POWERS - 1:
                faces(1, x, y, eta_ghost, ghost_up, ghost_down)

    def spread(ref, at, row):
        return jnp.broadcast_to(ref[at, row : row + 1, :], (RHS, LANES))

    def apply(outer, power, x, y, before, centre, after, up, down):
        at = SLOT[x, y]
        table = held(COEF + outer, x, y, 0)
        faces_of, inverse = held(FACE + outer, x, y, 1), held(SCALE + outer, x, y, 1)
        kappa = [faces_of[at * 6 + index] for index in range(6)]
        results = []
        for comp in range(COMP):
            beside = [
                load(outer, power, x - 1, y, comp), load(outer, power, x + 1, y, comp),
                before[comp], after[comp], down[comp], up[comp],
            ]
            terms = [k * v for k, v in zip(kappa, beside)]
            terms += [
                spread(table, at, comp * COMP + d) * centre[d] for d in range(COMP) if d != comp
            ]
            while len(terms) > 1:
                terms = [
                    terms[i] + terms[i + 1] if i + 1 < len(terms) else terms[i]
                    for i in range(0, len(terms), 2)
                ]
            results.append(terms[0] * spread(inverse, at, comp))
        return results

    def load(outer, power, x, y, comp):
        kind = (GHOST if outer else MAIN) + power % 2
        return held(kind, x, y, power)[SLOT[x, y] * COMP + comp]

    for power in range(1, POWERS + 1):
        limit = POWERS - power
        for x, ys in rows_of(limit):
            rows = {}

            def at_row(outer, y, x=x, rows=rows, power=power):
                if (outer, y) not in rows:
                    rows[outer, y] = [load(outer, power - 1, x, y, comp) for comp in range(COMP)]
                return rows[outer, y]

            for y in ys:
                if ready(x, y, power) != early:
                    continue
                at = SLOT[x, y]
                reach = distance(x) + distance(y)
                centre, outer = at_row(0, y), at_row(1, y)
                moves = [shifted(c, o) for c, o in zip(centre, outer)]
                results = apply(
                    0, power - 1, x, y, at_row(0, y - 1), centre, at_row(0, y + 1),
                    [m[0] for m in moves], [m[1] for m in moves],
                )
                for comp in range(COMP):
                    if limit:
                        mine[MAIN + power % 2][at * COMP + comp] = results[comp]
                if reach == 0:
                    for comp in range(COMP):
                        tile = comp * COLS + (x - POWERS) * BY + (y - POWERS)
                        if power == 1:
                            basis_ref[tile, 0:RHS, :] = centre[comp]
                        basis_ref[tile, power * RHS : power * RHS + RHS, :] = results[comp]
                if reach < limit:
                    outside = apply(
                        1, power - 1, x, y, at_row(1, y - 1), outer, at_row(1, y + 1),
                        [m[2] for m in moves], [m[3] for m in moves],
                    )
                    for comp in range(COMP):
                        mine[GHOST + power % 2][at * COMP + comp] = outside[comp]


def early_kernel(*refs):
    powers_part(True, refs[:7], refs[7:17], refs[7:17], refs[17])


def late_kernel(*refs):
    blocks, first_state, early_basis = refs[:2], refs[2:12], refs[12]
    basis_ref, gram_ref, mine, square = refs[13], refs[14], refs[15:25], refs[25]
    for x in range(BX):
        for y in range(BY):
            for power in range(1, POWERS + 1):
                if ready(POWERS + x, POWERS + y, power):
                    start = 0 if power == 1 else power * RHS
                    stop = power * RHS + RHS
                    for comp in range(COMP):
                        tile = comp * COLS + x * BY + y
                        basis_ref[tile, start:stop, :] = early_basis[tile, start:stop, :]
    powers_part(False, blocks, first_state, mine, basis_ref)
    lane = lane_index()
    order = (POWERS + 1) * RHS
    total = jnp.zeros((order, order), jnp.float32)
    for tile in range(0, COMP * COLS, 2):
        both = jnp.concatenate([basis_ref[tile], basis_ref[tile + 1]], axis=1)
        total = total + lax.dot_general(
            both, both, (((1,), (1,)), ((), ())),
            precision=HIGHEST, preferred_element_type=jnp.float32,
        )
    square[...] = jnp.zeros_like(square)
    square[:, 0:order] = total
    packed = jnp.zeros((RHS, LANES), jnp.float32)
    start = 0
    for block in range(POWERS + 1):
        width = order - block * RHS
        value = pltpu.roll(
            square[block * RHS : block * RHS + RHS, :], (start - block * RHS) % LANES, 1
        )
        packed = jnp.where((lane >= start) & (lane < start + width), value, packed)
        start += width
    gram_ref[...] = packed


def early_powers(*blocks):
    basis = (COMP * COLS, (POWERS + 1) * RHS, LANES)
    return pl.pallas_call(
        early_kernel,
        out_shape=[
            jax.ShapeDtypeStruct(shape, jnp.float32) for shape in state_shapes(EARLY) + [basis]
        ],
        in_specs=[VMEM] * 7,
        out_specs=[VMEM] * 11,
        compiler_params=pltpu.CompilerParams(vmem_limit_bytes=20 * 2**20),
        cost_estimate=pl.CostEstimate(flops=5_000_000, bytes_accessed=8_000_000, transcendentals=0),
    )(*blocks)


def late_powers(low, high, state):
    basis = (COMP * COLS, (POWERS + 1) * RHS, LANES)
    return pl.pallas_call(
        late_kernel,
        out_shape=(
            jax.ShapeDtypeStruct(basis, jnp.float32),
            jax.ShapeDtypeStruct((RHS, LANES), jnp.float32),
        ),
        in_specs=[VMEM] * 13,
        out_specs=(VMEM,) * 2,
        scratch_shapes=[pltpu.VMEM(shape, jnp.float32) for shape in state_shapes(len(PLACES))]
        + [pltpu.VMEM(((POWERS + 1) * RHS, LANES), jnp.float32)],
        compiler_params=pltpu.CompilerParams(vmem_limit_bytes=36 * 2**20),
    )(low, high, *state)


def finish_kernel(gram_ref, basis_ref, out_ref, factor_ref, square, upper):
    lane = lane_index()
    order = (POWERS + 1) * RHS
    parts = [gram_ref[i] for i in range(gram_ref.shape[0])]
    while len(parts) > 1:
        parts = [
            parts[i] + parts[i + 1] if i + 1 < len(parts) else parts[i]
            for i in range(0, len(parts), 2)
        ]
    packed = parts[0]
    square[...] = jnp.zeros_like(square)
    start = 0
    for block in range(POWERS + 1):
        width = order - block * RHS
        value = pltpu.roll(packed, (block * RHS - start) % LANES, 1)
        keep = (lane >= block * RHS) & (lane < order)
        square[block * RHS : block * RHS + RHS, :] = jnp.where(keep, value, 0.0)
        start += width
    half = square[...]
    other = half.T
    gram = []
    for block in range(POWERS + 1):
        rows = slice(block * RHS, block * RHS + RHS)
        gram.append(jnp.where(lane < block * RHS, other[rows, :], half[rows, :]))
    summed = [tile + pltpu.roll(tile, LANES - RHS, 1) for tile in gram]
    normal = [summed[i] + summed[i + 1] for i in range(POWERS)] + [summed[0]]

    upper[...] = jnp.zeros_like(upper)
    number = lane[0:1, :]

    def wide(value, column):
        return jnp.broadcast_to(value[:, column : column + 1], value.shape)

    def pair(matrix, step):
        tile, row = step // RHS, step % RHS
        p, q = matrix[tile][row : row + 1, :], matrix[tile][row + 1 : row + 2, :]
        one, cross, far = wide(p, step), wide(p, step + 1), wide(q, step + 1)
        inverse = 1.0 / one
        ratio = cross * inverse
        other = far - cross * ratio
        rest = q - ratio * p
        inverse_other = 1.0 / other
        second = rest * inverse_other
        first = p * inverse - ratio * second
        return p, rest, one, other, first, second, inverse, inverse_other, ratio

    for step in range(0, order, 2):
        tile = step // RHS
        low = tile if step % RHS < RHS - 2 else tile + 1
        p, rest, one, other, first, second, _, _, _ = pair(gram, step)
        top = jnp.where(number >= step, p * lax.rsqrt(one), 0.0)
        bottom = jnp.where(number > step, rest * lax.rsqrt(other), 0.0)
        upper[step : step + 1, :] = top[0:1, :]
        upper[step + 1 : step + 2, :] = bottom[0:1, :]
        for i in range(low, POWERS + 1):
            gram[i] = gram[i] - wide(gram[i], step) * first - wide(gram[i], step + 1) * second
        if step < POWERS * RHS:
            _, _, _, _, first, second, inverse, inverse_other, ratio = pair(normal, step)
            mixed = ratio * inverse_other
            at_one, at_other = number == step, number == step + 1
            cleared = (lane == step) | (lane == step + 1)
            first = jnp.where(
                at_one, -(inverse + ratio * mixed), jnp.where(at_other, mixed, first)
            )
            second = jnp.where(at_one, mixed, jnp.where(at_other, -inverse_other, second))
            for i in range(low, POWERS + 1):
                normal[i] = (
                    jnp.where(cleared, 0.0, normal[i])
                    - wide(normal[i], step) * first
                    - wide(normal[i], step + 1) * second
                )
    factor_ref[...] = upper[0:order, 0:order]
    answer = normal[POWERS]
    weights = [
        jnp.broadcast_to(answer[:, i : i + 1], (RHS, LANES)) for i in range(POWERS * RHS)
    ]

    def combine(tile, carry):
        sums = [None] * 4
        for i in range(POWERS * RHS):
            term = weights[i] * jnp.broadcast_to(basis_ref[tile, i : i + 1, :], (RHS, LANES))
            sums[i % 4] = term if sums[i % 4] is None else sums[i % 4] + term
        out_ref[pl.ds(tile, RHS, stride=COMP * COLS), :] = (sums[0] + sums[1]) + (
            sums[2] + sums[3]
        )
        return carry

    lax.fori_loop(0, COMP * COLS, combine, 0, unroll=4)


def finish(gram, basis):
    order = (POWERS + 1) * RHS
    return pl.pallas_call(
        finish_kernel,
        out_shape=(
            jax.ShapeDtypeStruct((RHS * COMP * COLS, LANES), jnp.float32),
            jax.ShapeDtypeStruct((order, order), jnp.float32),
        ),
        in_specs=[VMEM] * 2,
        out_specs=(VMEM,) * 2,
        scratch_shapes=[
            pltpu.VMEM((LANES, LANES), jnp.float32),
            pltpu.VMEM((order, LANES), jnp.float32),
        ],
        compiler_params=pltpu.CompilerParams(vmem_limit_bytes=6 * 2**20),
    )(gram, basis)


def swapped(to_low, to_high, axis, even):
    count = lax.axis_size(axis)
    inner = [(i, i ^ 1) for i in range(count)]
    outer = [(i, ((i + 1) ^ 1) - 1) for i in range(1, count - 1)]
    two = lax.ppermute(jnp.where(even, to_low, to_high), axis, outer)
    one = lax.ppermute(jnp.where(even, to_high, to_low), axis, inner)
    return two, one


def sorted_pair(two, one, even):
    return jnp.where(even, two, one), jnp.where(even, one, two)


def gathered(tile, axes):
    count = lax.axis_size(axes)
    return lax.all_to_all(jnp.broadcast_to(tile[None], (count,) + tile.shape), axes, 0, 0)


def local(residuals, shear_rate, coupling):
    block, low, high = pack(residuals, shear_rate, coupling)
    even_x, even_y, even_z = (lax.axis_index(axis) % 2 == 0 for axis in ("gx", "gy", "gz"))
    two, one = swapped(low, high, "gz", even_z)
    to_low, to_high = block[GHOST_ROWS : GHOST_ROWS + SIDE_ROWS], block[GHOST_ROWS + LAYER :]
    left, right = sorted_pair(*swapped(to_low, to_high, "gx", even_x), even_x)
    ghosts = two + one
    left_ghost, right_ghost = sorted_pair(*swapped(ghosts, ghosts, "gx", even_x), even_x)
    own = lax.dynamic_update_slice(block, ghosts, (0, 0))
    front, back = sorted_pair(*swapped(own, own, "gy", even_y), even_y)
    down, up = corners(left, right, left_ghost, right_ghost)
    low_corner, high_corner = sorted_pair(*swapped(down, up, "gy", even_y), even_y)
    state = early_powers(own, left, right, front, back, left_ghost, right_ghost)
    basis, gram = late_powers(low_corner, high_corner, state)
    gram = jnp.sum(gathered(gram, ("gy", "gz")), axis=0)
    correction, factor = finish(gathered(gram, "gx"), basis)
    return correction.reshape(residuals.shape), factor


def solution(mesh):
    in_specs = (
        P(None, None, "gx", "gy", "gz"),
        P("gx", "gy", "gz"),
        P(None, None, "gx", "gy", "gz"),
    )
    out_specs = (P(None, None, "gx", "gy", "gz"), P())
    return jax.shard_map(local, mesh=mesh, in_specs=in_specs, out_specs=out_specs, check_vma=False)
```
